128 devices in a mesh: tensor: 4 (over z), dp: 32 (over y, x, core).
Axes of the slice: x: 4, y: 4, z: 4, core: 2. Of those that a mesh axis runs over, the one named last changes fastest.
Arguments:
- text_in: bfloat16 [2, 96, 36, 768], P(None, 'dp', None, 'tensor'), may hold values from -6 to 6
- image_in: bfloat16 [2, 96, 101, 1024], P(None, 'dp', None, 'tensor'), may hold values from -6 to 6
- caption_len: int32 [2, 96], P(None, 'dp'), may hold values from 8 to 36, as said below
- region_count: int32 [2, 96], P(None, 'dp'), may hold values from 10 to 101, as said below
- text_cot: bfloat16 [2, 96, 36, 768], P(None, 'dp', None, 'tensor'), may hold values from -6 to 6
- image_cot: bfloat16 [2, 96, 101, 1024], P(None, 'dp', None, 'tensor'), may hold values from -6 to 6
- co_text_qkv: bfloat16 [3, 768, 1024], P(None, None, 'tensor'), may hold values from -0.21875 to 0.21875
- co_image_qkv: bfloat16 [3, 1024, 1024], P(None, None, 'tensor'), may hold values from -0.1875 to 0.1875
- co_text_out: bfloat16 [1024, 768], P('tensor'), may hold values from -0.5 to 0.5
- co_image_out: bfloat16 [1024, 1024], P('tensor'), may hold values from -0.5 to 0.5
- co_text_up: bfloat16 [768, 3072], P(None, 'tensor'), may hold values from -0.21875 to 0.21875
- co_text_down: bfloat16 [3072, 768], P('tensor'), may hold values from -0.109375 to 0.109375
- co_image_up: bfloat16 [1024, 1024], P(None, 'tensor'), may hold values from -0.1875 to 0.1875
- co_image_down: bfloat16 [1024, 1024], P('tensor'), may hold values from -0.1875 to 0.1875
- self_text_qkv: bfloat16 [3, 768, 768], P(None, None, 'tensor'), may hold values from -0.21875 to 0.21875
- self_image_qkv: bfloat16 [3, 1024, 1024], P(None, None, 'tensor'), may hold values from -0.1875 to 0.1875
- self_text_out: bfloat16 [768, 768], P('tensor'), may hold values from -0.625 to 0.625
- self_image_out: bfloat16 [1024, 1024], P('tensor'), may hold values from -0.5 to 0.5
- text_up: bfloat16 [768, 3072], P(None, 'tensor'), may hold values from -0.21875 to 0.21875
- text_down: bfloat16 [3072, 768], P('tensor'), may hold values from -0.109375 to 0.109375
- image_up: bfloat16 [1024, 1024], P(None, 'tensor'), may hold values from -0.1875 to 0.1875
- image_down: bfloat16 [1024, 1024], P('tensor'), may hold values from -0.1875 to 0.1875
- text_gains: float32 [4, 768], replicated, may hold values from 0.5 to 1.5
- text_shifts: float32 [4, 768], replicated, may hold values from -1.75 to 1.75
- image_gains: float32 [4, 1024], replicated, may hold values from 0.5 to 1.5
- image_shifts: float32 [4, 1024], replicated, may hold values from -1.75 to 1.75
Outputs:
- text_out: float32 [2, 96, 36, 768], P(None, 'dp', None, 'tensor')
- image_out: float32 [2, 96, 101, 1024], P(None, 'dp', None, 'tensor')
- text_grad: float32 [2, 96, 36, 768], P(None, 'dp', None, 'tensor')
- image_grad: float32 [2, 96, 101, 1024], P(None, 'dp', None, 'tensor')
- co_text_qkv_grad: float32 [3, 768, 1024], P(None, None, 'tensor')
- co_image_qkv_grad: float32 [3, 1024, 1024], P(None, None, 'tensor')
- co_text_out_grad: float32 [1024, 768], P('tensor')
- co_image_out_grad: float32 [1024, 1024], P('tensor')
- co_text_up_grad: float32 [768, 3072], P(None, 'tensor')
- co_text_down_grad: float32 [3072, 768], P('tensor')
- co_image_up_grad: float32 [1024, 1024], P(None, 'tensor')
- co_image_down_grad: float32 [1024, 1024], P('tensor')
- self_text_qkv_grad: float32 [3, 768, 768], P(None, None, 'tensor')
- self_image_qkv_grad: float32 [3, 1024, 1024], P(None, None, 'tensor')
- self_text_out_grad: float32 [768, 768], P('tensor')
- self_image_out_grad: float32 [1024, 1024], P('tensor')
- text_up_grad: float32 [768, 3072], P(None, 'tensor')
- text_down_grad: float32 [3072, 768], P('tensor')
- image_up_grad: float32 [1024, 1024], P(None, 'tensor')
- image_down_grad: float32 [1024, 1024], P('tensor')
- text_gains_grad: float32 [4, 768], replicated
- text_shifts_grad: float32 [4, 768], replicated
- image_gains_grad: float32 [4, 1024], replicated
- image_shifts_grad: float32 [4, 1024], replicated
The draws below stay inside these ranges and needn't reach their ends.
Inputs may be any that keep to these rules, and one draw needn't show every extreme that they name: `caption_len`: A sample's live caption tokens come first; in every draw some sample has all 36. `region_count`: A sample's live region slots come first; in every draw some sample has all 101.
All inputs are finite; a program needn't handle non-finite values.
Results may differ from the reference program's by a relative error of at most 0.023.
Values may be sent and summed in bfloat16 or wider, within the bound.
No kernel may reach another device: no remote copies, remote signals or barrier semaphores. Data moves between devices by JAX's collectives and lax.ppermute only.
A program may use at most 256 MiB of HBM per device.

```python
import jax
import jax.numpy as jnp
from jax import lax

DT = 768
BI = 1024
DV = 1024
FT = 3072
FV = 1024
CO_HEAD = 128
TEXT_HEAD = 64
IMAGE_HEAD = 128
TEXT = 36
REGIONS = 101
MICRO = 2
SAMP_DEV = 3
SAMPLES = 96
N_DP = 32


def draw_caption_len(key, part):
    key = jax.random.fold_in(key, 11)
    first_key, second_key = jax.random.split(key)
    lengths = jax.random.randint(first_key, (MICRO * SAMPLES,), 8, TEXT + 1)
    position = jax.random.randint(second_key, (), 0, MICRO * SAMPLES)
    lengths = lengths.at[position].set(TEXT)
    return lengths.reshape(MICRO, SAMPLES).astype(jnp.int32)


def draw_region_count(key, part):
    key = jax.random.fold_in(key, 23)
    first_key, second_key, third_key = jax.random.split(key, 3)
    base_count = jax.random.randint(first_key, (MICRO * SAMPLES,), 0, REGIONS - 9)
    halvings = jax.random.randint(second_key, (MICRO * SAMPLES,), 0, 4)
    counts = 10 + jnp.right_shift(base_count, halvings)
    position = jax.random.randint(third_key, (), 0, MICRO * SAMPLES)
    counts = counts.at[position].set(REGIONS)
    return counts.reshape(MICRO, SAMPLES).astype(jnp.int32)


def block_scale(stream_key, extent, cuts, least, high):
    level, own = 1.0, jax.random.fold_in(stream_key, 6)
    for axis_at, parts in cuts:
        heights = jnp.exp(jax.random.uniform(jax.random.fold_in(own, axis_at), (parts,), jnp.float32, least / len(cuts), high / len(cuts)))
        level = level * jnp.repeat(heights, extent[axis_at] // parts).reshape([-1 if axis == axis_at else 1 for axis in range(len(extent))])
    return level


def noise(stream_key, shape, width, limit, cuts=(), kind=jnp.bfloat16):
    drawn = width * jax.random.normal(stream_key, shape, jnp.float32)
    if cuts:
        drawn = drawn * block_scale(stream_key, shape, cuts, -0.22, 0.18)
    return jnp.clip(drawn, -limit, limit).astype(kind)


def setup_inputs(seed: int = 0) -> dict:
    key_of = jax.random.split(jax.random.key(seed), 27)
    return {
        "text_in": noise(key_of[0], (MICRO, SAMPLES, TEXT, DT), 1.0, 6.0, ((1, 32), (3, 4))),
        "image_in": noise(key_of[1], (MICRO, SAMPLES, REGIONS, DV), 1.0, 6.0, ((1, 32), (3, 4))),
        "caption_len": draw_caption_len(jax.random.fold_in(key_of[26], 71), 0),
        "region_count": draw_region_count(jax.random.fold_in(key_of[26], 71), 0),
        "text_cot": noise(key_of[4], (MICRO, SAMPLES, TEXT, DT), 1.0, 6.0, ((1, 32), (3, 4))),
        "image_cot": noise(key_of[5], (MICRO, SAMPLES, REGIONS, DV), 1.0, 6.0, ((1, 32), (3, 4))),
        "co_text_qkv": noise(key_of[6], (3, DT, BI), DT ** -0.5, 0.21875, ((2, 4),)),
        "co_image_qkv": noise(key_of[7], (3, DV, BI), DV ** -0.5, 0.1875, ((2, 4),)),
        "co_text_out": noise(key_of[8], (BI, DT), (BI // 8) ** -0.5, 0.5, ((0, 4),)),
        "co_image_out": noise(key_of[9], (BI, DV), (BI // 8) ** -0.5, 0.5, ((0, 4),)),
        "co_text_up": noise(key_of[10], (DT, FT), DT ** -0.5, 0.21875, ((1, 4),)),
        "co_text_down": noise(key_of[11], (FT, DT), FT ** -0.5, 0.109375, ((0, 4),)),
        "co_image_up": noise(key_of[12], (DV, FV), DV ** -0.5, 0.1875, ((1, 4),)),
        "co_image_down": noise(key_of[13], (FV, DV), FV ** -0.5, 0.1875, ((0, 4),)),
        "self_text_qkv": noise(key_of[14], (3, DT, DT), DT ** -0.5, 0.21875, ((2, 4),)),
        "self_image_qkv": noise(key_of[15], (3, DV, DV), DV ** -0.5, 0.1875, ((2, 4),)),
        "self_text_out": noise(key_of[16], (DT, DT), (DT // 8) ** -0.5, 0.625, ((0, 4),)),
        "self_image_out": noise(key_of[17], (DV, DV), (DV // 8) ** -0.5, 0.5, ((0, 4),)),
        "text_up": noise(key_of[18], (DT, FT), DT ** -0.5, 0.21875, ((1, 4),)),
        "text_down": noise(key_of[19], (FT, DT), FT ** -0.5, 0.109375, ((0, 4),)),
        "image_up": noise(key_of[20], (DV, FV), DV ** -0.5, 0.1875, ((1, 4),)),
        "image_down": noise(key_of[21], (FV, DV), FV ** -0.5, 0.1875, ((0, 4),)),
        "text_gains": jnp.clip(1.0 + 0.1 * jax.random.normal(key_of[22], (4, DT), jnp.float32), 0.5, 1.5),
        "text_shifts": noise(key_of[23], (4, DT), 0.3, 1.75, (), jnp.float32),
        "image_gains": jnp.clip(1.0 + 0.1 * jax.random.normal(key_of[24], (4, DV), jnp.float32), 0.5, 1.5),
        "image_shifts": noise(key_of[25], (4, DV), 0.3, 1.75, (), jnp.float32),
    }


@jax.custom_vjp
def low(v):
    return lax.optimization_barrier(v.astype(jnp.bfloat16)).astype(jnp.float32)

@jax.custom_vjp
def low_back(v):
    return v

def low_keep(v):
    return (low(v), None)

def low_pass(kept, grad):
    return (grad,)

def back_keep(v):
    return (v, None)

def back_low(kept, grad):
    return (low(grad),)
low.defvjp(low_keep, low_pass)
low_back.defvjp(back_keep, back_low)
norm_eps = 1e-05
mask_fill = -1000000000.0

def multiply(left_side, right_side, form):
    return jnp.einsum(form, left_side, right_side, precision=lax.Precision.HIGHEST)

def normed(values, gain_vec, shift_vec):
    centre = values - lax.optimization_barrier(jnp.mean(values, axis=-1, keepdims=True))
    spread = lax.optimization_barrier(jnp.mean(centre * centre, axis=-1, keepdims=True))
    return centre * lax.rsqrt(spread + norm_eps) * gain_vec + shift_vec

def residual_norm(norm_set, text_base, image_base, text_branch, image_branch):
    text_gain, text_shift, image_gain, image_shift = norm_set
    return (normed(text_base + text_branch, text_gain, text_shift), normed(image_base + image_branch, image_gain, image_shift))

def norm_row(norm_set, position):
    return tuple((member[position] for member in norm_set))

def project(rounded, stacked):
    triple = low(low_back(multiply(rounded, stacked, 'bsd,ide->ibse')))
    return (triple[0], triple[1], triple[2])

def attend(query_rows, key_rows, value_rows, key_mask, head_size):
    sample_count, query_count, feature_width = query_rows.shape
    key_count = key_rows.shape[1]
    head_count = feature_width // head_size
    query_heads = query_rows.reshape(sample_count, query_count, head_count, head_size)
    key_heads = key_rows.reshape(sample_count, key_count, head_count, head_size)
    value_heads = value_rows.reshape(sample_count, key_count, head_count, head_size)
    scores = low_back(multiply(query_heads, key_heads, 'bqhd,bkhd->bhqk') * head_size ** (-0.5))
    scores = jnp.where(key_mask[:, None, None, :] > 0, scores, mask_fill)
    row_top = lax.optimization_barrier(jnp.max(scores, axis=-1, keepdims=True))
    exponent = jnp.exp(scores - row_top)
    probability = exponent / lax.optimization_barrier(jnp.sum(exponent, axis=-1, keepdims=True))
    attended = multiply(low(probability), value_heads, 'bhqk,bkhd->bqhd')
    return low(low_back(attended.reshape(sample_count, query_count, feature_width)))

def co_branch(weight_set, text_base, image_base, text_mask, image_mask):
    text_qkv, image_qkv, text_proj, image_proj = weight_set
    text_query, text_key, text_value = project(low(text_base), text_qkv)
    image_query, image_key, image_value = project(low(image_base), image_qkv)
    text_mixed = attend(text_query, image_key, image_value, image_mask, CO_HEAD)
    image_mixed = attend(image_query, text_key, text_value, text_mask, CO_HEAD)
    return (low_back(multiply(text_mixed, text_proj, 'bse,ed->bsd')), low_back(multiply(image_mixed, image_proj, 'bse,ed->bsd')))

def self_branch(weight_set, text_base, image_base, text_mask, image_mask):
    text_qkv, image_qkv, text_proj, image_proj = weight_set
    text_query, text_key, text_value = project(low(text_base), text_qkv)
    image_query, image_key, image_value = project(low(image_base), image_qkv)
    text_mixed = attend(text_query, text_key, text_value, text_mask, TEXT_HEAD)
    image_mixed = attend(image_query, image_key, image_value, image_mask, IMAGE_HEAD)
    return (low_back(multiply(text_mixed, text_proj, 'bse,ed->bsd')), low_back(multiply(image_mixed, image_proj, 'bse,ed->bsd')))

def mlp_branch(weight_set, text_base, image_base):
    text_up_w, text_down_w, image_up_w, image_down_w = weight_set
    text_hidden = low_back(multiply(low(text_base), text_up_w, 'bsd,df->bsf'))
    text_branch = low_back(multiply(low(jax.nn.gelu(text_hidden, approximate=False)), text_down_w, 'bsf,fd->bsd'))
    image_hidden = low_back(multiply(low(image_base), image_up_w, 'bsd,df->bsf'))
    image_branch = low_back(multiply(low(jax.nn.gelu(image_hidden, approximate=False)), image_down_w, 'bsf,fd->bsd'))
    return (text_branch, image_branch)

def layer_forward(params, text_base, image_base, text_mask, image_mask):
    co_set, co_mlp_set, self_set, mlp_set, norm_set = params
    co_text, co_image = co_branch(co_set, text_base, image_base, text_mask, image_mask)
    text_a, image_a = residual_norm(norm_row(norm_set, 0), text_base, image_base, co_text, co_image)
    ffn_text, ffn_image = mlp_branch(co_mlp_set, text_a, image_a)
    text_b, image_b = residual_norm(norm_row(norm_set, 1), text_a, image_a, ffn_text, ffn_image)
    self_text, self_image = self_branch(self_set, text_b, image_b, text_mask, image_mask)
    text_c, image_c = residual_norm(norm_row(norm_set, 2), text_b, image_b, self_text, self_image)
    mlp_text, mlp_image = mlp_branch(mlp_set, text_c, image_c)
    return residual_norm(norm_row(norm_set, 3), text_c, image_c, mlp_text, mlp_image)

def reference(text_in, image_in, caption_len, region_count, text_cot, image_cot, co_text_qkv, co_image_qkv, co_text_out, co_image_out, co_text_up, co_text_down, co_image_up, co_image_down, self_text_qkv, self_image_qkv, self_text_out, self_image_out, text_up, text_down, image_up, image_down, text_gains, text_shifts, image_gains, image_shifts):
    arrays = [co_text_qkv, co_image_qkv, co_text_out, co_image_out, co_text_up, co_text_down, co_image_up, co_image_down, self_text_qkv, self_image_qkv, self_text_out, self_image_out, text_up, text_down, image_up, image_down, text_gains, text_shifts, image_gains, image_shifts]
    arrays = [member.astype(jnp.float32) for member in arrays]
    params = (tuple(arrays[0:4]), tuple(arrays[4:8]), tuple(arrays[8:12]), tuple(arrays[12:16]), tuple(arrays[16:20]))
    groups = MICRO * N_DP
    text_mask = (jnp.arange(TEXT, dtype=jnp.int32)[None, None, :] < caption_len[:, :, None]).astype(jnp.int32)
    image_mask = (jnp.arange(REGIONS, dtype=jnp.int32)[None, None, :] < region_count[:, :, None]).astype(jnp.int32)

    def regroup(values):
        return values.reshape((groups, SAMP_DEV) + values.shape[2:])
    inputs_all = (regroup(text_in.astype(jnp.float32)), regroup(image_in.astype(jnp.float32)), regroup(text_mask), regroup(image_mask), regroup(text_cot.astype(jnp.float32)), regroup(image_cot.astype(jnp.float32)))
    zero_grads = jax.tree.map(jnp.zeros_like, params)

    def advance(totals, pieces):
        text_base, image_base, text_keys, image_keys, text_cotan, image_cotan = pieces

        def forward(params_in, text_arg, image_arg):
            return layer_forward(params_in, text_arg, image_arg, text_keys, image_keys)
        results, pullback = jax.vjp(forward, params, text_base, image_base)
        grad_params, grad_text, grad_image = pullback((text_cotan, image_cotan))
        totals = jax.tree.map(jnp.add, totals, grad_params)
        return (totals, (results[0], results[1], grad_text, grad_image))
    totals, stacked = lax.scan(advance, zero_grads, inputs_all)
    flattened = [*totals[0], *totals[1], *totals[2], *totals[3], *totals[4]]
    return (stacked[0].reshape(text_in.shape), stacked[1].reshape(image_in.shape), stacked[2].reshape(text_in.shape), stacked[3].reshape(image_in.shape), flattened[0], flattened[1], flattened[2], flattened[3], flattened[4], flattened[5], flattened[6], flattened[7], flattened[8], flattened[9], flattened[10], flattened[11], flattened[12], flattened[13], flattened[14], flattened[15], flattened[16], flattened[17], flattened[18], flattened[19])
```

```python
import functools

import jax
import jax.numpy as jnp
from jax import lax
from jax.experimental import pallas as pl
from jax.experimental.pallas import tpu as pltpu
from jax.sharding import PartitionSpec as P

CO_HEAD = 128
TEXT_HEAD = 64
IMAGE_HEAD = 128
EPS = 1e-05
FILL = -1000000000.0
ROOT_HALF = 0.7071067811865476
INV_ROOT_TWO_PI = 0.3989422804014327
F32 = jnp.float32
BF = jnp.bfloat16
Z = 4


def dot(a, b):
    return lax.dot_general(a, b, (((1,), (0,)), ((), ())), preferred_element_type=F32)


def dot_nt(a, b):
    return lax.dot_general(a, b, (((1,), (1,)), ((), ())), preferred_element_type=F32)


def dot_tn(a, b):
    return lax.dot_general(a, b, (((0,), (0,)), ((), ())), preferred_element_type=F32)


def part(index, size):
    return pl.ds(pl.multiple_of(index * size, size), size)


def row_ids(count, step, samples):
    place = lax.broadcasted_iota(jnp.int32, (count, 1), 0)
    ids = jnp.zeros((count, 1), jnp.int32)
    for s in range(1, samples):
        ids = ids + (place >= s * step).astype(jnp.int32)
    return ids


def probabilities(q, k, same, scale):
    s = jnp.where(same, dot_nt(q, k) * scale, FILL)
    e = jnp.exp(s - jnp.max(s, axis=-1, keepdims=True))
    return e / jnp.sum(e, axis=-1, keepdims=True)


def head_fwd(q, k, v, same, scale):
    return dot(probabilities(q, k, same, scale).astype(BF), v).astype(BF)


def head_bwd(q, k, v, same, scale, do):
    p = probabilities(q, k, same, scale)
    dv = dot_tn(p.astype(BF), do)
    dp = dot_nt(do, v)
    ds = (p * (dp - jnp.sum(dp * p, axis=-1, keepdims=True))).astype(BF)
    dq = dot(ds, k) * scale
    dk = dot_tn(ds, q) * scale
    return dq.astype(BF), dk.astype(BF), dv.astype(BF)


def gelu(u):
    return u * (1.0 + lax.erf(u * ROOT_HALF)) * 0.5


def gelu_slope(u):
    return (1.0 + lax.erf(u * ROOT_HALF)) * 0.5 + u * jnp.exp(u * u * -0.5) * INV_ROOT_TWO_PI


def normalise(z):
    centre = z - jnp.mean(z, axis=-1, keepdims=True)
    rstd = lax.rsqrt(jnp.mean(centre * centre, axis=-1, keepdims=True) + EPS)
    return centre * rstd, rstd


def norm_back(z, gain, dy):
    xhat, rstd = normalise(z)
    dxh = dy * gain
    dz = rstd * (
        dxh
        - jnp.mean(dxh, axis=-1, keepdims=True)
        - xhat * jnp.mean(dxh * xhat, axis=-1, keepdims=True)
    )
    return dz, jnp.sum(dy * xhat, axis=0, keepdims=True), jnp.sum(dy, axis=0, keepdims=True)


def tiles(count, tile, body):
    def step(i, carry):
        body(part(i, tile))
        return carry

    lax.fori_loop(0, count // tile, step, 0)


def total(refs, rows):
    acc = refs[0][rows, :].astype(F32)
    for ref in refs[1:]:
        acc = acc + ref[rows, :].astype(F32)
    return acc


def lanes_in_order(refs, r, width):
    near = [refs[0], refs[3], refs[2], refs[1]]
    joined = jnp.concatenate([ref[...].astype(F32) for ref in near], axis=1)
    return pltpu.roll(joined, r * width, 1)


def lanes_from_own(values, r, width):
    return pltpu.roll(values, ((Z - r) & 3) * width, 1)


def rows_in_order(full, refs, r):
    size = refs[0].shape[0]
    for k, ref in enumerate(refs):
        full[part((r - k) & 3, size), :] = ref[...]


def split(refs, *counts):
    found, at = [], 0
    for count in counts:
        found.append(refs[at] if count == 0 else list(refs[at : at + count]))
        at += max(count, 1)
    assert at == len(refs)
    return found


def co_fwd(dims, *refs):
    rank, tin, vin, kt, kv, wt, wv, pt, pv, xt, xv, bt, bv, qt, qv, ot, ov, st, sv = split(
        refs, 0, 4, 4, 0, 0, 0, 0, 0, 0, 0, 0, 0, 0, 0, 0, 0, 0, 4, 4
    )
    samples, text, regions, nt, nv = dims
    r = rank[0]
    width_t, width_v = tin[0].shape[1], vin[0].shape[1]
    ct, cv = bt.shape[0], bv.shape[0]
    xt[...] = lanes_in_order(tin, r, width_t).astype(BF)
    for k, ref in enumerate(vin):
        xv[:, part((r - k) & 3, width_v)] = ref[...]
    bt[...] = xt[part(r, ct), :]
    bv[...] = xv[part(r, cv), :]
    for i in range(3):
        qt[i] = dot(xt[...], wt[i]).astype(BF)

    def project(rows):
        for i in range(3):
            qv[i, rows, :] = dot(xv[rows, :], wv[i]).astype(BF)

    tiles(xv.shape[0], cv, project)
    scale = CO_HEAD ** (-0.5)
    rid_t, rid_v = row_ids(nt, text, samples), row_ids(nv, regions, samples)
    for m in range(2):
        rt, rv = slice(m * nt, (m + 1) * nt), slice(m * nv, (m + 1) * nv)
        same_tv = rid_t == kv[m : m + 1, :]
        same_vt = rid_v == kt[m : m + 1, :]
        for h in range(qt.shape[2] // CO_HEAD):
            c = slice(h * CO_HEAD, (h + 1) * CO_HEAD)
            ot[rt, c] = head_fwd(qt[0, rt, c], qv[1, rv, c], qv[2, rv, c], same_tv, scale)
            ov[rv, c] = head_fwd(qv[0, rv, c], qt[1, rt, c], qt[2, rt, c], same_vt, scale)
    for k in range(Z):
        c = (r + k) & 3
        st[k][...] = dot(ot[part(c, ct), :], pt[...]).astype(BF)
        sv[k][...] = dot(ov[part(c, cv), :], pv[...]).astype(BF)


def co_bwd(dims, *refs):
    (rank, dt, dv, kt, kv, qt, qv, wt, wv, pt, pv, gt, gv,
     zt, zv, dqt, dqv, st, sv, dot_s, dov_s, acc_t, acc_v) = split(
        refs, 0, 4, 4, 0, 0, 0, 0, 0, 0, 0, 0, 0, 0, 0, 0, 0, 0, 4, 4, 0, 0, 0, 0
    )
    samples, text, regions, nt, nv = dims
    r = rank[0]
    ct, cv = dt[0].shape[0], dv[0].shape[0]
    rows_in_order(zt, dt, r)
    rows_in_order(zv, dv, r)
    dot_s[...] = dot_nt(zt[...], pt[...]).astype(BF)

    def back_out(rows):
        dov_s[rows, :] = dot_nt(zv[rows, :], pv[...]).astype(BF)

    tiles(zv.shape[0], cv, back_out)
    scale = CO_HEAD ** (-0.5)
    rid_t, rid_v = row_ids(nt, text, samples), row_ids(nv, regions, samples)
    for m in range(2):
        rt, rv = slice(m * nt, (m + 1) * nt), slice(m * nv, (m + 1) * nv)
        same_tv = rid_t == kv[m : m + 1, :]
        same_vt = rid_v == kt[m : m + 1, :]
        for h in range(qt.shape[2] // CO_HEAD):
            c = slice(h * CO_HEAD, (h + 1) * CO_HEAD)
            a, b, d = head_bwd(
                qt[0, rt, c], qv[1, rv, c], qv[2, rv, c], same_tv, scale, dot_s[rt, c]
            )
            dqt[0, rt, c], dqv[1, rv, c], dqv[2, rv, c] = a, b, d
            a, b, d = head_bwd(
                qv[0, rv, c], qt[1, rt, c], qt[2, rt, c], same_vt, scale, dov_s[rv, c]
            )
            dqv[0, rv, c], dqt[1, rt, c], dqt[2, rt, c] = a, b, d
    width_t, width_v = st[0].shape[1], sv[0].shape[1]
    own_t = lanes_from_own(gt[...], r, width_t)
    for k in range(Z):
        c = (r + k) & 3
        acc_t[...] = sum(dot_nt(dqt[i], wt[i, part(c, width_t), :]) for i in range(3))
        acc_t[part(r, ct), :] += own_t[:, k * width_t : (k + 1) * width_t]
        st[k][...] = acc_t[...].astype(BF)

        def back_in(rows):
            acc_v[rows, :] = sum(
                dot_nt(dqv[i, rows, :], wv[i, part(c, width_v), :]) for i in range(3)
            )

        tiles(acc_v.shape[0], cv, back_in)
        acc_v[part(r, cv), :] += gv[:, part(c, width_v)]
        sv[k][...] = acc_v[...].astype(BF)


def self_fwd(dims, *refs):
    rank, xin, kid, w, po, x, q, o, s = split(refs, 0, 4, 0, 0, 0, 0, 0, 0, 4)
    samples, step, n, head = dims
    r = rank[0]
    size = xin[0].shape[0]
    rows_in_order(x, xin, r)

    def project(rows):
        for i in range(3):
            q[i, rows, :] = dot(x[rows, :], w[i]).astype(BF)

    tiles(x.shape[0], size, project)
    rid = row_ids(n, step, samples)
    for m in range(2):
        rm = slice(m * n, (m + 1) * n)
        same = rid == kid[m : m + 1, :]
        for h in range(q.shape[2] // head):
            c = slice(h * head, (h + 1) * head)
            o[rm, c] = head_fwd(q[0, rm, c], q[1, rm, c], q[2, rm, c], same, head ** (-0.5))
    for k in range(Z):
        s[k][...] = dot(o[part((r + k) & 3, size), :], po[...]).astype(BF)


def self_bwd(dims, *refs):
    rank, din, kid, q, w, po, z, dq, s, do = split(refs, 0, 4, 0, 0, 0, 0, 0, 0, 4, 0)
    samples, step, n, head = dims
    r = rank[0]
    size = din[0].shape[0]
    rows_in_order(z, din, r)

    def back_out(rows):
        do[rows, :] = dot_nt(z[rows, :], po[...]).astype(BF)

    tiles(z.shape[0], size, back_out)
    rid = row_ids(n, step, samples)
    for m in range(2):
        rm = slice(m * n, (m + 1) * n)
        same = rid == kid[m : m + 1, :]
        for h in range(q.shape[2] // head):
            c = slice(h * head, (h + 1) * head)
            a, b, d = head_bwd(
                q[0, rm, c], q[1, rm, c], q[2, rm, c], same, head ** (-0.5), do[rm, c]
            )
            dq[0, rm, c], dq[1, rm, c], dq[2, rm, c] = a, b, d
    for k in range(Z):
        rows = part((r + k) & 3, size)
        s[k][...] = sum(dot_nt(dq[i, rows, :], w[i]) for i in range(3)).astype(BF)


def text_norm(position, *refs):
    rank, s, base, gains, shifts, z, y, yb = split(refs, 0, 4, 0, 0, 0, 0, 0, 0)
    g, b = gains[position : position + 1, :], shifts[position : position + 1, :]

    def step(rows):
        zz = base[rows, :].astype(F32) + total(s, rows)
        z[rows, :] = zz
        yy = normalise(zz)[0] * g + b
        y[rows, :] = yy
        yb[rows, :] = yy.astype(BF)

    tiles(z.shape[0], 32, step)


def text_norm_back(position, *refs):
    rank, s, base, z, gains, dz, dzb, stat = split(refs, 0, 4, 0, 0, 0, 0, 0, 0)
    g = gains[position : position + 1, :]
    stat[...] = jnp.zeros_like(stat)

    def step(rows):
        d, dg, ds = norm_back(z[rows, :], g, base[rows, :] + total(s, rows))
        dz[rows, :] = d
        dzb[rows, :] = d.astype(BF)
        stat[0:1, :] += dg
        stat[1:2, :] += ds

    tiles(z.shape[0], 32, step)


def text_turn(position, *refs):
    rank, s, base, cot, gains, shifts, out, dz, dzb, stat = split(
        refs, 0, 4, 0, 4, 0, 0, 4, 0, 0, 0
    )
    r = rank[0]
    g, b = gains[position : position + 1, :], shifts[position : position + 1, :]
    width = cot[0].shape[1]
    dy = lanes_in_order(cot, r, width)
    z = base[...] + total(s, slice(None))
    y = lanes_from_own(normalise(z)[0] * g + b, r, width)
    for k in range(Z):
        out[k][...] = y[:, k * width : (k + 1) * width].astype(BF)
    d, dg, ds = norm_back(z, g, dy)
    dz[...] = d
    dzb[...] = d.astype(BF)
    stat[0:1, :] = dg
    stat[1:2, :] = ds


def text_ffn(*refs):
    rank, xin, up, down, x, u, g, s = split(refs, 0, 4, 0, 0, 0, 0, 0, 4)
    r = rank[0]
    size = xin[0].shape[0]
    rows_in_order(x, xin, r)

    def hidden(rows):
        uu = dot(x[rows, :], up[...])
        u[rows, :] = uu
        g[rows, :] = gelu(uu).astype(BF)

    tiles(x.shape[0], size, hidden)
    for k in range(Z):
        s[k][...] = dot(g[part((r + k) & 3, size), :], down[...]).astype(BF)


def text_ffn_back(*refs):
    rank, din, up, down, u, z, du, s = split(refs, 0, 4, 0, 0, 0, 0, 0, 4)
    r = rank[0]
    size = din[0].shape[0]
    rows_in_order(z, din, r)

    def hidden(rows):
        du[rows, :] = (dot_nt(z[rows, :], down[...]) * gelu_slope(u[rows, :])).astype(BF)

    tiles(z.shape[0], size, hidden)
    for k in range(Z):
        s[k][...] = dot_nt(du[part((r + k) & 3, size), :], up[...]).astype(BF)


def image_hidden(a, w, u, g):
    width = w.shape[2]
    depth = w.shape[1] // Z
    for c in range(Z):
        cols = slice(c * width, (c + 1) * width)
        uu = dot(a[...], w[0, c * depth : (c + 1) * depth, :])
        u[:, cols] = uu
        g[:, cols] = gelu(uu).astype(BF)


def image_down(af, g, w, z):
    width = w.shape[2]
    depth = w.shape[1] // Z
    for n in range(Z):
        out = slice(n * width, (n + 1) * width)
        acc = af[:, out]
        for c in range(Z):
            cols = slice(c * width, (c + 1) * width)
            rows = slice(c * depth + n * width, c * depth + (n + 1) * width)
            acc = acc + dot_nt(g[:, cols], w[1, rows, :])
        z[:, out] = acc


def image_hidden_back(dzb, w, u, du):
    width = w.shape[2]
    depth = w.shape[1] // Z
    for c in range(Z):
        cols = slice(c * width, (c + 1) * width)
        dg = dot(dzb[...], w[1, c * depth : (c + 1) * depth, :])
        du[:, cols] = (dg * gelu_slope(u[:, cols])).astype(BF)


def image_up_back(dz, du, w, da):
    width = w.shape[2]
    depth = w.shape[1] // Z
    for n in range(Z):
        out = slice(n * width, (n + 1) * width)
        acc = dz[:, out]
        for c in range(Z):
            cols = slice(c * width, (c + 1) * width)
            rows = slice(c * depth + n * width, c * depth + (n + 1) * width)
            acc = acc + dot_nt(du[:, cols], w[0, rows, :])
        da[:, out] = acc


def image_mid(position, *refs):
    rank, s, base, w, gains, shifts, z0, a, u, g, z1, y, yb, af = split(
        refs, 0, 4, 0, 0, 0, 0, 0, 0, 0, 0, 0, 0, 0, 0
    )
    g0, b0 = gains[position : position + 1, :], shifts[position : position + 1, :]
    g1, b1 = gains[position + 1 : position + 2, :], shifts[position + 1 : position + 2, :]

    def first(rows):
        zz = base[rows, :].astype(F32) + total(s, rows)
        z0[rows, :] = zz
        aa = normalise(zz)[0] * g0 + b0
        af[rows, :] = aa
        a[rows, :] = aa.astype(BF)

    tiles(z0.shape[0], 32, first)
    image_hidden(a, w, u, g)
    image_down(af, g, w, z1)

    def second(rows):
        yy = normalise(z1[rows, :])[0] * g1 + b1
        y[rows, :] = yy
        yb[rows, :] = yy.astype(BF)

    tiles(z0.shape[0], 32, second)


def image_mid_back(position, *refs):
    rank, s, base, z1, z0, u, w, gains, d1b, du, d0, d0b, stat, d1, da = split(
        refs, 0, 4, 0, 0, 0, 0, 0, 0, 0, 0, 0, 0, 0, 0, 0
    )
    g0 = gains[position : position + 1, :]
    g1 = gains[position + 1 : position + 2, :]
    stat[...] = jnp.zeros_like(stat)

    def first(rows):
        d, dg, ds = norm_back(z1[rows, :], g1, base[rows, :] + total(s, rows))
        d1[rows, :] = d
        d1b[rows, :] = d.astype(BF)
        stat[2:3, :] += dg
        stat[3:4, :] += ds

    tiles(z0.shape[0], 32, first)
    image_hidden_back(d1b, w, u, du)
    image_up_back(d1, du, w, da)

    def second(rows):
        d, dg, ds = norm_back(z0[rows, :], g0, da[rows, :])
        d0[rows, :] = d
        d0b[rows, :] = d.astype(BF)
        stat[0:1, :] += dg
        stat[1:2, :] += ds

    tiles(z0.shape[0], 32, second)


def image_turn(position, *refs):
    (rank, s, base, cot, w, gains, shifts, out, a, g, d1b, du, d0, d0b, stat,
     z0, af, u, z1, y, dy, d1, da) = split(
        refs, 0, 4, 0, 4, 0, 0, 0, 4, 0, 0, 0, 0, 0, 0, 0, 0, 0, 0, 0, 0, 0, 0, 0
    )
    r = rank[0]
    g0, b0 = gains[position : position + 1, :], shifts[position : position + 1, :]
    g1, b1 = gains[position + 1 : position + 2, :], shifts[position + 1 : position + 2, :]
    width = cot[0].shape[1]
    stat[...] = jnp.zeros_like(stat)
    for k, ref in enumerate(cot):
        dy[:, part((r - k) & 3, width)] = ref[...].astype(F32)

    def first(rows):
        zz = base[rows, :] + total(s, rows)
        z0[rows, :] = zz
        aa = normalise(zz)[0] * g0 + b0
        af[rows, :] = aa
        a[rows, :] = aa.astype(BF)

    tiles(z0.shape[0], 32, first)
    image_hidden(a, w, u, g)
    image_down(af, g, w, z1)

    def second(rows):
        zz = z1[rows, :]
        y[rows, :] = normalise(zz)[0] * g1 + b1
        d, dg, ds = norm_back(zz, g1, dy[rows, :])
        d1[rows, :] = d
        d1b[rows, :] = d.astype(BF)
        stat[2:3, :] += dg
        stat[3:4, :] += ds

    tiles(z0.shape[0], 32, second)
    for k in range(Z):
        out[k][...] = y[:, part((r + k) & 3, width)].astype(BF)
    image_hidden_back(d1b, w, u, du)
    image_up_back(d1, du, w, da)

    def third(rows):
        d, dg, ds = norm_back(z0[rows, :], g0, da[rows, :])
        d0[rows, :] = d
        d0b[rows, :] = d.astype(BF)
        stat[0:1, :] += dg
        stat[1:2, :] += ds

    tiles(z0.shape[0], 32, third)


def image_ffn_weights(*refs):
    rank, a, du, g, dz, out = split(refs, 0, 0, 0, 0, 0, 4)
    r = rank[0]
    width = out[0].shape[2]
    for k in range(Z):
        cols = part((r + k) & 3, width)
        right_up, right_down = du[:, cols], g[:, cols]
        for n in range(Z):
            rows = slice(n * width, (n + 1) * width)
            out[k][0, rows, :] = dot_tn(a[:, rows], right_up).astype(BF)
            out[k][1, rows, :] = dot_tn(dz[:, rows], right_down).astype(BF)


def run(name, body, outs, args, scratch=()):
    flat = []
    for arg in args:
        flat.extend(arg if isinstance(arg, (list, tuple)) else [arg])
    vmem = pl.BlockSpec(memory_space=pltpu.VMEM)
    shapes, groups = [], []
    for shape, dtype, count in outs:
        groups.append(count)
        shapes.extend([jax.ShapeDtypeStruct(shape, dtype)] * max(count, 1))
    results = pl.pallas_call(
        body,
        out_shape=shapes,
        in_specs=[pl.BlockSpec(memory_space=pltpu.SMEM)] + [vmem] * (len(flat) - 1),
        out_specs=[vmem] * len(shapes),
        scratch_shapes=[pltpu.VMEM(shape, dtype) for shape, dtype in scratch],
        compiler_params=pltpu.CompilerParams(vmem_limit_bytes=48 * 1024 * 1024),
        name=name,
    )(*flat)
    return split(list(results), *groups)


def shift(values, k):
    return lax.ppermute(values, "tensor", [(i, (i + k) % Z) for i in range(Z)])


def spread(own):
    return [own] + [shift(own, k) for k in (1, 2, 3)]


def swap(chunks):
    return [chunks[0]] + [shift(chunks[k], k) for k in (1, 2, 3)]


def pad_rows(values, n):
    micro, samples, rows, width = values.shape
    flat = values.reshape(micro, samples * rows, width)
    flat = jnp.pad(flat, ((0, 0), (0, n - samples * rows), (0, 0)))
    return flat.reshape(micro * n, width)


def unpad_rows(values, shape, n):
    micro, samples, rows, width = shape
    return values.reshape(micro, n, width)[:, : samples * rows].reshape(shape)


def key_ids(lengths, rows, n):
    micro, samples = lengths.shape
    live = jnp.arange(rows, dtype=jnp.int32)[None, None, :] < lengths[:, :, None]
    ids = jnp.where(live, jnp.arange(samples, dtype=jnp.int32)[None, :, None], -1)
    ids = ids.reshape(micro, samples * rows)
    return jnp.pad(ids, ((0, 0), (0, n - samples * rows)), constant_values=-1)


def row_chunks(values, rank):
    size = values.shape[0] // Z
    return [lax.dynamic_slice_in_dim(values, ((rank + k) & 3) * size, size, 0) for k in range(Z)]


def from_row_chunks(chunks, rank, shape, n):
    joined = jnp.concatenate(
        [chunks[0], chunks[3], chunks[2], chunks[1]] * 2, axis=0
    )
    size = chunks[0].shape[0]
    ordered = lax.dynamic_slice_in_dim(joined, ((Z - rank) & 3) * size, size * Z, 0)
    return unpad_rows(ordered, shape, n).astype(F32)


def weight_grad(left, right):
    return dot_tn(left, right).astype(BF)


def shards(
    text_in, image_in, caption_len, region_count, text_cot, image_cot,
    co_text_qkv, co_image_qkv, co_text_out, co_image_out,
    co_text_up, co_text_down, co_image_up, co_image_down,
    self_text_qkv, self_image_qkv, self_text_out, self_image_out,
    text_up, text_down, image_up, image_down,
    text_gains, text_shifts, image_gains, image_shifts,
):
    rank = lax.axis_index("tensor")
    place = lax.axis_index("dp")
    n_dp = lax.axis_size("dp")
    rk = rank.reshape(1).astype(jnp.int32)
    micro, samples, text, wt = text_in.shape
    regions, wv = image_in.shape[2:]
    dt, dv = wt * Z, wv * Z
    nt = -(-samples * text // 64) * 64
    nv = -(-samples * regions // 64) * 64
    rt, rv = micro * nt, micro * nv
    ct, cv = rt // Z, rv // Z
    co_w = co_text_qkv.shape[2]
    st_w = self_text_qkv.shape[2]
    si_w = self_image_qkv.shape[2]
    ft = co_text_up.shape[1]

    def gathered(up, down):
        cut = up.shape[0] // n_dp
        mine = lax.dynamic_slice_in_dim(up, place * cut, cut, 0)
        other = lax.dynamic_slice_in_dim(down, place * cut, cut, 1).T
        return lax.all_gather(jnp.stack([mine, other]), ("tensor", "dp"), axis=1, tiled=True)

    tin = spread(pad_rows(text_in, nt))
    vin = spread(pad_rows(image_in, nv))
    w_mid = gathered(co_image_up, co_image_down)
    w_end = gathered(image_up, image_down)
    tcot = swap(row_chunks(pad_rows(text_cot, nt), rank))
    vcot = swap(row_chunks(pad_rows(image_cot, nv), rank))
    kt = key_ids(caption_len, text, nt)
    kv = key_ids(region_count, regions, nv)

    co_dims = (samples, text, regions, nt, nv)
    text_dims = (samples, text, nt, TEXT_HEAD)
    image_dims = (samples, regions, nv, IMAGE_HEAD)

    xt0, xv0, bt, bv, qt0, qv0, ot0, ov0, st, sv = run(
        "co_fwd", functools.partial(co_fwd, co_dims),
        [((rt, dt), BF, 0), ((rv, dv), BF, 0), ((ct, dt), BF, 0), ((cv, dv), BF, 0),
         ((3, rt, co_w), BF, 0), ((3, rv, co_w), BF, 0), ((rt, co_w), BF, 0), ((rv, co_w), BF, 0),
         ((ct, dt), BF, Z), ((cv, dv), BF, Z)],
        [rk, tin, vin, kt, kv, co_text_qkv, co_image_qkv, co_text_out, co_image_out],
    )
    norm_t = [((ct, dt), F32, 0), ((ct, dt), F32, 0), ((ct, dt), BF, 0)]
    zt0, at, atb = run(
        "text_norm0", functools.partial(text_norm, 0), norm_t,
        [rk, swap(st), bt, text_gains, text_shifts],
    )
    ffn_t = [((rt, dt), BF, 0), ((rt, ft), F32, 0), ((rt, ft), BF, 0), ((ct, dt), BF, Z)]
    xt1, ut1, gt1, st = run(
        "text_ffn1", text_ffn, ffn_t, [rk, spread(atb), co_text_up, co_text_down]
    )
    zv0, av, uv1, gv1, zv1, bv, bvb = run(
        "image_mid", functools.partial(image_mid, 0),
        [((cv, dv), F32, 0), ((cv, dv), BF, 0), ((cv, dv), F32, 0), ((cv, dv), BF, 0),
         ((cv, dv), F32, 0), ((cv, dv), F32, 0), ((cv, dv), BF, 0)],
        [rk, swap(sv), bv, w_mid, image_gains, image_shifts],
        [((cv, dv), F32)],
    )
    zt1, bt, btb = run(
        "text_norm1", functools.partial(text_norm, 1), norm_t,
        [rk, swap(st), at, text_gains, text_shifts],
    )
    xv2, qv2, ov2, sv = run(
        "image_self", functools.partial(self_fwd, image_dims),
        [((rv, dv), BF, 0), ((3, rv, si_w), BF, 0), ((rv, si_w), BF, 0), ((cv, dv), BF, Z)],
        [rk, spread(bvb), kv, self_image_qkv, self_image_out],
    )
    xt2, qt2, ot2, st = run(
        "text_self", functools.partial(self_fwd, text_dims),
        [((rt, dt), BF, 0), ((3, rt, st_w), BF, 0), ((rt, st_w), BF, 0), ((ct, dt), BF, Z)],
        [rk, spread(btb), kt, self_text_qkv, self_text_out],
    )
    out_v, av3, gv3, dv3, duv3, gv, gvb, stat_v1 = run(
        "image_turn", functools.partial(image_turn, 2),
        [((cv, wv), BF, Z), ((cv, dv), BF, 0), ((cv, dv), BF, 0), ((cv, dv), BF, 0),
         ((cv, dv), BF, 0), ((cv, dv), F32, 0), ((cv, dv), BF, 0), ((4, dv), F32, 0)],
        [rk, swap(sv), bv, vcot, w_end, image_gains, image_shifts],
        [((cv, dv), F32)] * 8,
    )
    zt2, ctf, ctb = run(
        "text_norm2", functools.partial(text_norm, 2), norm_t,
        [rk, swap(st), bt, text_gains, text_shifts],
    )
    xt3, ut3, gt3, st = run("text_ffn3", text_ffn, ffn_t, [rk, spread(ctb), text_up, text_down])
    out_t, gt, gtb, stat_t3 = run(
        "text_turn", functools.partial(text_turn, 3),
        [((ct, wt), BF, Z), ((ct, dt), F32, 0), ((ct, dt), BF, 0), ((2, dt), F32, 0)],
        [rk, swap(st), ctf, tcot, text_gains, text_shifts],
    )
    text_out = from_row_chunks(swap(out_t), rank, text_in.shape, nt)
    image_out = from_row_chunks(swap(out_v), rank, image_in.shape, nv)

    back_ffn = [((rt, dt), BF, 0), ((rt, ft), BF, 0), ((ct, dt), BF, Z)]
    back_norm = [((ct, dt), F32, 0), ((ct, dt), BF, 0), ((2, dt), F32, 0)]
    dt3, dut3, st = run(
        "text_ffn3_back", text_ffn_back, back_ffn, [rk, spread(gtb), text_up, text_down, ut3]
    )
    dv2, dqv2, sv = run(
        "image_self_back", functools.partial(self_bwd, image_dims),
        [((rv, dv), BF, 0), ((3, rv, si_w), BF, 0), ((cv, dv), BF, Z)],
        [rk, spread(gvb), kv, qv2, self_image_qkv, self_image_out],
        [((rv, si_w), BF)],
    )
    gt, gtb, stat_t2 = run(
        "text_norm2_back", functools.partial(text_norm_back, 2), back_norm,
        [rk, swap(st), gt, zt2, text_gains],
    )
    dt2, dqt2, st = run(
        "text_self_back", functools.partial(self_bwd, text_dims),
        [((rt, dt), BF, 0), ((3, rt, st_w), BF, 0), ((ct, dt), BF, Z)],
        [rk, spread(gtb), kt, qt2, self_text_qkv, self_text_out],
        [((rt, st_w), BF)],
    )
    dv1, duv1, gv, gvb, stat_v0 = run(
        "image_mid_back", functools.partial(image_mid_back, 0),
        [((cv, dv), BF, 0), ((cv, dv), BF, 0), ((cv, dv), F32, 0), ((cv, dv), BF, 0),
         ((4, dv), F32, 0)],
        [rk, swap(sv), gv, zv1, zv0, uv1, w_mid, image_gains],
        [((cv, dv), F32)] * 2,
    )
    gt, gtb, stat_t1 = run(
        "text_norm1_back", functools.partial(text_norm_back, 1), back_norm,
        [rk, swap(st), gt, zt1, text_gains],
    )
    dt1, dut1, st = run(
        "text_ffn1_back", text_ffn_back, back_ffn, [rk, spread(gtb), co_text_up, co_text_down, ut1]
    )
    gt, gtb, stat_t0 = run(
        "text_norm0_back", functools.partial(text_norm_back, 0), back_norm,
        [rk, swap(st), gt, zt0, text_gains],
    )
    dt0, dv0, dqt0, dqv0, st, sv = run(
        "co_back", functools.partial(co_bwd, co_dims),
        [((rt, dt), BF, 0), ((rv, dv), BF, 0), ((3, rt, co_w), BF, 0), ((3, rv, co_w), BF, 0),
         ((rt, wt), BF, Z), ((rv, wv), BF, Z)],
        [rk, spread(gtb), spread(gvb), kt, kv, qt0, qv0, co_text_qkv, co_image_qkv,
         co_text_out, co_image_out, gt, gv],
        [((rt, co_w), BF), ((rv, co_w), BF), ((rt, wt), F32), ((rv, wv), F32)],
    )
    text_grad = sum(piece.astype(F32) for piece in swap(st))
    image_grad = sum(piece.astype(F32) for piece in swap(sv))
    text_grad = unpad_rows(text_grad, text_in.shape, nt)
    image_grad = unpad_rows(image_grad, image_in.shape, nv)

    def image_ffn_grad(name, a, du, g, dz):
        (pieces,) = run(name, image_ffn_weights, [((2, dv, wv), BF, Z)], [rk, a, du, g, dz])
        return sum(piece.astype(F32) for piece in swap(pieces)).astype(BF)

    end_ffn = image_ffn_grad("image_ffn3_weights", av3, duv3, gv3, dv3)
    mid_ffn = image_ffn_grad("image_ffn1_weights", av, duv1, gv1, dv1)
    stats = jnp.concatenate(
        [
            jnp.pad(
                jnp.concatenate([stat_t0, stat_t1, stat_t2, stat_t3], axis=0),
                ((0, 0), (0, dv - dt)),
            ),
            stat_v0,
            stat_v1,
        ],
        axis=0,
    )
    stats = sum(spread(stats)).astype(BF)
    parts = [
        weight_grad(xt0, dqt0[0]), weight_grad(xt0, dqt0[1]), weight_grad(xt0, dqt0[2]),
        weight_grad(xv0, dqv0[0]), weight_grad(xv0, dqv0[1]), weight_grad(xv0, dqv0[2]),
        weight_grad(ot0, dt0), weight_grad(ov0, dv0),
        weight_grad(xt1, dut1), weight_grad(gt1, dt1),
        mid_ffn,
        weight_grad(xt2, dqt2[0]), weight_grad(xt2, dqt2[1]), weight_grad(xt2, dqt2[2]),
        weight_grad(xv2, dqv2[0]), weight_grad(xv2, dqv2[1]), weight_grad(xv2, dqv2[2]),
        weight_grad(ot2, dt2), weight_grad(ov2, dv2),
        weight_grad(xt3, dut3), weight_grad(gt3, dt3),
        end_ffn,
        stats,
    ]
    parts = [member.astype(F32) for member in lax.psum(tuple(parts), "dp")]
    mid_ffn, end_ffn, stats = parts[10], parts[21], parts[22]
    text_stats = stats[:8, :dt].reshape(4, 2, dt)
    image_stats = stats[8:16].reshape(4, 2, dv)
    return (
        text_out, image_out, text_grad, image_grad,
        jnp.stack(parts[0:3]), jnp.stack(parts[3:6]), parts[6], parts[7],
        parts[8], parts[9], mid_ffn[0], mid_ffn[1].T,
        jnp.stack(parts[11:14]), jnp.stack(parts[14:17]), parts[17], parts[18],
        parts[19], parts[20], end_ffn[0], end_ffn[1].T,
        text_stats[:, 0], text_stats[:, 1], image_stats[:, 0], image_stats[:, 1],
    )


def solution(mesh):
    stream = P(None, "dp", None, "tensor")
    lengths = P(None, "dp")
    stacked = P(None, None, "tensor")
    rows = P("tensor", None)
    cols = P(None, "tensor")
    weights = (
        stacked, stacked, rows, rows, cols, rows, cols, rows,
        stacked, stacked, rows, rows, cols, rows, cols, rows,
        P(), P(), P(), P(),
    )
    in_specs = (stream, stream, lengths, lengths, stream, stream) + weights
    out_specs = (stream,) * 4 + weights
    return jax.shard_map(shards, mesh=mesh, in_specs=in_specs, out_specs=out_specs, check_vma=False)
```

```python
import functools
import math

import jax
import jax.numpy as jnp
from jax import lax
from jax.experimental import pallas as pl
from jax.experimental.pallas import tpu as pltpu
from jax.sharding import PartitionSpec as P

CO_HEAD = 128
TEXT_HEAD = 64
IMAGE_HEAD = 128
EPS = 1e-05
FILL = -1000000000.0
ROOT_HALF = 0.7071067811865476
INV_ROOT_TWO_PI = 0.3989422804014327
F32 = jnp.float32
BF = jnp.bfloat16
Z = 4
SHORT = pl.CostEstimate(flops=1000, bytes_accessed=1000, transcendentals=0)
LENGTHS = 5


def dot(a, b):
    return lax.dot_general(a, b, (((1,), (0,)), ((), ())), preferred_element_type=F32)


def dot_nt(a, b):
    return lax.dot_general(a, b, (((1,), (1,)), ((), ())), preferred_element_type=F32)


def dot_tn(a, b):
    return lax.dot_general(a, b, (((0,), (0,)), ((), ())), preferred_element_type=F32)


def part(index, size):
    return pl.ds(pl.multiple_of(index * size, size), size)


def row_ids(count, step, samples):
    place = lax.broadcasted_iota(jnp.int32, (count, 1), 0)
    ids = jnp.zeros((count, 1), jnp.int32)
    for s in range(1, samples):
        ids = ids + (place >= s * step).astype(jnp.int32)
    return ids


def key_ids(pos, first, m, step, samples, count):
    place = lax.broadcasted_iota(jnp.int32, (1, count), 1)
    ids = jnp.full((1, count), -1, jnp.int32)
    for s in range(samples):
        live = pos[first + m * samples + s]
        ids = jnp.where((place >= s * step) & (place < s * step + live), s, ids)
    return ids


def probabilities(q, k, same, scale):
    s = jnp.where(same, dot_nt(q, k) * scale, FILL)
    e = jnp.exp(s - jnp.max(s, axis=-1, keepdims=True))
    return e / jnp.sum(e, axis=-1, keepdims=True)


def head_fwd(q, k, v, same, scale):
    return dot(probabilities(q, k, same, scale).astype(BF), v).astype(BF)


def head_bwd(q, k, v, same, scale, do):
    p = probabilities(q, k, same, scale)
    dv = dot_tn(p.astype(BF), do)
    dp = dot_nt(do, v)
    ds = (p * (dp - jnp.sum(dp * p, axis=-1, keepdims=True))).astype(BF)
    dq = dot(ds, k) * scale
    dk = dot_tn(ds, q) * scale
    return dq.astype(BF), dk.astype(BF), dv.astype(BF)


def gelu(u):
    return u * (1.0 + lax.erf(u * ROOT_HALF)) * 0.5


def gelu_slope(u):
    return (1.0 + lax.erf(u * ROOT_HALF)) * 0.5 + u * jnp.exp(u * u * -0.5) * INV_ROOT_TWO_PI


def normalise(z):
    centre = z - jnp.mean(z, axis=-1, keepdims=True)
    rstd = lax.rsqrt(jnp.mean(centre * centre, axis=-1, keepdims=True) + EPS)
    return centre * rstd, rstd


def norm_back(z, gain, dy):
    xhat, rstd = normalise(z)
    dxh = dy * gain
    dz = rstd * (
        dxh
        - jnp.mean(dxh, axis=-1, keepdims=True)
        - xhat * jnp.mean(dxh * xhat, axis=-1, keepdims=True)
    )
    return dz, jnp.sum(dy * xhat, axis=0, keepdims=True), jnp.sum(dy, axis=0, keepdims=True)


class Arriving:
    in_loop = False

    def __init__(self, ref, copy):
        self.ref, self.copy = ref, copy
        self.shape, self.dtype = ref.shape, ref.dtype

    def wait(self):
        if self.copy is not None:
            assert not Arriving.in_loop
            self.copy.wait()
            self.copy = None

    def __getitem__(self, index):
        self.wait()
        return self.ref[index]

    @property
    def at(self):
        self.wait()
        return self.ref.at


class View:
    def __init__(self, array, index, shape):
        self.array, self.index, self.shape, self.dtype = array, index, shape, array.dtype


class Leaving:
    def __init__(self, ref, target, sem):
        self.ref, self.target, self.sem, self.sent = ref, target, sem, False
        self.copy = pltpu.make_async_copy(ref, target, sem)
        self.shape, self.dtype, self.at = ref.shape, ref.dtype, ref.at

    def send(self):
        if not self.sent:
            self.copy.start()
            self.sent = True

    def __getitem__(self, index):
        return self.ref[index]

    def __setitem__(self, index, value):
        assert not self.sent
        self.ref[index] = value


def send(*refs):
    for ref in refs:
        for one in ref if isinstance(ref, list) else [ref]:
            one.send()


def ready(*refs):
    for ref in refs:
        for one in ref if isinstance(ref, list) else [ref]:
            one.wait()


def tiles(count, tile, body):
    def step(i, carry):
        body(part(i, tile))
        return carry

    Arriving.in_loop = True
    lax.fori_loop(0, count // tile, step, 0)
    Arriving.in_loop = False


def total(refs, rows):
    acc = refs[0][rows, :].astype(F32)
    for ref in refs[1:]:
        acc = acc + ref[rows, :].astype(F32)
    return acc


def lanes_in_order(values, r, width):
    near = [values[0], values[3], values[2], values[1]]
    joined = jnp.concatenate([value.astype(F32) for value in near], axis=1)
    return pltpu.roll(joined, r * width, 1)


def lanes_from_own(values, r, width):
    return pltpu.roll(values, ((Z - r) & 3) * width, 1)


def rows_in_order(full, refs, r):
    size = refs[0].shape[0]
    for k, ref in enumerate(refs):
        full[part((r - k) & 3, size), :] = ref[...]


def packed_rows(rows, width, wide):
    return rows * width // wide if width < wide else rows


def put_text(ref, at, value):
    rows, width = value.shape
    wide = ref.shape[1]
    main = packed_rows(rows, width, wide)
    rest = rows - main
    ref[at : at + main, 0:width] = value[0:main]
    for j in range(width // (wide - width)):
        cols = slice(j * (wide - width), (j + 1) * (wide - width))
        ref[at + j * rest : at + (j + 1) * rest, width:wide] = value[main:rows, cols]


def get_text(ref, at, rows, width):
    wide = ref.shape[1]
    if width == wide:
        return ref[at : at + rows, :]
    main = packed_rows(rows, width, wide)
    rest = rows - main
    tail = [
        ref[at + j * rest : at + (j + 1) * rest, width:wide]
        for j in range(width // (wide - width))
    ]
    return jnp.concatenate([ref[at : at + main, 0:width], jnp.concatenate(tail, axis=1)], axis=0)


def both_in_order(xt, xv, both, r):
    ct, cv = xt.shape[0] // Z, xv.shape[0] // Z
    for k, ref in enumerate(both):
        src = (r - k) & 3
        xv[part(src, cv), :] = ref[0:cv, :]
        xt[part(src, ct), :] = get_text(ref, cv, ct, xt.shape[1])


def split(refs, *counts):
    found, at = [], 0
    for count in counts:
        found.append(refs[at] if count == 0 else list(refs[at : at + count]))
        at += max(count, 1)
    assert at == len(refs)
    return found


def co_fwd(dims, *refs):
    rank, both, wt, wv, pt, pv, xt, xv, bt, bv, qt, qv, ot, ov, s = split(
        refs, 0, 4, 0, 0, 0, 0, 0, 0, 0, 0, 0, 0, 0, 0, 4
    )
    samples, text, regions, nt, nv = dims
    r = rank[0]
    rows_t, rows_v = xt.shape[0], xv.shape[0]
    width_t, width_v = xt.shape[1] // Z, xv.shape[1] // Z
    ct, cv = bt.shape[0], bv.shape[0]
    tin = [get_text(ref, rows_v, rows_t, width_t) for ref in both]
    xt[...] = lanes_in_order(tin, r, width_t).astype(BF)
    for k, ref in enumerate(both):
        xv[:, part((r - k) & 3, width_v)] = ref[0:rows_v, :]
    bt[...] = xt[part(r, ct), :]
    bv[...] = xv[part(r, cv), :]
    send(xt, xv, bt, bv)
    for i in range(3):
        qt[i] = dot(xt[...], wt[i]).astype(BF)

    def project(rows):
        for i in range(3):
            qv[i, rows, :] = dot(xv[rows, :], wv[i]).astype(BF)

    ready(wv)
    tiles(xv.shape[0], cv, project)
    send(qt, qv)
    scale = CO_HEAD ** (-0.5)
    rid_t, rid_v = row_ids(nt, text, samples), row_ids(nv, regions, samples)
    for m in range(2):
        rt, rv = slice(m * nt, (m + 1) * nt), slice(m * nv, (m + 1) * nv)
        same_tv = rid_t == key_ids(rank, LENGTHS + 2 * samples, m, regions, samples, nv)
        same_vt = rid_v == key_ids(rank, LENGTHS, m, text, samples, nt)
        for h in range(qt.shape[2] // CO_HEAD):
            c = slice(h * CO_HEAD, (h + 1) * CO_HEAD)
            ot[rt, c] = head_fwd(qt[0, rt, c], qv[1, rv, c], qv[2, rv, c], same_tv, scale)
            ov[rv, c] = head_fwd(qv[0, rv, c], qt[1, rt, c], qt[2, rt, c], same_vt, scale)
    for k in range(Z):
        c = (r + k) & 3
        s[k][0:cv, :] = dot(ov[part(c, cv), :], pv[...]).astype(BF)
        put_text(s[k], cv, dot(ot[part(c, ct), :], pt[...]).astype(BF))
        send(s[k])


def co_bwd(dims, *refs):
    (rank, both, qt, qv, pt, pv, xt, xv, ot, ov,
     dqt, dqv, tq, vq, to, vo, zt, zv, dot_s, dov_s) = split(
        refs, 0, 4, *([0] * 18)
    )
    samples, text, regions, nt, nv = dims
    r = rank[0]
    cv = zv.shape[0] // Z
    both_in_order(zt, zv, both, r)
    dot_s[...] = dot_nt(zt[...], pt[...]).astype(BF)

    def back_out(rows):
        dov_s[rows, :] = dot_nt(zv[rows, :], pv[...]).astype(BF)

    ready(pv)
    tiles(zv.shape[0], cv, back_out)
    scale = CO_HEAD ** (-0.5)
    rid_t, rid_v = row_ids(nt, text, samples), row_ids(nv, regions, samples)
    for m in range(2):
        rt, rv = slice(m * nt, (m + 1) * nt), slice(m * nv, (m + 1) * nv)
        same_tv = rid_t == key_ids(rank, LENGTHS + 2 * samples, m, regions, samples, nv)
        same_vt = rid_v == key_ids(rank, LENGTHS, m, text, samples, nt)
        for h in range(qt.shape[2] // CO_HEAD):
            c = slice(h * CO_HEAD, (h + 1) * CO_HEAD)
            a, b, d = head_bwd(
                qt[0, rt, c], qv[1, rv, c], qv[2, rv, c], same_tv, scale, dot_s[rt, c]
            )
            dqt[0, rt, c], dqv[1, rv, c], dqv[2, rv, c] = a, b, d
            a, b, d = head_bwd(
                qv[0, rv, c], qt[1, rt, c], qt[2, rt, c], same_vt, scale, dov_s[rv, c]
            )
            dqv[0, rv, c], dqt[1, rt, c], dqt[2, rt, c] = a, b, d
    send(dqt, dqv)
    for i in range(3):
        matrix_whole(tq.at[i], xt, dqt.at[i])
        matrix_whole(vq.at[i], xv, dqv.at[i])
    send(tq, vq)
    matrix_whole(to, ot, zt)
    matrix_whole(vo, ov, zv)


def co_bwd_in(*refs):
    rank, dqt, dqv, wt, wv, gt, gv, s, acc_t, acc_v = split(
        refs, 0, 0, 0, 0, 0, 0, 0, 4, 0, 0
    )
    r = rank[0]
    rows_v = acc_v.shape[0]
    ct, cv = gt.shape[0], gv.shape[0]
    width_t, width_v = acc_t.shape[1], acc_v.shape[1]
    own_t = lanes_from_own(gt[...], r, width_t)
    for k in range(Z):
        c = (r + k) & 3
        acc_t[...] = sum(dot_nt(dqt[i], wt[i, part(c, width_t), :]) for i in range(3))
        acc_t[part(r, ct), :] += own_t[:, k * width_t : (k + 1) * width_t]
        put_text(s[k], rows_v, acc_t[...].astype(BF))

        ready(wv, dqv)

        def back_in(rows):
            acc_v[rows, :] = sum(
                dot_nt(dqv[i, rows, :], wv[i, part(c, width_v), :]) for i in range(3)
            )

        tiles(acc_v.shape[0], cv, back_in)
        acc_v[part(r, cv), :] += gv[:, part(c, width_v)]
        s[k][0:rows_v, :] = acc_v[...].astype(BF)
        send(s[k])


def self_fwd(dims_t, dims_v, *refs):
    rank, both, wt, wv, pt, pv, xt, xv, qt, qv, ot, ov, s = split(
        refs, 0, 4, 0, 0, 0, 0, 0, 0, 0, 0, 0, 0, 4
    )
    r = rank[0]
    ct, cv = xt.shape[0] // Z, xv.shape[0] // Z
    both_in_order(xt, xv, both, r)
    send(xt, xv)
    for dims, x, w, q, o in ((dims_v, xv, wv, qv, ov), (dims_t, xt, wt, qt, ot)):
        samples, step, n, head, first = dims

        def project(rows, x=x, w=w, q=q):
            for i in range(3):
                q[i, rows, :] = dot(x[rows, :], w[i]).astype(BF)

        ready(w)
        tiles(x.shape[0], x.shape[0] // Z, project)
        send(q)
        rid = row_ids(n, step, samples)
        for m in range(2):
            rm = slice(m * n, (m + 1) * n)
            same = rid == key_ids(rank, first, m, step, samples, n)
            for h in range(q.shape[2] // head):
                c = slice(h * head, (h + 1) * head)
                o[rm, c] = head_fwd(q[0, rm, c], q[1, rm, c], q[2, rm, c], same, head ** (-0.5))
    for k in range(Z):
        c = (r + k) & 3
        s[k][0:cv, :] = dot(ov[part(c, cv), :], pv[...]).astype(BF)
        put_text(s[k], cv, dot(ot[part(c, ct), :], pt[...]).astype(BF))
        send(s[k])


def self_bwd(dims_t, dims_v, *refs):
    (rank, both, qt, qv, wt, wv, pt, pv,
     zt, zv, dqt, dqv, s, dot_s, dov_s) = split(
        refs, 0, 4, 0, 0, 0, 0, 0, 0, 0, 0, 0, 0, 4, 0, 0
    )
    r = rank[0]
    ct, cv = zt.shape[0] // Z, zv.shape[0] // Z
    both_in_order(zt, zv, both, r)
    send(zt, zv)
    for dims, z, po, q, do, dq in (
        (dims_v, zv, pv, qv, dov_s, dqv),
        (dims_t, zt, pt, qt, dot_s, dqt),
    ):
        samples, step, n, head, first = dims

        def back_out(rows, z=z, po=po, do=do):
            do[rows, :] = dot_nt(z[rows, :], po[...]).astype(BF)

        ready(po)
        tiles(z.shape[0], z.shape[0] // Z, back_out)
        rid = row_ids(n, step, samples)
        for m in range(2):
            rm = slice(m * n, (m + 1) * n)
            same = rid == key_ids(rank, first, m, step, samples, n)
            for h in range(q.shape[2] // head):
                c = slice(h * head, (h + 1) * head)
                a, b, d = head_bwd(
                    q[0, rm, c], q[1, rm, c], q[2, rm, c], same, head ** (-0.5), do[rm, c]
                )
                dq[0, rm, c], dq[1, rm, c], dq[2, rm, c] = a, b, d
    for k in range(Z):
        c = (r + k) & 3
        rows = part(c, cv)
        s[k][0:cv, :] = sum(dot_nt(dqv[i, rows, :], wv[i]) for i in range(3)).astype(BF)
        rows = part(c, ct)
        put_text(s[k], cv, sum(dot_nt(dqt[i, rows, :], wt[i]) for i in range(3)).astype(BF))


def text_total(base, s):
    rows, width = base.shape
    at = s[0].shape[0] - packed_rows(rows, width, s[0].shape[1])
    acc = base[...].astype(F32)
    for ref in s:
        acc = acc + get_text(ref, at, rows, width).astype(F32)
    return acc


def send_text(out, value, image):
    if image is not None:
        out[0 : image.shape[0], :] = image[...]
        put_text(out, image.shape[0], value)
    else:
        out[...] = value


def cut(*refs):
    pos, whole, out = split(refs, 0, 0, 4)
    for k in range(Z):
        out[k][...] = whole[(pos[0] + k) & 3]


def text_norm(position, joint, *refs):
    rank, s, base, gains, shifts, image, z, y, out = split(
        refs if joint else list(refs[:8]) + [None] + list(refs[8:]), 0, 4, 0, 0, 0, 0, 0, 0, 0
    )
    zz = text_total(base, s)
    z[...] = zz
    yy = normalise(zz)[0] * gains[position : position + 1, :] + shifts[position : position + 1, :]
    y[...] = yy
    send_text(out, yy.astype(BF), image)


def text_norm_back(position, joint, *refs):
    rank, s, base, z, gains, image, dz, out, stat = split(
        refs if joint else list(refs[:8]) + [None] + list(refs[8:]), 0, 4, 0, 0, 0, 0, 0, 0, 0
    )
    d, dg, ds = norm_back(z[...], gains[position : position + 1, :], text_total(base, s))
    dz[...] = d
    send_text(out, d.astype(BF), image)
    stat[0:1, :] = dg
    stat[1:2, :] = ds


def text_norm_back_stats(position, *refs):
    rank, s, base, z, gains, image, stats_t, stats_v, dz, out = split(
        refs, 0, 4, 0, 0, 0, 0, 2, 2, 0, 0
    )
    d, dg, ds = norm_back(z[...], gains[position : position + 1, :], text_total(base, s))
    dz[...] = d
    send_text(out, d.astype(BF), image)
    wide = out.shape[1]
    short = [dg, ds] + [ref[...] for ref in stats_t]
    short = jnp.concatenate(short, axis=0)
    short = jnp.concatenate(
        [short, jnp.zeros((short.shape[0], wide - short.shape[1]), F32)], axis=1
    )
    every = jnp.concatenate([short] + [ref[...] for ref in stats_v], axis=0)
    out[out.shape[0] - every.shape[0] : out.shape[0], :] = every.astype(BF)


def text_turn(position, *refs):
    (rank, s, base, cot, image, image_back, w, gains, shifts, out, a, g, d1b, du, dz, send_on, stat,
     u, x, d1) = split(refs, 0, 4, 0, 4, 4, 0, 0, 0, 0, 4, 0, 0, 0, 0, 0, 0, 0, 0, 0, 0)
    r = rank[0]
    g0, b0 = gains[position : position + 1, :], shifts[position : position + 1, :]
    g1, b1 = gains[position + 1 : position + 2, :], shifts[position + 1 : position + 2, :]
    rows, width = base.shape[0], base.shape[1] // Z
    at = image[0].shape[0]
    wide, deep = w.shape[2], base.shape[1]
    blocks = deep // wide
    z0 = text_total(base, s)
    x[...] = normalise(z0)[0] * g0 + b0
    a[...] = x[...].astype(BF)
    send(a)
    down = blocks * deep
    for c in range(Z):
        for j in range(blocks):
            cols = slice((c * blocks + j) * wide, (c * blocks + j + 1) * wide)
            uu = dot(a[...], w[c, j * deep : (j + 1) * deep, :])
            u[:, cols] = uu
            g[:, cols] = gelu(uu).astype(BF)
    send(g)
    for j in range(blocks):
        cols = slice(j * wide, (j + 1) * wide)
        acc = x[:, cols]
        for c in range(Z):
            own = slice(c * deep, (c + 1) * deep)
            acc = acc + dot(g[:, own], w[c, down + j * deep : down + (j + 1) * deep, :])
        x[:, cols] = acc
    z1 = x[...]
    y = lanes_from_own(normalise(z1)[0] * g1 + b1, r, width)
    for k in range(Z):
        send_text(out[k], y[:, k * width : (k + 1) * width].astype(BF), image[k])
        send(out[k])
    dy = lanes_in_order([get_text(ref, at, rows, width) for ref in cot], r, width)
    d, dg, ds = norm_back(z1, g1, dy)
    d1[...] = d
    d1b[...] = d.astype(BF)
    send(d1b)
    stat[2:3, :] = dg
    stat[3:4, :] = ds
    for c in range(Z):
        own = slice(c * deep, (c + 1) * deep)
        back = sum(
            dot_nt(
                d1b[:, j * wide : (j + 1) * wide],
                w[c, down + j * deep : down + (j + 1) * deep, :],
            )
            for j in range(blocks)
        )
        du[:, own] = (back * gelu_slope(u[:, own])).astype(BF)
    send(du)
    back = d1[...]
    for c in range(Z):
        for j in range(blocks):
            cols = slice((c * blocks + j) * wide, (c * blocks + j + 1) * wide)
            back = back + dot_nt(du[:, cols], w[c, j * deep : (j + 1) * deep, :])
    d, dg, ds = norm_back(z0, g0, back)
    dz[...] = d
    send_text(send_on, d.astype(BF), image_back)
    stat[0:1, :] = dg
    stat[1:2, :] = ds


def text_ffn(*refs):
    rank, xin, up, down, x, u, g, s = split(refs, 0, 4, 0, 0, 0, 0, 0, 4)
    r = rank[0]
    size = xin[0].shape[0]
    rows_in_order(x, xin, r)

    def hidden(rows):
        uu = dot(x[rows, :], up[...])
        u[rows, :] = uu
        g[rows, :] = gelu(uu).astype(BF)

    ready(up)
    tiles(x.shape[0], size, hidden)
    send(x, u, g)
    for k in range(Z):
        s[k][...] = dot(g[part((r + k) & 3, size), :], down[...]).astype(BF)
        send(s[k])


def text_ffn_back(*refs):
    rank, din, up, down, u, z, du, s = split(refs, 0, 4, 0, 0, 0, 0, 0, 4)
    r = rank[0]
    size = din[0].shape[0]
    rows_in_order(z, din, r)

    def hidden(rows):
        du[rows, :] = (dot_nt(z[rows, :], down[...]) * gelu_slope(u[rows, :])).astype(BF)

    ready(down, u)
    tiles(z.shape[0], size, hidden)
    send(z, du)
    for k in range(Z):
        s[k][...] = dot_nt(du[part((r + k) & 3, size), :], up[...]).astype(BF)


def image_hidden(a, w, u, g):
    width = w.shape[2]
    depth = w.shape[1] // 2
    for c in range(Z):
        cols = slice(c * width, (c + 1) * width)
        uu = dot(a[...], w[c, 0:depth, :])
        u[:, cols] = uu
        g[:, cols] = gelu(uu).astype(BF)


def image_down(af, g, w, z):
    width = w.shape[2]
    depth = w.shape[1] // 2
    for n in range(Z):
        out = slice(n * width, (n + 1) * width)
        acc = af[:, out]
        rows = slice(depth + n * width, depth + (n + 1) * width)
        for c in range(Z):
            cols = slice(c * width, (c + 1) * width)
            acc = acc + dot(g[:, cols], w[c, rows, :])
        z[:, out] = acc


def image_hidden_back(dzb, w, u, du):
    width = w.shape[2]
    depth = w.shape[1] // 2
    for c in range(Z):
        cols = slice(c * width, (c + 1) * width)
        dg = sum(
            dot_nt(
                dzb[:, n * width : (n + 1) * width],
                w[c, depth + n * width : depth + (n + 1) * width, :],
            )
            for n in range(Z)
        )
        du[:, cols] = (dg * gelu_slope(u[:, cols])).astype(BF)


def image_up_back(dz, du, w, da):
    width = w.shape[2]
    width = w.shape[2]
    for n in range(Z):
        out = slice(n * width, (n + 1) * width)
        acc = dz[:, out]
        for c in range(Z):
            cols = slice(c * width, (c + 1) * width)
            acc = acc + dot_nt(du[:, cols], w[c, n * width : (n + 1) * width, :])
        da[:, out] = acc


def image_mid(position, *refs):
    rank, s, base, w, gains, shifts, z0, a, u, g, z1, y, yb, af = split(
        refs, 0, 4, 0, 0, 0, 0, 0, 0, 0, 0, 0, 0, 0, 0
    )
    g0, b0 = gains[position : position + 1, :], shifts[position : position + 1, :]
    g1, b1 = gains[position + 1 : position + 2, :], shifts[position + 1 : position + 2, :]

    def first(rows):
        zz = base[rows, :].astype(F32) + total(s, rows)
        z0[rows, :] = zz
        aa = normalise(zz)[0] * g0 + b0
        af[rows, :] = aa
        a[rows, :] = aa.astype(BF)

    ready(base, s, gains, shifts)
    tiles(z0.shape[0], 32, first)
    send(z0, a)
    image_hidden(a, w, u, g)
    send(u, g)
    image_down(af, g, w, z1)
    send(z1)

    def second(rows):
        yy = normalise(z1[rows, :])[0] * g1 + b1
        y[rows, :] = yy
        yb[rows, :] = yy.astype(BF)

    tiles(z0.shape[0], 32, second)


def image_mid_back(position, *refs):
    rank, s, base, z1, z0, u, w, gains, d1b, du, d0, d0b, stat, d1, da = split(
        refs, 0, 4, 0, 0, 0, 0, 0, 0, 0, 0, 0, 0, 0, 0, 0
    )
    g0 = gains[position : position + 1, :]
    g1 = gains[position + 1 : position + 2, :]
    stat[...] = jnp.zeros_like(stat)

    def first(rows):
        d, dg, ds = norm_back(z1[rows, :], g1, base[rows, :] + total(s, rows))
        d1[rows, :] = d
        d1b[rows, :] = d.astype(BF)
        stat[2:3, :] += dg
        stat[3:4, :] += ds

    ready(z1, base, s)
    tiles(z0.shape[0], 32, first)
    image_hidden_back(d1b, w, u, du)
    image_up_back(d1, du, w, da)
    ready(z0)

    def second(rows):
        d, dg, ds = norm_back(z0[rows, :], g0, da[rows, :])
        d0[rows, :] = d
        d0b[rows, :] = d.astype(BF)
        stat[0:1, :] += dg
        stat[1:2, :] += ds

    tiles(z0.shape[0], 32, second)


def image_turn(position, *refs):
    (rank, s, base, cot, w, gains, shifts, out, a, g, d1b, du, d0, d0b, stat,
     z0, af, u, z1, y, dy, d1, da) = split(
        refs, 0, 4, 0, 4, 0, 0, 0, 4, 0, 0, 0, 0, 0, 0, 0, 0, 0, 0, 0, 0, 0, 0, 0
    )
    r = rank[0]
    g0, b0 = gains[position : position + 1, :], shifts[position : position + 1, :]
    g1, b1 = gains[position + 1 : position + 2, :], shifts[position + 1 : position + 2, :]
    width = dy.shape[1] // Z
    stat[...] = jnp.zeros_like(stat)
    for k, ref in enumerate(cot):
        dy[:, part((r - k) & 3, width)] = ref[0 : dy.shape[0], :].astype(F32)

    def first(rows):
        zz = base[rows, :] + total(s, rows)
        z0[rows, :] = zz
        aa = normalise(zz)[0] * g0 + b0
        af[rows, :] = aa
        a[rows, :] = aa.astype(BF)

    ready(base, s, gains, shifts)
    tiles(z0.shape[0], 32, first)
    image_hidden(a, w, u, g)
    image_down(af, g, w, z1)

    def second(rows):
        zz = z1[rows, :]
        y[rows, :] = normalise(zz)[0] * g1 + b1
        d, dg, ds = norm_back(zz, g1, dy[rows, :])
        d1[rows, :] = d
        d1b[rows, :] = d.astype(BF)
        stat[2:3, :] += dg
        stat[3:4, :] += ds

    tiles(z0.shape[0], 32, second)
    for k in range(Z):
        out[k][...] = y[:, part((r + k) & 3, width)].astype(BF)
    image_hidden_back(d1b, w, u, du)
    image_up_back(d1, du, w, da)

    def third(rows):
        d, dg, ds = norm_back(z0[rows, :], g0, da[rows, :])
        d0[rows, :] = d
        d0b[rows, :] = d.astype(BF)
        stat[0:1, :] += dg
        stat[1:2, :] += ds

    tiles(z0.shape[0], 32, third)


def ffn_pieces(core, keep, give, a, du, g, dz):
    width = a.shape[1] // Z
    half = a.shape[1] // 2
    for out, which in ((keep, core), (give, 1 - core)):
        cols = part(which, half)
        left_up, right_down = a[:, cols], dz[:, cols]
        for c in range(Z):
            block = slice(c * width, (c + 1) * width)
            row = c * 2 * half
            out[row : row + half, :] = dot_tn(left_up, du[:, block]).astype(BF)
            down = dot_tn(g[:, block], right_down).astype(BF)
            for j in range(half // width):
                at = row + half + j * width
                out[at : at + width, :] = down[:, j * width : (j + 1) * width]


def matrix_whole(out, left, right):
    step = 256 if left.shape[1] % 256 == 0 else left.shape[1]
    for j in range(left.shape[1] // step):
        rows = slice(j * step, (j + 1) * step)
        out[rows, :] = dot_tn(left[:, rows], right[...]).astype(BF)
    if isinstance(out, Leaving):
        send(out)


def grads_image_ffn(*refs):
    pos, a, du, g, dz, keep, give = refs
    ffn_pieces(pos[3], keep, give, a, du, g, dz)


def grads_end(*refs):
    pos, x, du, g, dz, xv, duv, gv, dzv, out = refs
    count, size, wide = out.shape[0], out.shape[2], out.shape[3]
    deep, tall = x.shape[1], xv.shape[1]
    blocks = deep // wide
    ready(x, du, g, dz, xv, duv, gv, dzv)

    def write(c, row, value):
        value = value.astype(BF)
        for d in range(row // size, (row + value.shape[0] - 1) // size + 1):
            lo, hi = max(row, d * size), min(row + value.shape[0], (d + 1) * size)
            out[d, c, lo - d * size : hi - d * size, :] = value[lo - row : hi - row]

    for c in range(Z):
        for j in range(blocks):
            cols = slice((c * blocks + j) * wide, (c * blocks + j + 1) * wide)
            write(c, j * deep, dot_tn(x[...], du[:, cols]))
            own, cols = slice(c * deep, (c + 1) * deep), slice(j * wide, (j + 1) * wide)
            write(c, (blocks + j) * deep, dot_tn(g[:, own], dz[:, cols]))
        row = 2 * blocks * deep
        cols = slice(c * wide, (c + 1) * wide)
        for n in range(tall // wide):
            rows = slice(n * wide, (n + 1) * wide)
            write(c, row + n * wide, dot_tn(xv[:, rows], duv[:, cols]))
            write(c, row + tall + n * wide, dot_tn(gv[:, cols], dzv[:, rows]))


def cut_static(*refs):
    pos, whole, out = split(refs, 0, 0, 4)
    for k in range(Z):
        out[k][...] = whole[-k % Z]


def place_rows(*refs):
    pos, s, out = split(refs, 0, 4, 0)
    out[...] = jnp.zeros(out.shape, BF)
    out[part(pos[4], s[0].shape[0]), :] = total(s, slice(None)).astype(BF)


def grads_text_ffn(*refs):
    pos, x, du, g, dz, up, down = refs
    matrix_whole(up, x, du)
    matrix_whole(down, g, dz)


def grads_attention(*refs):
    pos, xt, dqt, xv, dqv, ot, dzt, ov, dzv, tq, vq, to, vo = refs
    for i in range(3):
        matrix_whole(tq.at[i], xt, dqt.at[i])
        matrix_whole(vq.at[i], xv, dqv.at[i])
    matrix_whole(to, ot, dzt)
    matrix_whole(vo, ov, dzv)


def core_sum(*refs):
    pos, keep, recv, out = split(refs, 0, 0, 0, 4)
    size = out[0].shape[0]
    for k in range(Z):
        rows = slice(-k % Z * size, (-k % Z + 1) * size)
        out[k][...] = (keep[rows, :].astype(F32) + recv[rows, :].astype(F32)).astype(BF)


def tensor_sum_stats(*refs):
    pos, s, both, out = split(refs, 0, 4, 4, 0)
    size, rows = s[0].shape[0], 16
    out[pos[3], 0:size, :] = total(s, slice(None)).astype(BF)
    out[1 - pos[3], 0:size, :] = jnp.zeros(s[0].shape, BF)
    stats = total(both, slice(both[0].shape[0] - rows, both[0].shape[0])).astype(BF)
    wide = out.shape[2]
    for j in range(Z):
        at = size + (j % 2) * rows
        out[j // 2, at : at + rows, :] = stats[:, j * wide : (j + 1) * wide]


def finish(*refs):
    count = 10
    stq, ins, both, end = refs[1], refs[2 : 1 + count], refs[1 + count], refs[2 + count]
    stqo, outs = refs[3 + count], refs[4 + count : 3 + 2 * count]
    up, down, tg, ts, vg, vs = refs[3 + 2 * count : 9 + 2 * count]
    end_refs = refs[9 + 2 * count :]
    for source, out in zip(ins, outs):
        out[...] = source[...].astype(F32)
        send(out)
    for j in range(3):
        stqo[j] = stq[j].astype(F32).T
    send(stqo)
    half, wide = up.shape[0] // 2, up.shape[1]
    for h in range(2):
        up[h * half : (h + 1) * half, :] = both[h, 0:half, :].astype(F32)
        for j in range(half // wide):
            at, to = half + j * wide, h * half + j * wide
            down[:, to : to + wide] = both[h, at : at + wide, :].astype(F32)
    send(up, down)
    blocks = [both[j // 2, 2 * half + j % 2 * 16 : 2 * half + j % 2 * 16 + 16, :] for j in range(Z)]
    stats = jnp.concatenate(blocks, axis=1).astype(F32)
    for i in range(4):
        tg[i : i + 1, :] = stats[2 * i : 2 * i + 1, 0 : tg.shape[1]]
        ts[i : i + 1, :] = stats[2 * i + 1 : 2 * i + 2, 0 : tg.shape[1]]
        vg[i : i + 1, :] = stats[8 + 2 * i : 9 + 2 * i, :]
        vs[i : i + 1, :] = stats[9 + 2 * i : 10 + 2 * i, :]
    up, down, image_up, image_down = end_refs
    deep, tall = up.shape[0], image_up.shape[0]
    blocks = deep // wide
    for j in range(blocks):
        cols = slice(j * wide, (j + 1) * wide)
        up[:, cols] = end[j * deep : (j + 1) * deep, :].astype(F32)
        down[:, cols] = end[(blocks + j) * deep : (blocks + j + 1) * deep, :].astype(F32)
    send(up, down)
    at = 2 * blocks * deep
    image_up[...] = end[at : at + tall, :].astype(F32)
    for j in range(tall // wide):
        row = at + tall + j * wide
        image_down[:, j * wide : (j + 1) * wide] = end[row : row + wide, :].astype(F32)


def placed(array):
    if any(array is one for one in arrived):
        return array
    return pltpu.with_memory_space_constraint(array, pltpu.HBM)


def run(name, body, outs, args, scratch=(), after=()):
    flat = []
    for arg in args:
        flat.extend(arg if isinstance(arg, (list, tuple)) else [arg])
    shapes, groups = [], []
    for shape, dtype, count in outs:
        groups.append(count)
        shapes.extend([pltpu.HBM(shape, dtype)] * max(count, 1))
    scratch = [jax.ShapeDtypeStruct(shape, dtype) for shape, dtype in scratch]
    held = sum(
        math.prod(x.shape) * jnp.dtype(x.dtype).itemsize for x in flat + shapes + scratch
    )
    n_in, n_out = len(flat) - 1, len(shapes)
    first = 1 + n_in + len(after)
    stage = first + n_out
    indices = [x.index if isinstance(x, View) else None for x in flat[1:]]

    def staged_body(*refs):
        sems = refs[-1]
        moves = [
            pltpu.make_async_copy(ref if index is None else ref.at[index], place, sems.at[i])
            for i, (ref, index, place) in enumerate(zip(refs[1 : 1 + n_in], indices, refs[stage:]))
        ]
        for move in moves:
            move.start()
        operands = [Arriving(ref, move) for ref, move in zip(refs[stage:], moves)]
        results = [
            Leaving(ref, target, sems.at[n_in + i])
            for i, (ref, target) in enumerate(zip(refs[stage + n_in :], refs[first:stage]))
        ]
        body(refs[0], *operands, *results, *refs[stage + n_in + n_out : -1])
        for operand in operands:
            operand.wait()
        for result in results:
            result.send()
        for result in results:
            result.copy.wait()

    hbm, free = pl.BlockSpec(memory_space=pltpu.HBM), pl.BlockSpec(memory_space=pl.ANY)
    arrays = [x.array if isinstance(x, View) else x for x in flat[1:]]
    results = pl.pallas_call(
        staged_body,
        out_shape=shapes,
        in_specs=[pl.BlockSpec(memory_space=pltpu.SMEM)] + [free] * (first - 1),
        out_specs=[hbm] * n_out,
        scratch_shapes=[pltpu.VMEM(x.shape, x.dtype) for x in flat[1:] + shapes + scratch]
        + [pltpu.SemaphoreType.DMA((n_in + n_out,))],
        compiler_params=pltpu.CompilerParams(
            vmem_limit_bytes=min(60 << 20, max(16 << 20, held + (8 << 20)))
        ),
        cost_estimate=SHORT,
        name=name,
    )(
        flat[0], *[placed(x) for x in arrays + list(after)])
    return split(list(results), *groups)


def cut_weights(pos, groups, n_dp, wide, after):
    flat = [matrix for group in groups for matrix in group]
    sizes = [sum(math.prod(m.shape) for m in group) // wide // n_dp for group in groups]
    step = 16

    def body(pos_ref, *refs):
        out, sem = refs[-2:]
        sources, base = list(refs[: len(flat)]), 0
        for group, size in zip(groups, sizes):
            steps, offset = size // step, 0
            begin = pos_ref[4] * steps
            for matrix in group:
                source = sources.pop(0)
                rows, width = matrix.shape
                for j in range(width // wide):
                    first = jnp.clip(offset // step - begin, 0, steps)
                    last = jnp.clip((offset + rows) // step - begin, 0, steps)

                    def move(i, carry, source=source, offset=offset, j=j, base=base, begin=begin):
                        row = pl.multiple_of((begin + i) * step - offset, step)
                        to = pl.multiple_of(base + i * step, step)
                        pltpu.make_async_copy(
                            source.at[pl.ds(row, step), pl.ds(j * wide, wide)],
                            out.at[pl.ds(to, step), :],
                            sem,
                        ).start()
                        return carry

                    lax.fori_loop(first, last, move, 0)
                    offset += rows
            base += size
        pltpu.make_async_copy(out, out, sem).wait()

    hbm, free = pl.BlockSpec(memory_space=pltpu.HBM), pl.BlockSpec(memory_space=pl.ANY)
    return pl.pallas_call(
        body,
        out_shape=pltpu.HBM((sum(sizes), wide), BF),
        in_specs=[pl.BlockSpec(memory_space=pltpu.SMEM)] + [free] * (len(flat) + len(after)),
        out_specs=hbm,
        scratch_shapes=[pltpu.SemaphoreType.DMA(())],
        cost_estimate=SHORT,
        name="cut_weights",
    )(pos, *[placed(x) for x in flat + list(after)])


arrived = []


def shift(values, k):
    arrived.append(lax.ppermute(values, "tensor", [(i, (i + k) % Z) for i in range(Z)]))
    return arrived[-1]


def spread(own):
    return [own] + [shift(own, k) for k in (1, 2, 3)]


def swap(chunks):
    return [chunks[0]] + [shift(chunks[k], k) for k in (1, 2, 3)]


def along(values, dy, dx, dc):
    pairs = []
    for y in range(4):
        for x in range(4):
            for c in range(2):
                to = (((y + dy) % 4) * 4 + (x + dx) % 4) * 2 + (c + dc) % 2
                pairs.append(((y * 4 + x) * 2 + c, to))
    arrived.append(lax.ppermute(values, "dp", pairs))
    return arrived[-1]


def pad_rows(values, n):
    micro, samples, rows, width = values.shape
    flat = values.reshape(micro, samples * rows, width)
    flat = jnp.pad(flat, ((0, 0), (0, n - samples * rows), (0, 0)))
    return flat.reshape(micro * n, width)


def unpad_rows(values, shape, n):
    micro, samples, rows, width = shape
    return values.reshape(micro, n, width)[:, : samples * rows].reshape(shape)


def joined(text, image, chunks):
    wide, width = image.shape[1], text.shape[1]
    t = text.reshape(chunks, text.shape[0] // chunks, width)
    main = packed_rows(t.shape[1], width, wide)
    rest = t[:, main:].reshape(chunks, t.shape[1] - main, width // (wide - width), wide - width)
    rest = rest.transpose(0, 2, 1, 3).reshape(chunks, main, wide - width)
    t = jnp.concatenate([t[:, :main], rest], axis=2)
    v = image.reshape(chunks, image.shape[0] // chunks, wide)
    return jnp.concatenate([v, t], axis=1)


def parted(both, text_rows, width):
    wide = both.shape[2]
    main = packed_rows(text_rows, width, wide)
    image, t = both[:, : both.shape[1] - main], both[:, both.shape[1] - main :]
    parts = width // (wide - width)
    rest = t[:, :, width:].reshape(t.shape[0], parts, main // parts, wide - width)
    rest = rest.transpose(0, 2, 1, 3).reshape(t.shape[0], main // parts, width)
    text = jnp.concatenate([t[:, :, :width], rest], axis=1)
    return text.reshape(-1, width), image.reshape(-1, wide)


def in_order(chunks, rank):
    ring = jnp.stack([chunks[0], chunks[3], chunks[2], chunks[1]] * 2)
    return lax.dynamic_slice_in_dim(ring, (Z - rank) & 3, Z, 0)


def shards(
    text_in, image_in, caption_len, region_count, text_cot, image_cot,
    co_text_qkv, co_image_qkv, co_text_out, co_image_out,
    co_text_up, co_text_down, co_image_up, co_image_down,
    self_text_qkv, self_image_qkv, self_text_out, self_image_out,
    text_up, text_down, image_up, image_down,
    text_gains, text_shifts, image_gains, image_shifts,
):
    arrived.clear()
    rank = lax.axis_index("tensor")
    place = lax.axis_index("dp")
    n_dp = lax.axis_size("dp")
    pos = jnp.stack([rank, (place // 2) % 4, place // 8, place % 2, place]).astype(jnp.int32)
    pos = jnp.concatenate([pos, caption_len.reshape(-1), region_count.reshape(-1)])
    micro, samples, text, wt = text_in.shape
    regions, wv = image_in.shape[2:]
    dt, dv = wt * Z, wv * Z
    nt = -(-samples * text // 64) * 64
    nv = -(-samples * regions // 64) * 64
    rt, rv = micro * nt, micro * nv
    ct, cv = rt // Z, rv // Z
    co_w = co_text_qkv.shape[2]
    st_w = self_text_qkv.shape[2]
    si_w = self_image_qkv.shape[2]
    ft = co_text_up.shape[1]
    chunk = ((cv + packed_rows(ct, dt, dv), dv), BF)
    shard = ((cv + packed_rows(ct, wt, wv), wv), BF)
    whole = ((rv + packed_rows(rt, wt, wv), wv), BF)

    both = spread(joined(pad_rows(text_in, nt), pad_rows(image_in, nv), 1)[0])
    groups = [(co_image_up, co_image_down), (text_up, text_down, image_up, image_down)]
    cuts = cut_weights(pos, groups, n_dp, wv, [])
    n_cut = 2 * dv // n_dp
    pieces = spread(cuts)
    w_mid = lax.all_gather(
        jnp.stack([piece[:n_cut] for piece in pieces]), "dp", axis=1, tiled=True
    )
    w_end = lax.all_gather(
        jnp.stack([piece[n_cut:] for piece in pieces]), "dp", axis=1, tiled=True
    )
    n_text = 2 * dt * (ft // wv)
    w_text = View(w_end, (slice(None), pl.ds(0, n_text)), (Z, n_text, wv))
    w_image = View(w_end, (slice(None), pl.ds(n_text, 2 * dv)), (Z, 2 * dv, wv))

    co_dims = (samples, text, regions, nt, nv)
    text_dims = (samples, text, nt, TEXT_HEAD, LENGTHS)
    image_dims = (samples, regions, nv, IMAGE_HEAD, LENGTHS + micro * samples)

    xt0, xv0, bt, bv, qt0, qv0, ot0, ov0, s = run(
        "co_fwd", functools.partial(co_fwd, co_dims),
        [((rt, dt), BF, 0), ((rv, dv), BF, 0), ((ct, dt), BF, 0), ((cv, dv), BF, 0),
         ((3, rt, co_w), BF, 0), ((3, rv, co_w), BF, 0), ((rt, co_w), BF, 0),
         ((rv, co_w), BF, 0), (*chunk, Z)],
        [pos, both, co_text_qkv, co_image_qkv, co_text_out, co_image_out],
    )
    s = swap(s)
    norm_t = [((ct, dt), F32, 0), ((ct, dt), F32, 0)]
    zt0, at, atb = run(
        "text_norm0", functools.partial(text_norm, 0, False), norm_t + [((ct, dt), BF, 0)],
        [pos, s, bt, text_gains, text_shifts],
    )
    cot = joined(pad_rows(text_cot, nt), pad_rows(image_cot, nv), Z)
    (cot,) = run("cut", cut, [(*shard, Z)], [pos, cot], after=[atb])
    cot = swap(cot)
    ffn_t = [((rt, dt), BF, 0), ((rt, ft), F32, 0), ((rt, ft), BF, 0), ((ct, dt), BF, Z)]
    xt1, ut1, gt1, st = run(
        "text_ffn1", text_ffn, ffn_t, [pos, spread(atb), co_text_up, co_text_down]
    )
    zv0, av, uv1, gv1, zv1, bv, bvb = run(
        "image_mid", functools.partial(image_mid, 0),
        [((cv, dv), F32, 0), ((cv, dv), BF, 0), ((cv, dv), F32, 0), ((cv, dv), BF, 0),
         ((cv, dv), F32, 0), ((cv, dv), F32, 0), ((cv, dv), BF, 0)],
        [pos, s, bv, w_mid, image_gains, image_shifts],
        [((cv, dv), F32)],
        after=[st[0]],
    )
    zt1, bt, both = run(
        "text_norm1", functools.partial(text_norm, 1, True), norm_t + [(*chunk, 0)],
        [pos, swap(st), at, text_gains, text_shifts, bvb],
        after=cot[1:],
    )
    both = spread(both)
    xt2, xv2, qt2, qv2, ot2, ov2, s = run(
        "self_fwd", functools.partial(self_fwd, text_dims, image_dims),
        [((rt, dt), BF, 0), ((rv, dv), BF, 0), ((3, rt, st_w), BF, 0),
         ((3, rv, si_w), BF, 0), ((rt, st_w), BF, 0), ((rv, si_w), BF, 0), (*chunk, Z)],
        [pos, both, self_text_qkv, self_image_qkv, self_text_out, self_image_out],
    )
    s = swap(s)
    out_v, av3, gv3, dv3, duv3, gv, gvb, stat_v1 = run(
        "image_turn", functools.partial(image_turn, 2),
        [((cv, wv), BF, Z), ((cv, dv), BF, 0), ((cv, dv), BF, 0), ((cv, dv), BF, 0),
         ((cv, dv), BF, 0), ((cv, dv), F32, 0), ((cv, dv), BF, 0), ((4, dv), F32, 0)],
        [pos, s, bv, cot, w_image, image_gains, image_shifts],
        [((cv, dv), F32)] * 8,
    )
    hidden = Z * ft
    outs, at3, gt3, dt3, dut3, gt, both, stat_t1 = run(
        "text_turn", functools.partial(text_turn, 2),
        [(*shard, Z), ((ct, dt), BF, 0), ((ct, hidden), BF, 0), ((ct, dt), BF, 0),
         ((ct, hidden), BF, 0), ((ct, dt), F32, 0), (*chunk, 0), ((4, dt), F32, 0)],
        [pos, s, bt, cot, out_v, gvb, w_text, text_gains, text_shifts],
        [((ct, hidden), F32), ((ct, dt), F32), ((ct, dt), F32)],
    )

    back_ffn = [((rt, dt), BF, 0), ((rt, ft), BF, 0), ((ct, dt), BF, Z)]
    stat_shape = ((2, dt), F32, 0)

    def image_ffn_grads(name, *saved, after):
        keep, give = run(
            "grads_" + name, grads_image_ffn, [((Z * dv, wv), BF, 0)] * 2, [pos, *saved],
            after=after,
        )
        return keep, along(give, 0, 0, 1)

    def core_summed(name, halves, after):
        (chunks,) = run(
            "core_sum_" + name, core_sum, [((dv, wv), BF, Z)], [pos, *halves], after=after
        )
        return chunks

    both = spread(both)
    (end,) = run(
        "grads_end", grads_end, [((n_dp, Z, (n_text + 2 * dv) // n_dp, wv), BF, 0)],
        [pos, at3, dut3, gt3, dt3, av3, duv3, gv3, dv3],
    )
    end_cut = lax.psum_scatter(end, "dp", scatter_dimension=0, tiled=False)
    dt2, dv2, dqt2, dqv2, s = run(
        "self_back", functools.partial(self_bwd, text_dims, image_dims),
        [((rt, dt), BF, 0), ((rv, dv), BF, 0), ((3, rt, st_w), BF, 0), ((3, rv, si_w), BF, 0),
         (*chunk, Z)],
        [pos, both, qt2, qv2, self_text_qkv, self_image_qkv,
         self_text_out, self_image_out],
        [((rt, st_w), BF), ((rv, si_w), BF)],
        after=[end],
    )
    s = swap(s)
    st_q, sv_q, st_o, sv_o = run(
        "grads_self", grads_attention,
        [((3, dt, st_w), BF, 0), ((3, dv, si_w), BF, 0), ((st_w, dt), BF, 0), ((si_w, dv), BF, 0)],
        [pos, xt2, dqt2, xv2, dqv2, ot2, dt2, ov2, dv2],
    )
    gt, gtb, stat_t2 = run(
        "text_norm1_back", functools.partial(text_norm_back, 1, False),
        [((ct, dt), F32, 0), ((ct, dt), BF, 0), stat_shape],
        [pos, s, gt, zt1, text_gains],
        after=[st_o],
    )
    g = spread(gtb)
    dv1, duv1, gv, gvb, stat_v0 = run(
        "image_mid_back", functools.partial(image_mid_back, 0),
        [((cv, dv), BF, 0), ((cv, dv), BF, 0), ((cv, dv), F32, 0), ((cv, dv), BF, 0),
         ((4, dv), F32, 0)],
        [pos, s, gv, zv1, zv0, uv1, w_mid, image_gains],
        [((cv, dv), F32)] * 2,
        after=[stat_t2],
    )
    dt1, dut1, st = run(
        "text_ffn1_back", text_ffn_back, back_ffn,
        [pos, g, co_text_up, co_text_down, ut1],
        after=[stat_v0],
    )
    st = swap(st)
    mid_f = image_ffn_grads("mid", av, duv1, gv1, dv1, after=[dt1])
    gt, both = run(
        "text_norm0_back", functools.partial(text_norm_back_stats, 0),
        [((ct, dt), F32, 0), ((chunk[0][0] + 16, dv), BF, 0)],
        [pos, st, gt, zt0, text_gains, gvb, stat_t2, stat_t1, stat_v0, stat_v1],
        after=[mid_f[0]],
    )
    both = spread(both)
    (end_cut,) = run(
        "cut_end", cut_static, [(end_cut.shape[1:], BF, Z)], [pos, end_cut], after=[gt]
    )
    end_cut = swap(end_cut)
    t1_up, t1_down = run(
        "grads_ffn1", grads_text_ffn, [((dt, ft), BF, 0), ((ft, dt), BF, 0)],
        [pos, xt1, dut1, gt1, dt1], after=[gt],
    )
    mid_f = core_summed("mid", mid_f, [t1_up, end_cut[0]])
    dqt0, dqv0, tq, vq, to, vo = run(
        "co_back", functools.partial(co_bwd, co_dims),
        [((3, rt, co_w), BF, 0), ((3, rv, co_w), BF, 0),
         ((3, dt, co_w), BF, 0), ((3, dv, co_w), BF, 0), ((co_w, dt), BF, 0), ((co_w, dv), BF, 0)],
        [pos, both, qt0, qv0, co_text_out, co_image_out, xt0, xv0, ot0, ov0],
        [((rt, dt), BF), ((rv, dv), BF), ((rt, co_w), BF), ((rv, co_w), BF)],
        after=[mid_f[0]],
    )
    (end,) = run(
        "place_end", place_rows, [((n_text + 2 * dv, wv), BF, 0)], [pos, end_cut], after=[to]
    )
    (s,) = run(
        "co_back_in", co_bwd_in, [(*whole, Z)],
        [pos, dqt0, dqv0, co_text_qkv, co_image_qkv, gt, gv],
        [((rt, wt), F32), ((rv, wv), F32)],
        after=[end],
    )
    (mid_f,) = run(
        "tensor_sum_mid", tensor_sum_stats, [((2, dv + 32, wv), BF, 0)],
        [pos, swap(mid_f), both], after=[end, s[0]],
    )
    late = lax.psum((st_q, t1_up, t1_down, sv_q, st_o, sv_o, tq, vq, to, vo, mid_f, end), "dp")
    s = swap(s)
    outs = swap(outs)
    ffn_out = [((dt, ft), F32, 0), ((ft, dt), F32, 0)]
    image_out_shapes = [((dv, wv), F32, 0), ((wv, dv), F32, 0)]
    (st_q, t1_up, t1_down, sv_q, st_o, sv_o, tq, vq, to, vo, mid_up, mid_down, tg, ts, vg, vs,
     t_up, t_down, end_up, end_down) = run(
        "finish", finish,
        [((3, st_w, dt), F32, 0)] + ffn_out
        + [((3, dv, si_w), F32, 0), ((st_w, dt), F32, 0), ((si_w, dv), F32, 0),
           ((3, dt, co_w), F32, 0), ((3, dv, co_w), F32, 0),
           ((co_w, dt), F32, 0), ((co_w, dv), F32, 0)] + image_out_shapes
        + [((4, dt), F32, 0)] * 2 + [((4, dv), F32, 0)] * 2 + ffn_out + image_out_shapes,
        [pos, *late],
    )
    st_q = st_q.transpose(0, 2, 1)

    text_out, image_out = parted(in_order(outs, rank), ct, wt)
    text_grad, image_grad = parted(sum(member.astype(F32) for member in s)[None], rt, wt)
    return (
        unpad_rows(text_out, text_in.shape, nt).astype(F32),
        unpad_rows(image_out, image_in.shape, nv).astype(F32),
        unpad_rows(text_grad, text_in.shape, nt),
        unpad_rows(image_grad, image_in.shape, nv),
        tq, vq, to, vo, t1_up, t1_down, mid_up, mid_down,
        st_q, sv_q, st_o, sv_o, t_up, t_down, end_up, end_down,
        tg, ts, vg, vs,
    )


def solution(mesh):
    stream = P(None, "dp", None, "tensor")
    lengths = P(None, "dp")
    stacked = P(None, None, "tensor")
    rows = P("tensor", None)
    cols = P(None, "tensor")
    weights = (
        stacked, stacked, rows, rows, cols, rows, cols, rows,
        stacked, stacked, rows, rows, cols, rows, cols, rows,
        P(), P(), P(), P(),
    )
    in_specs = (stream, stream, lengths, lengths, stream, stream) + weights
    out_specs = (stream,) * 4 + weights
    return jax.shard_map(shards, mesh=mesh, in_specs=in_specs, out_specs=out_specs, check_vma=False)
```

```python
import functools
import math

import jax
import jax.numpy as jnp
from jax import lax
from jax.experimental import pallas as pl
from jax.experimental.pallas import tpu as pltpu
from jax.sharding import PartitionSpec as P

CO_HEAD = 128
TEXT_HEAD = 64
IMAGE_HEAD = 128
EPS = 1e-05
FILL = -1000000000.0
ROOT_HALF = 0.7071067811865476
INV_ROOT_TWO_PI = 0.3989422804014327
F32 = jnp.float32
BF = jnp.bfloat16
Z = 4
COST = pl.CostEstimate(flops=20_000_000_000, bytes_accessed=1000, transcendentals=0)
LENGTHS = 5


def dot(a, b):
    return lax.dot_general(a, b, (((1,), (0,)), ((), ())), preferred_element_type=F32)


def dot_nt(a, b):
    return lax.dot_general(a, b, (((1,), (1,)), ((), ())), preferred_element_type=F32)


def dot_tn(a, b):
    return lax.dot_general(a, b, (((0,), (0,)), ((), ())), preferred_element_type=F32)


def part(index, size):
    return pl.ds(pl.multiple_of(index * size, size), size)


def row_ids(count, step, samples):
    place = lax.broadcasted_iota(jnp.int32, (count, 1), 0)
    ids = jnp.zeros((count, 1), jnp.int32)
    for s in range(1, samples):
        ids = ids + (place >= s * step).astype(jnp.int32)
    return ids


def key_ids(pos, first, m, step, samples, count):
    place = lax.broadcasted_iota(jnp.int32, (1, count), 1)
    ids = jnp.full((1, count), -1, jnp.int32)
    for s in range(samples):
        live = pos[first + m * samples + s]
        ids = jnp.where((place >= s * step) & (place < s * step + live), s, ids)
    return ids


def probabilities(q, k, same, scale):
    s = jnp.where(same, dot_nt(q, k) * scale, FILL)
    e = jnp.exp(s - jnp.max(s, axis=-1, keepdims=True))
    return e / jnp.sum(e, axis=-1, keepdims=True)


def head_fwd(q, k, v, same, scale):
    return dot(probabilities(q, k, same, scale).astype(BF), v).astype(BF)


def head_bwd(q, k, v, same, scale, do):
    p = probabilities(q, k, same, scale)
    dv = dot_tn(p.astype(BF), do)
    dp = dot_nt(do, v)
    ds = (p * (dp - jnp.sum(dp * p, axis=-1, keepdims=True))).astype(BF)
    dq = dot(ds, k) * scale
    dk = dot_tn(ds, q) * scale
    return dq.astype(BF), dk.astype(BF), dv.astype(BF)


def gelu(u):
    return u * (1.0 + lax.erf(u * ROOT_HALF)) * 0.5


def gelu_slope(u):
    return (1.0 + lax.erf(u * ROOT_HALF)) * 0.5 + u * jnp.exp(u * u * -0.5) * INV_ROOT_TWO_PI


def normalise(z):
    centre = z - jnp.mean(z, axis=-1, keepdims=True)
    rstd = lax.rsqrt(jnp.mean(centre * centre, axis=-1, keepdims=True) + EPS)
    return centre * rstd, rstd


def norm_back(z, gain, dy):
    xhat, rstd = normalise(z)
    dxh = dy * gain
    dz = rstd * (
        dxh
        - jnp.mean(dxh, axis=-1, keepdims=True)
        - xhat * jnp.mean(dxh * xhat, axis=-1, keepdims=True)
    )
    return dz, jnp.sum(dy * xhat, axis=0, keepdims=True), jnp.sum(dy, axis=0, keepdims=True)


class Arriving:
    in_loop = False

    def __init__(self, ref, copy):
        self.ref, self.copy = ref, copy
        self.shape, self.dtype = ref.shape, ref.dtype

    def wait(self):
        if self.copy is not None:
            assert not Arriving.in_loop
            self.copy.wait()
            self.copy = None

    def __getitem__(self, index):
        self.wait()
        return self.ref[index]

    @property
    def at(self):
        self.wait()
        return self.ref.at


class Scalars:
    def __init__(self, places, *lengths):
        self.places, self.lengths = places, lengths

    def __getitem__(self, i):
        if i < LENGTHS:
            return self.places[i]
        micro, samples = self.lengths[0].shape
        which, at = divmod(i - LENGTHS, micro * samples)
        return self.lengths[which][at // samples, at % samples]


class View:
    def __init__(self, array, index, shape):
        self.array, self.index, self.shape, self.dtype = array, index, shape, array.dtype


class Leaving:
    def __init__(self, ref, target, sem):
        self.ref, self.target, self.sem, self.sent = ref, target, sem, False
        self.copy = pltpu.make_async_copy(ref, target, sem)
        self.shape, self.dtype, self.at = ref.shape, ref.dtype, ref.at

    def send(self):
        if not self.sent:
            self.copy.start()
            self.sent = True

    def __getitem__(self, index):
        return self.ref[index]

    def __setitem__(self, index, value):
        assert not self.sent
        self.ref[index] = value


def send(*refs):
    for ref in refs:
        for one in ref if isinstance(ref, list) else [ref]:
            one.send()


def ready(*refs):
    for ref in refs:
        for one in ref if isinstance(ref, list) else [ref]:
            one.wait()


def tiles(count, tile, body):
    def step(i, carry):
        body(part(i, tile))
        return carry

    Arriving.in_loop = True
    lax.fori_loop(0, count // tile, step, 0)
    Arriving.in_loop = False


def total(refs, rows):
    acc = refs[0][rows, :].astype(F32)
    for ref in refs[1:]:
        acc = acc + ref[rows, :].astype(F32)
    return acc


def lanes_in_order(values, r, width):
    near = [values[0], values[3], values[2], values[1]]
    joined = jnp.concatenate([value.astype(F32) for value in near], axis=1)
    return pltpu.roll(joined, r * width, 1)


def lanes_from_own(values, r, width):
    return pltpu.roll(values, ((Z - r) & 3) * width, 1)


def rows_in_order(full, refs, r):
    size = full.shape[0] // Z
    for k, ref in enumerate(refs):
        full[part((r - k) & 3, size), :] = ref[0:size, :]


def packed_rows(rows, width, wide):
    return rows * width // wide if width < wide else rows


def put_text(ref, at, value):
    rows, width = value.shape
    wide = ref.shape[1]
    main = packed_rows(rows, width, wide)
    rest = rows - main
    ref[at : at + main, 0:width] = value[0:main]
    for j in range(width // (wide - width)):
        cols = slice(j * (wide - width), (j + 1) * (wide - width))
        ref[at + j * rest : at + (j + 1) * rest, width:wide] = value[main:rows, cols]


def get_text(ref, at, rows, width):
    wide = ref.shape[1]
    if width == wide:
        return ref[at : at + rows, :]
    main = packed_rows(rows, width, wide)
    rest = rows - main
    tail = [
        ref[at + j * rest : at + (j + 1) * rest, width:wide]
        for j in range(width // (wide - width))
    ]
    return jnp.concatenate([ref[at : at + main, 0:width], jnp.concatenate(tail, axis=1)], axis=0)


def split(refs, *counts):
    found, at = [], 0
    for count in counts:
        found.append(refs[at] if count == 0 else list(refs[at : at + count]))
        at += max(count, 1)
    assert at == len(refs)
    return found


def co_fwd(dims, *refs):
    rank, both, wt, wv, pt, pv, xt, xv, bt, bv, qt, qv, ot, ov, st, sv = split(
        refs, 0, 4, 0, 0, 0, 0, 0, 0, 0, 0, 0, 0, 0, 0, 4, 4
    )
    samples, text, regions, nt, nv = dims
    r = rank[0]
    rows_t, rows_v = xt.shape[0], xv.shape[0]
    width_t, width_v = xt.shape[1] // Z, xv.shape[1] // Z
    ct, cv = bt.shape[0], bv.shape[0]
    tin = [get_text(ref, rows_v, rows_t, width_t) for ref in both]
    xt[...] = lanes_in_order(tin, r, width_t).astype(BF)
    for k, ref in enumerate(both):
        xv[:, part((r - k) & 3, width_v)] = ref[0:rows_v, :]
    bt[...] = xt[part(r, ct), :]
    bv[...] = xv[part(r, cv), :]
    send(xt, xv, bt, bv)
    for i in range(3):
        qt[i] = dot(xt[...], wt[i]).astype(BF)

    def project(rows):
        for i in range(3):
            qv[i, rows, :] = dot(xv[rows, :], wv[i]).astype(BF)

    ready(wv)
    tiles(xv.shape[0], cv, project)
    send(qt, qv)
    scale = CO_HEAD ** (-0.5)
    rid_t, rid_v = row_ids(nt, text, samples), row_ids(nv, regions, samples)
    for m in range(2):
        rt, rv = slice(m * nt, (m + 1) * nt), slice(m * nv, (m + 1) * nv)
        same_tv = rid_t == key_ids(rank, LENGTHS + 2 * samples, m, regions, samples, nv)
        same_vt = rid_v == key_ids(rank, LENGTHS, m, text, samples, nt)
        for h in range(qt.shape[2] // CO_HEAD):
            c = slice(h * CO_HEAD, (h + 1) * CO_HEAD)
            ot[rt, c] = head_fwd(qt[0, rt, c], qv[1, rv, c], qv[2, rv, c], same_tv, scale)
            ov[rv, c] = head_fwd(qv[0, rv, c], qt[1, rt, c], qt[2, rt, c], same_vt, scale)
    for k in range(Z):
        c = (r + k) & 3
        st[k][...] = dot(ot[part(c, ct), :], pt[...]).astype(BF)
        sv[k][...] = dot(ov[part(c, cv), :], pv[...]).astype(BF)
        send(st[k], sv[k])


def co_bwd(dims, *refs):
    (rank, dt, dv, qt, qv, pt, pv, xt, xv, ot, ov,
     dqt, dqv, tq, vq, to, vo, zt, zv, dot_s, dov_s) = split(
        refs, 0, 4, 4, *([0] * 18)
    )
    samples, text, regions, nt, nv = dims
    r = rank[0]
    cv = zv.shape[0] // Z
    rows_in_order(zt, dt, r)
    rows_in_order(zv, dv, r)
    dot_s[...] = dot_nt(zt[...], pt[...]).astype(BF)

    def back_out(rows):
        dov_s[rows, :] = dot_nt(zv[rows, :], pv[...]).astype(BF)

    ready(pv)
    tiles(zv.shape[0], cv, back_out)
    scale = CO_HEAD ** (-0.5)
    rid_t, rid_v = row_ids(nt, text, samples), row_ids(nv, regions, samples)
    for m in range(2):
        rt, rv = slice(m * nt, (m + 1) * nt), slice(m * nv, (m + 1) * nv)
        same_tv = rid_t == key_ids(rank, LENGTHS + 2 * samples, m, regions, samples, nv)
        same_vt = rid_v == key_ids(rank, LENGTHS, m, text, samples, nt)
        for h in range(qt.shape[2] // CO_HEAD):
            c = slice(h * CO_HEAD, (h + 1) * CO_HEAD)
            a, b, d = head_bwd(
                qt[0, rt, c], qv[1, rv, c], qv[2, rv, c], same_tv, scale, dot_s[rt, c]
            )
            dqt[0, rt, c], dqv[1, rv, c], dqv[2, rv, c] = a, b, d
            a, b, d = head_bwd(
                qv[0, rv, c], qt[1, rt, c], qt[2, rt, c], same_vt, scale, dov_s[rv, c]
            )
            dqv[0, rv, c], dqt[1, rt, c], dqt[2, rt, c] = a, b, d
    send(dqt, dqv)
    for i in range(3):
        matrix_whole(tq.at[i], xt, dqt.at[i])
        matrix_whole(vq.at[i], xv, dqv.at[i])
    send(tq, vq)
    matrix_whole(to, ot, zt)
    matrix_whole(vo, ov, zv)


def co_bwd_in(*refs):
    rank, dqt, dqv, wt, wv, gt, gv, s, acc_t, acc_v = split(
        refs, 0, 0, 0, 0, 0, 0, 0, 4, 0, 0
    )
    r = rank[0]
    rows_v = acc_v.shape[0]
    ct, cv = gt.shape[0], gv.shape[0]
    width_t, width_v = acc_t.shape[1], acc_v.shape[1]
    own_t = lanes_from_own(gt[...], r, width_t)
    for k in range(Z):
        c = (r + k) & 3
        acc_t[...] = sum(dot_nt(dqt[i], wt[i, part(c, width_t), :]) for i in range(3))
        acc_t[part(r, ct), :] += own_t[:, k * width_t : (k + 1) * width_t]
        put_text(s[k], rows_v, acc_t[...].astype(BF))

        ready(wv, dqv)

        def back_in(rows):
            acc_v[rows, :] = sum(
                dot_nt(dqv[i, rows, :], wv[i, part(c, width_v), :]) for i in range(3)
            )

        tiles(acc_v.shape[0], cv, back_in)
        acc_v[part(r, cv), :] += gv[:, part(c, width_v)]
        s[k][0:rows_v, :] = acc_v[...].astype(BF)
        send(s[k])


def self_fwd(dims, *refs):
    rank, xin, w, po, x, q, o, s = split(refs, 0, 4, 0, 0, 0, 0, 0, 4)
    samples, step, n, head, first = dims
    r = rank[0]
    size = xin[0].shape[0]
    rows_in_order(x, xin, r)
    send(x)

    def project(rows):
        for i in range(3):
            q[i, rows, :] = dot(x[rows, :], w[i]).astype(BF)

    ready(w)
    tiles(x.shape[0], size, project)
    send(q)
    rid = row_ids(n, step, samples)
    for m in range(2):
        rm = slice(m * n, (m + 1) * n)
        same = rid == key_ids(rank, first, m, step, samples, n)
        for h in range(q.shape[2] // head):
            c = slice(h * head, (h + 1) * head)
            o[rm, c] = head_fwd(q[0, rm, c], q[1, rm, c], q[2, rm, c], same, head ** (-0.5))
    send(o)
    for k in range(Z):
        s[k][...] = dot(o[part((r + k) & 3, size), :], po[...]).astype(BF)
        send(s[k])


def self_bwd(dims, *refs):
    rank, din, q, w, po, z, dq, s, do = split(refs, 0, 4, 0, 0, 0, 0, 0, 4, 0)
    samples, step, n, head, first = dims
    r = rank[0]
    size = din[0].shape[0]
    rows_in_order(z, din, r)
    send(z)

    def back_out(rows):
        do[rows, :] = dot_nt(z[rows, :], po[...]).astype(BF)

    ready(po)
    tiles(z.shape[0], size, back_out)
    rid = row_ids(n, step, samples)
    for m in range(2):
        rm = slice(m * n, (m + 1) * n)
        same = rid == key_ids(rank, first, m, step, samples, n)
        for h in range(q.shape[2] // head):
            c = slice(h * head, (h + 1) * head)
            a, b, d = head_bwd(
                q[0, rm, c], q[1, rm, c], q[2, rm, c], same, head ** (-0.5), do[rm, c]
            )
            dq[0, rm, c], dq[1, rm, c], dq[2, rm, c] = a, b, d
    send(dq)
    for k in range(Z):
        rows = part((r + k) & 3, size)
        s[k][...] = sum(dot_nt(dq[i, rows, :], w[i]) for i in range(3)).astype(BF)
        send(s[k])


def text_total(base, s):
    return base[...].astype(F32) + total(s, slice(None))


def stat_rows(out, at, *stats):
    every = jnp.concatenate([ref[...] for ref in stats], axis=0)
    pad = jnp.zeros((out.shape[0] - at - every.shape[0], out.shape[1]), F32)
    out[at : out.shape[0], :] = jnp.concatenate([every, pad], axis=0).astype(BF)


def cut(*refs):
    pos, whole, out = split(refs, 0, 0, 4)
    for k in range(Z):
        out[k][...] = whole[(pos[0] + k) & 3]


def text_norm(position, *refs):
    rank, s, base, gains, shifts, z, y, out = split(refs, 0, 4, 0, 0, 0, 0, 0, 0)
    zz = text_total(base, s)
    z[...] = zz
    yy = normalise(zz)[0] * gains[position : position + 1, :] + shifts[position : position + 1, :]
    y[...] = yy
    out[...] = yy.astype(BF)


def text_norm_back(position, *refs):
    rank, s, base, z, gains, dz, out, stat = split(refs, 0, 4, 0, 0, 0, 0, 0, 0)
    d, dg, ds = norm_back(z[...], gains[position : position + 1, :], text_total(base, s))
    dz[...] = d
    out[...] = d.astype(BF)
    stat[0:1, :] = dg
    stat[1:2, :] = ds


def text_norm_back_stats(position, *refs):
    rank, s, base, z, gains, stat_1, stat_2, dz, out, stat = split(
        refs, 0, 4, 0, 0, 0, 0, 0, 0, 0, 0
    )
    d, dg, ds = norm_back(z[...], gains[position : position + 1, :], text_total(base, s))
    dz[...] = d
    rows = d.shape[0]
    out[0:rows, :] = d.astype(BF)
    stat[0:1, :] = dg
    stat[1:2, :] = ds
    stat_rows(out, rows, stat, stat_1, stat_2)


def text_turn(position, *refs):
    (rank, s, base, cot, w, gains, shifts, out, a, g, d1b, du, dz, send_on, stat,
     u, x, d1) = split(refs, 0, 4, 0, 4, 0, 0, 0, 4, 0, 0, 0, 0, 0, 0, 0, 0, 0, 0)
    r = rank[0]
    g0, b0 = gains[position : position + 1, :], shifts[position : position + 1, :]
    g1, b1 = gains[position + 1 : position + 2, :], shifts[position + 1 : position + 2, :]
    rows, width = base.shape[0], base.shape[1] // Z
    at = cot[0].shape[0] - packed_rows(rows, width, cot[0].shape[1])
    wide, deep = w.shape[2], base.shape[1]
    blocks = deep // wide
    z0 = text_total(base, s)
    x[...] = normalise(z0)[0] * g0 + b0
    a[...] = x[...].astype(BF)
    send(a)
    down = blocks * deep
    for c in range(Z):
        for j in range(blocks):
            cols = slice((c * blocks + j) * wide, (c * blocks + j + 1) * wide)
            uu = dot(a[...], w[c, j * deep : (j + 1) * deep, :])
            u[:, cols] = uu
            g[:, cols] = gelu(uu).astype(BF)
    send(g)
    for j in range(blocks):
        cols = slice(j * wide, (j + 1) * wide)
        acc = x[:, cols]
        for c in range(Z):
            own = slice(c * deep, (c + 1) * deep)
            acc = acc + dot(g[:, own], w[c, down + j * deep : down + (j + 1) * deep, :])
        x[:, cols] = acc
    z1 = x[...]
    y = lanes_from_own(normalise(z1)[0] * g1 + b1, r, width)
    for k in range(Z):
        out[k][...] = y[:, k * width : (k + 1) * width].astype(BF)
        send(out[k])
    dy = lanes_in_order([get_text(ref, at, rows, width) for ref in cot], r, width)
    d, dg, ds = norm_back(z1, g1, dy)
    d1[...] = d
    d1b[...] = d.astype(BF)
    send(d1b)
    stat[2:3, :] = dg
    stat[3:4, :] = ds
    for c in range(Z):
        own = slice(c * deep, (c + 1) * deep)
        back = sum(
            dot_nt(
                d1b[:, j * wide : (j + 1) * wide],
                w[c, down + j * deep : down + (j + 1) * deep, :],
            )
            for j in range(blocks)
        )
        du[:, own] = (back * gelu_slope(u[:, own])).astype(BF)
    send(du)
    back = d1[...]
    for c in range(Z):
        for j in range(blocks):
            cols = slice((c * blocks + j) * wide, (c * blocks + j + 1) * wide)
            back = back + dot_nt(du[:, cols], w[c, j * deep : (j + 1) * deep, :])
    d, dg, ds = norm_back(z0, g0, back)
    dz[...] = d
    send_on[...] = d.astype(BF)
    stat[0:1, :] = dg
    stat[1:2, :] = ds


def text_ffn(*refs):
    rank, xin, up, down, x, u, g, s = split(refs, 0, 4, 0, 0, 0, 0, 0, 4)
    r = rank[0]
    size = xin[0].shape[0]
    rows_in_order(x, xin, r)

    def hidden(rows):
        uu = dot(x[rows, :], up[...])
        u[rows, :] = uu
        g[rows, :] = gelu(uu).astype(BF)

    ready(up)
    tiles(x.shape[0], size, hidden)
    send(x, u, g)
    for k in range(Z):
        s[k][...] = dot(g[part((r + k) & 3, size), :], down[...]).astype(BF)
        send(s[k])


def text_ffn_back(*refs):
    rank, din, up, down, u, z, du, s = split(refs, 0, 4, 0, 0, 0, 0, 0, 4)
    r = rank[0]
    size = din[0].shape[0]
    rows_in_order(z, din, r)

    def hidden(rows):
        du[rows, :] = (dot_nt(z[rows, :], down[...]) * gelu_slope(u[rows, :])).astype(BF)

    ready(down, u)
    tiles(z.shape[0], size, hidden)
    send(z, du)
    for k in range(Z):
        s[k][...] = dot_nt(du[part((r + k) & 3, size), :], up[...]).astype(BF)


def image_hidden(a, w, u, g):
    width = w.shape[2]
    depth = w.shape[1] // 2
    for c in range(Z):
        cols = slice(c * width, (c + 1) * width)
        uu = dot(a[...], w[c, 0:depth, :])
        u[:, cols] = uu
        g[:, cols] = gelu(uu).astype(BF)


def image_down(af, g, w, z):
    width = w.shape[2]
    depth = w.shape[1] // 2
    for n in range(Z):
        out = slice(n * width, (n + 1) * width)
        acc = af[:, out]
        rows = slice(depth + n * width, depth + (n + 1) * width)
        for c in range(Z):
            cols = slice(c * width, (c + 1) * width)
            acc = acc + dot(g[:, cols], w[c, rows, :])
        z[:, out] = acc


def image_hidden_back(dzb, w, u, du):
    width = w.shape[2]
    depth = w.shape[1] // 2
    for c in range(Z):
        cols = slice(c * width, (c + 1) * width)
        dg = sum(
            dot_nt(
                dzb[:, n * width : (n + 1) * width],
                w[c, depth + n * width : depth + (n + 1) * width, :],
            )
            for n in range(Z)
        )
        du[:, cols] = (dg * gelu_slope(u[:, cols])).astype(BF)


def image_up_back(dz, du, w, da):
    width = w.shape[2]
    width = w.shape[2]
    for n in range(Z):
        out = slice(n * width, (n + 1) * width)
        acc = dz[:, out]
        for c in range(Z):
            cols = slice(c * width, (c + 1) * width)
            acc = acc + dot_nt(du[:, cols], w[c, n * width : (n + 1) * width, :])
        da[:, out] = acc


def image_mid(position, *refs):
    rank, s, base, w, gains, shifts, z0, a, u, g, z1, y, yb, af = split(
        refs, 0, 4, 0, 0, 0, 0, 0, 0, 0, 0, 0, 0, 0, 0
    )
    g0, b0 = gains[position : position + 1, :], shifts[position : position + 1, :]
    g1, b1 = gains[position + 1 : position + 2, :], shifts[position + 1 : position + 2, :]

    def first(rows):
        zz = base[rows, :].astype(F32) + total(s, rows)
        z0[rows, :] = zz
        aa = normalise(zz)[0] * g0 + b0
        af[rows, :] = aa
        a[rows, :] = aa.astype(BF)

    ready(base, s, gains, shifts)
    tiles(z0.shape[0], 32, first)
    send(z0, a)
    image_hidden(a, w, u, g)
    send(u, g)
    image_down(af, g, w, z1)
    send(z1)

    def second(rows):
        yy = normalise(z1[rows, :])[0] * g1 + b1
        y[rows, :] = yy
        yb[rows, :] = yy.astype(BF)

    tiles(z0.shape[0], 32, second)


def image_mid_back(position, *refs):
    rank, s, base, z1, z0, u, w, gains, stat_1, d1b, du, d0, d0b, stat, d1, da = split(
        refs, 0, 4, 0, 0, 0, 0, 0, 0, 0, 0, 0, 0, 0, 0, 0, 0
    )
    g0 = gains[position : position + 1, :]
    g1 = gains[position + 1 : position + 2, :]
    stat[...] = jnp.zeros_like(stat)

    def first(rows):
        d, dg, ds = norm_back(z1[rows, :], g1, base[rows, :] + total(s, rows))
        d1[rows, :] = d
        d1b[rows, :] = d.astype(BF)
        stat[2:3, :] += dg
        stat[3:4, :] += ds

    ready(z1, base, s)
    tiles(z0.shape[0], 32, first)
    image_hidden_back(d1b, w, u, du)
    image_up_back(d1, du, w, da)
    ready(z0)

    def second(rows):
        d, dg, ds = norm_back(z0[rows, :], g0, da[rows, :])
        d0[rows, :] = d
        d0b[rows, :] = d.astype(BF)
        stat[0:1, :] += dg
        stat[1:2, :] += ds

    tiles(z0.shape[0], 32, second)
    stat_rows(d0b, z0.shape[0], stat, stat_1)


def image_turn(position, *refs):
    (rank, s, base, cot, w, gains, shifts, out, a, g, d1b, du, d0, d0b, stat,
     z0, af, u, z1, y, dy, d1, da) = split(
        refs, 0, 4, 0, 4, 0, 0, 0, 4, 0, 0, 0, 0, 0, 0, 0, 0, 0, 0, 0, 0, 0, 0, 0
    )
    r = rank[0]
    g0, b0 = gains[position : position + 1, :], shifts[position : position + 1, :]
    g1, b1 = gains[position + 1 : position + 2, :], shifts[position + 1 : position + 2, :]
    width = dy.shape[1] // Z
    stat[...] = jnp.zeros_like(stat)
    for k, ref in enumerate(cot):
        dy[:, part((r - k) & 3, width)] = ref[0 : dy.shape[0], :].astype(F32)

    def first(rows):
        zz = base[rows, :] + total(s, rows)
        z0[rows, :] = zz
        aa = normalise(zz)[0] * g0 + b0
        af[rows, :] = aa
        a[rows, :] = aa.astype(BF)

    ready(base, s, gains, shifts)
    tiles(z0.shape[0], 32, first)
    image_hidden(a, w, u, g)
    image_down(af, g, w, z1)

    def second(rows):
        zz = z1[rows, :]
        y[rows, :] = normalise(zz)[0] * g1 + b1
        d, dg, ds = norm_back(zz, g1, dy[rows, :])
        d1[rows, :] = d
        d1b[rows, :] = d.astype(BF)
        stat[2:3, :] += dg
        stat[3:4, :] += ds

    tiles(z0.shape[0], 32, second)
    for k in range(Z):
        out[k][...] = y[:, part((r + k) & 3, width)].astype(BF)
    image_hidden_back(d1b, w, u, du)
    image_up_back(d1, du, w, da)

    def third(rows):
        d, dg, ds = norm_back(z0[rows, :], g0, da[rows, :])
        d0[rows, :] = d
        d0b[rows, :] = d.astype(BF)
        stat[0:1, :] += dg
        stat[1:2, :] += ds

    tiles(z0.shape[0], 32, third)


def ffn_pieces(core, keep, give, a, du, g, dz):
    width = a.shape[1] // Z
    half = a.shape[1] // 2
    for out, which in ((keep, core), (give, 1 - core)):
        cols = part(which, half)
        left_up, right_down = a[:, cols], dz[:, cols]
        for c in range(Z):
            block = slice(c * width, (c + 1) * width)
            row = c * 2 * half
            out[row : row + half, :] = dot_tn(left_up, du[:, block]).astype(BF)
            down = dot_tn(g[:, block], right_down).astype(BF)
            for j in range(half // width):
                at = row + half + j * width
                out[at : at + width, :] = down[:, j * width : (j + 1) * width]


def matrix_whole(out, left, right):
    step = 256 if left.shape[1] % 256 == 0 else left.shape[1]
    for j in range(left.shape[1] // step):
        rows = slice(j * step, (j + 1) * step)
        out[rows, :] = dot_tn(left[:, rows], right[...]).astype(BF)
    if isinstance(out, Leaving):
        send(out)


def grads_image_ffn(*refs):
    pos, a, du, g, dz, keep, give = refs
    ffn_pieces(pos[3], keep, give, a, du, g, dz)


def grads_end(*refs):
    pos, x, du, g, dz, xv, duv, gv, dzv, out = refs
    count, size, wide = out.shape[0], out.shape[2], out.shape[3]
    deep, tall = x.shape[1], xv.shape[1]
    blocks = deep // wide
    ready(x, du, g, dz, xv, duv, gv, dzv)

    def write(c, row, value):
        value = value.astype(BF)
        for d in range(row // size, (row + value.shape[0] - 1) // size + 1):
            lo, hi = max(row, d * size), min(row + value.shape[0], (d + 1) * size)
            out[d, c, lo - d * size : hi - d * size, :] = value[lo - row : hi - row]

    for c in range(Z):
        for j in range(blocks):
            cols = slice((c * blocks + j) * wide, (c * blocks + j + 1) * wide)
            write(c, j * deep, dot_tn(x[...], du[:, cols]))
            own, cols = slice(c * deep, (c + 1) * deep), slice(j * wide, (j + 1) * wide)
            write(c, (blocks + j) * deep, dot_tn(g[:, own], dz[:, cols]))
        row = 2 * blocks * deep
        cols = slice(c * wide, (c + 1) * wide)
        for n in range(tall // wide):
            rows = slice(n * wide, (n + 1) * wide)
            write(c, row + n * wide, dot_tn(xv[:, rows], duv[:, cols]))
            write(c, row + tall + n * wide, dot_tn(gv[:, cols], dzv[:, rows]))


def cut_static(*refs):
    pos, whole, out = split(refs, 0, 0, 4)
    for k in range(Z):
        out[k][...] = whole[-k % Z]


def place_rows(*refs):
    pos, s, out = split(refs, 0, 4, 0)
    out[...] = jnp.zeros(out.shape, BF)
    out[part(pos[4], s[0].shape[0]), :] = total(s, slice(None)).astype(BF)


def grads_text_ffn(*refs):
    pos, x, du, g, dz, up, down = refs
    matrix_whole(up, x, du)
    matrix_whole(down, g, dz)


def grads_attention(*refs):
    pos, xt, dqt, xv, dqv, ot, dzt, ov, dzv, tq, vq, to, vo = refs
    for i in range(3):
        matrix_whole(tq.at[i], xt, dqt.at[i])
        matrix_whole(vq.at[i], xv, dqv.at[i])
    matrix_whole(to, ot, dzt)
    matrix_whole(vo, ov, dzv)


def core_sum(*refs):
    pos, keep, recv, out = split(refs, 0, 0, 0, 4)
    size = out[0].shape[0]
    for k in range(Z):
        rows = slice(-k % Z * size, (-k % Z + 1) * size)
        out[k][...] = (keep[rows, :].astype(F32) + recv[rows, :].astype(F32)).astype(BF)


def tensor_sum_stats(*refs):
    pos, s, text, image, out = split(refs, 0, 4, 4, 4, 0)
    size, rows = s[0].shape[0], 16
    out[pos[3], 0:size, :] = total(s, slice(None)).astype(BF)
    out[1 - pos[3], 0:size, :] = jnp.zeros(s[0].shape, BF)
    last = [slice(x[0].shape[0] - rows, x[0].shape[0] - rows // 2) for x in (text, image)]
    wide, tall = out.shape[2], image[0].shape[1]
    narrow = total(text, last[0])
    narrow = jnp.concatenate(
        [narrow, jnp.zeros((narrow.shape[0], tall - narrow.shape[1]), F32)], axis=1
    )
    stats = jnp.concatenate([narrow, total(image, last[1])], axis=0).astype(BF)
    for j in range(Z):
        at = size + (j % 2) * rows
        out[j // 2, at : at + rows, :] = stats[:, j * wide : (j + 1) * wide]


def finish(*refs):
    count = 10
    stq, ins, both, end = refs[1], refs[2 : 1 + count], refs[1 + count], refs[2 + count]
    stqo, outs = refs[3 + count], refs[4 + count : 3 + 2 * count]
    up, down, tg, ts, vg, vs = refs[3 + 2 * count : 9 + 2 * count]
    end_refs = refs[9 + 2 * count :]
    for source, out in zip(ins, outs):
        out[...] = source[...].astype(F32)
        send(out)
    for j in range(3):
        stqo[j] = stq[j].astype(F32).T
    send(stqo)
    half, wide = up.shape[0] // 2, up.shape[1]
    for h in range(2):
        up[h * half : (h + 1) * half, :] = both[h, 0:half, :].astype(F32)
        for j in range(half // wide):
            at, to = half + j * wide, h * half + j * wide
            down[:, to : to + wide] = both[h, at : at + wide, :].astype(F32)
    send(up, down)
    blocks = [both[j // 2, 2 * half + j % 2 * 16 : 2 * half + j % 2 * 16 + 16, :] for j in range(Z)]
    stats = jnp.concatenate(blocks, axis=1).astype(F32)
    for i in range(4):
        tg[i : i + 1, :] = stats[2 * i : 2 * i + 1, 0 : tg.shape[1]]
        ts[i : i + 1, :] = stats[2 * i + 1 : 2 * i + 2, 0 : tg.shape[1]]
        vg[i : i + 1, :] = stats[8 + 2 * i : 9 + 2 * i, :]
        vs[i : i + 1, :] = stats[9 + 2 * i : 10 + 2 * i, :]
    up, down, image_up, image_down = end_refs
    deep, tall = up.shape[0], image_up.shape[0]
    blocks = deep // wide
    for j in range(blocks):
        cols = slice(j * wide, (j + 1) * wide)
        up[:, cols] = end[j * deep : (j + 1) * deep, :].astype(F32)
        down[:, cols] = end[(blocks + j) * deep : (blocks + j + 1) * deep, :].astype(F32)
    send(up, down)
    at = 2 * blocks * deep
    image_up[...] = end[at : at + tall, :].astype(F32)
    for j in range(tall // wide):
        row = at + tall + j * wide
        image_down[:, j * wide : (j + 1) * wide] = end[row : row + wide, :].astype(F32)


def placed(array):
    if any(array is one for one in arrived):
        return array
    return pltpu.with_memory_space_constraint(array, pltpu.HBM)


latest = []


def follow(results):
    latest[:] = [min(results, key=lambda x: x.size)]


def run(name, body, outs, args, scratch=(), after=()):
    after = latest + list(after)
    flat = [None]
    for arg in args[1:]:
        flat.extend(arg if isinstance(arg, (list, tuple)) else [arg])
    shapes, groups = [], []
    for shape, dtype, count in outs:
        groups.append(count)
        shapes.extend([pltpu.HBM(shape, dtype)] * max(count, 1))
    scratch = [jax.ShapeDtypeStruct(shape, dtype) for shape, dtype in scratch]
    held = sum(
        math.prod(x.shape) * jnp.dtype(x.dtype).itemsize for x in flat[1:] + shapes + scratch
    )
    n_in, n_out = len(flat) - 1, len(shapes)
    first = 1 + n_in + len(after)
    stage = first + n_out
    indices = [x.index if isinstance(x, View) else None for x in flat[1:]]

    def staged_body(*refs):
        refs = (Scalars(*refs[:3]), *refs[3:])
        sems = refs[-1]
        moves = [
            pltpu.make_async_copy(ref if index is None else ref.at[index], place, sems.at[i])
            for i, (ref, index, place) in enumerate(zip(refs[1 : 1 + n_in], indices, refs[stage:]))
        ]
        for move in moves:
            move.start()
        operands = [Arriving(ref, move) for ref, move in zip(refs[stage:], moves)]
        results = [
            Leaving(ref, target, sems.at[n_in + i])
            for i, (ref, target) in enumerate(zip(refs[stage + n_in :], refs[first:stage]))
        ]
        body(refs[0], *operands, *results, *refs[stage + n_in + n_out : -1])
        for operand in operands:
            operand.wait()
        for result in results:
            result.send()
        for result in results:
            result.copy.wait()

    hbm, free = pl.BlockSpec(memory_space=pltpu.HBM), pl.BlockSpec(memory_space=pl.ANY)
    arrays = [x.array if isinstance(x, View) else x for x in flat[1:]]
    results = pl.pallas_call(
        staged_body,
        out_shape=shapes,
        in_specs=[pl.BlockSpec(memory_space=pltpu.SMEM)] * 3 + [free] * (first - 1),
        out_specs=[hbm] * n_out,
        scratch_shapes=[pltpu.VMEM(x.shape, x.dtype) for x in flat[1:] + shapes + scratch]
        + [pltpu.SemaphoreType.DMA((n_in + n_out,))],
        compiler_params=pltpu.CompilerParams(
            vmem_limit_bytes=min(60 << 20, max(16 << 20, held + (8 << 20)))
        ),
        cost_estimate=COST,
        name=name,
    )(
        *args[0], *[placed(x) for x in arrays + after])
    follow(results)
    return split(list(results), *groups)


def cut_weights(scalars, groups, n_dp, wide):
    flat = [matrix for group in groups for matrix in group]
    sizes = [sum(math.prod(m.shape) for m in group) // wide // n_dp for group in groups]
    step = 16

    def body(pos_ref, *refs):
        out, sem = refs[-2:]
        sources, base = list(refs[: len(flat)]), 0
        for group, size in zip(groups, sizes):
            steps, offset = size // step, 0
            begin = pos_ref[4] * steps
            for matrix in group:
                source = sources.pop(0)
                rows, width = matrix.shape
                for j in range(width // wide):
                    first = jnp.clip(offset // step - begin, 0, steps)
                    last = jnp.clip((offset + rows) // step - begin, 0, steps)

                    def move(i, carry, source=source, offset=offset, j=j, base=base, begin=begin):
                        row = pl.multiple_of((begin + i) * step - offset, step)
                        to = pl.multiple_of(base + i * step, step)
                        pltpu.make_async_copy(
                            source.at[pl.ds(row, step), pl.ds(j * wide, wide)],
                            out.at[pl.ds(to, step), :],
                            sem,
                        ).start()
                        return carry

                    lax.fori_loop(first, last, move, 0)
                    offset += rows
            base += size
        pltpu.make_async_copy(out, out, sem).wait()

    hbm, free = pl.BlockSpec(memory_space=pltpu.HBM), pl.BlockSpec(memory_space=pl.ANY)
    after = list(latest)
    result = pl.pallas_call(
        body,
        out_shape=pltpu.HBM((sum(sizes), wide), BF),
        in_specs=[pl.BlockSpec(memory_space=pltpu.SMEM)] + [free] * (len(flat) + len(after)),
        out_specs=hbm,
        scratch_shapes=[pltpu.SemaphoreType.DMA(())],
        cost_estimate=COST,
        name="cut_weights",
    )(scalars[0], *[placed(x) for x in flat + after])
    follow([result])
    return result


arrived = []


def shift(values, k):
    arrived.append(lax.ppermute(values, "tensor", [(i, (i + k) % Z) for i in range(Z)]))
    return arrived[-1]


def spread(own):
    return [own] + [shift(own, k) for k in (1, 2, 3)]


def swap(chunks):
    return [chunks[0]] + [shift(chunks[k], k) for k in (1, 2, 3)]


def along(values, dy, dx, dc):
    pairs = []
    for y in range(4):
        for x in range(4):
            for c in range(2):
                to = (((y + dy) % 4) * 4 + (x + dx) % 4) * 2 + (c + dc) % 2
                pairs.append(((y * 4 + x) * 2 + c, to))
    arrived.append(lax.ppermute(values, "dp", pairs))
    return arrived[-1]


def pad_rows(values, n):
    micro, samples, rows, width = values.shape
    flat = values.reshape(micro, samples * rows, width)
    flat = jnp.pad(flat, ((0, 0), (0, n - samples * rows), (0, 0)))
    return flat.reshape(micro * n, width)


def unpad_rows(values, shape, n):
    micro, samples, rows, width = shape
    return values.reshape(micro, n, width)[:, : samples * rows].reshape(shape)


def joined(text, image, chunks):
    wide, width = image.shape[1], text.shape[1]
    t = text.reshape(chunks, text.shape[0] // chunks, width)
    main = packed_rows(t.shape[1], width, wide)
    rest = t[:, main:].reshape(chunks, t.shape[1] - main, width // (wide - width), wide - width)
    rest = rest.transpose(0, 2, 1, 3).reshape(chunks, main, wide - width)
    t = jnp.concatenate([t[:, :main], rest], axis=2)
    v = image.reshape(chunks, image.shape[0] // chunks, wide)
    return jnp.concatenate([v, t], axis=1)


def parted(both, text_rows, width):
    wide = both.shape[2]
    main = packed_rows(text_rows, width, wide)
    image, t = both[:, : both.shape[1] - main], both[:, both.shape[1] - main :]
    parts = width // (wide - width)
    rest = t[:, :, width:].reshape(t.shape[0], parts, main // parts, wide - width)
    rest = rest.transpose(0, 2, 1, 3).reshape(t.shape[0], main // parts, width)
    text = jnp.concatenate([t[:, :, :width], rest], axis=1)
    return text.reshape(-1, width), image.reshape(-1, wide)


def in_order(chunks, rank):
    ring = jnp.stack([chunks[0], chunks[3], chunks[2], chunks[1]] * 2)
    return lax.dynamic_slice_in_dim(ring, (Z - rank) & 3, Z, 0)


def shards(
    text_in, image_in, caption_len, region_count, text_cot, image_cot,
    co_text_qkv, co_image_qkv, co_text_out, co_image_out,
    co_text_up, co_text_down, co_image_up, co_image_down,
    self_text_qkv, self_image_qkv, self_text_out, self_image_out,
    text_up, text_down, image_up, image_down,
    text_gains, text_shifts, image_gains, image_shifts,
):
    arrived.clear()
    latest.clear()
    rank = lax.axis_index("tensor")
    place = lax.axis_index("dp")
    n_dp = lax.axis_size("dp")
    pos = jnp.stack([rank, (place // 2) % 4, place // 8, place % 2, place]).astype(jnp.int32)
    scalars = [pos, caption_len, region_count]
    micro, samples, text, wt = text_in.shape
    regions, wv = image_in.shape[2:]
    dt, dv = wt * Z, wv * Z
    nt = -(-samples * text // 64) * 64
    nv = -(-samples * regions // 64) * 64
    rt, rv = micro * nt, micro * nv
    ct, cv = rt // Z, rv // Z
    co_w = co_text_qkv.shape[2]
    st_w = self_text_qkv.shape[2]
    si_w = self_image_qkv.shape[2]
    ft = co_text_up.shape[1]
    shard = ((cv + packed_rows(ct, wt, wv), wv), BF)
    whole = ((rv + packed_rows(rt, wt, wv), wv), BF)

    groups = [(co_image_up, co_image_down), (text_up, text_down, image_up, image_down)]
    cuts = cut_weights(scalars, groups, n_dp, wv)
    shards_in = joined(pad_rows(text_in, nt), pad_rows(image_in, nv), 1)[0]
    both = spread(jnp.concatenate([shards_in, cuts], axis=0))
    first, last = whole[0][0], whole[0][0] + 2 * dv // n_dp
    w_mid = lax.all_gather(
        jnp.stack([piece[first:last] for piece in both]), "dp", axis=1, tiled=True
    )
    w_end = lax.all_gather(
        jnp.stack([piece[last:] for piece in both]), "dp", axis=1, tiled=True
    )
    co_dims = (samples, text, regions, nt, nv)
    text_dims = (samples, text, nt, TEXT_HEAD, LENGTHS)
    image_dims = (samples, regions, nv, IMAGE_HEAD, LENGTHS + micro * samples)
    xt0, xv0, bt, bv, qt0, qv0, ot0, ov0, st, sv = run(
        "co_fwd", functools.partial(co_fwd, co_dims),
        [((rt, dt), BF, 0), ((rv, dv), BF, 0), ((ct, dt), BF, 0), ((cv, dv), BF, 0),
         ((3, rt, co_w), BF, 0), ((3, rv, co_w), BF, 0), ((rt, co_w), BF, 0),
         ((rv, co_w), BF, 0), ((ct, dt), BF, Z), ((cv, dv), BF, Z)],
        [scalars, both, co_text_qkv, co_image_qkv, co_text_out, co_image_out],
    )
    n_text = 2 * dt * (ft // wv)
    w_text = View(w_end, (slice(None), pl.ds(0, n_text)), (Z, n_text, wv))
    w_image = View(w_end, (slice(None), pl.ds(n_text, 2 * dv)), (Z, 2 * dv, wv))
    norm_t = [((ct, dt), F32, 0), ((ct, dt), F32, 0), ((ct, dt), BF, 0)]
    ffn_t = [((rt, dt), BF, 0), ((rt, ft), F32, 0), ((rt, ft), BF, 0), ((ct, dt), BF, Z)]
    zt0, at, atb = run(
        "text_norm0", functools.partial(text_norm, 0), norm_t,
        [scalars, swap(st), bt, text_gains, text_shifts],
    )
    xt1, ut1, gt1, st = run(
        "text_ffn1", text_ffn, ffn_t, [scalars, spread(atb), co_text_up, co_text_down]
    )
    zv0, av, uv1, gv1, zv1, bv, bvb = run(
        "image_mid", functools.partial(image_mid, 0),
        [((cv, dv), F32, 0), ((cv, dv), BF, 0), ((cv, dv), F32, 0), ((cv, dv), BF, 0),
         ((cv, dv), F32, 0), ((cv, dv), F32, 0), ((cv, dv), BF, 0)],
        [scalars, swap(sv), bv, w_mid, image_gains, image_shifts],
        [((cv, dv), F32)],
    )
    zt1, bt, btb = run(
        "text_norm1", functools.partial(text_norm, 1), norm_t,
        [scalars, swap(st), at, text_gains, text_shifts],
    )
    cot = joined(pad_rows(text_cot, nt), pad_rows(image_cot, nv), Z)
    (cot,) = run("cut", cut, [(*shard, Z)], [scalars, cot])
    cot = swap(cot)
    xt2, qt2, ot2, st = run(
        "text_self", functools.partial(self_fwd, text_dims),
        [((rt, dt), BF, 0), ((3, rt, st_w), BF, 0), ((rt, st_w), BF, 0), ((ct, dt), BF, Z)],
        [scalars, spread(btb), self_text_qkv, self_text_out],
    )
    xv2, qv2, ov2, sv = run(
        "image_self", functools.partial(self_fwd, image_dims),
        [((rv, dv), BF, 0), ((3, rv, si_w), BF, 0), ((rv, si_w), BF, 0), ((cv, dv), BF, Z)],
        [scalars, spread(bvb), self_image_qkv, self_image_out],
    )
    hidden = Z * ft
    out_t, at3, gt3, dt3, dut3, gt, gtb, stat_t1 = run(
        "text_turn", functools.partial(text_turn, 2),
        [((ct, wt), BF, Z), ((ct, dt), BF, 0), ((ct, hidden), BF, 0), ((ct, dt), BF, 0),
         ((ct, hidden), BF, 0), ((ct, dt), F32, 0), ((ct, dt), BF, 0), ((4, dt), F32, 0)],
        [scalars, swap(st), bt, cot, w_text, text_gains, text_shifts],
        [((ct, hidden), F32), ((ct, dt), F32), ((ct, dt), F32)],
    )
    out_v, av3, gv3, dv3, duv3, gv, gvb, stat_v1 = run(
        "image_turn", functools.partial(image_turn, 2),
        [((cv, wv), BF, Z), ((cv, dv), BF, 0), ((cv, dv), BF, 0), ((cv, dv), BF, 0),
         ((cv, dv), BF, 0), ((cv, dv), F32, 0), ((cv, dv), BF, 0), ((4, dv), F32, 0)],
        [scalars, swap(sv), bv, cot, w_image, image_gains, image_shifts],
        [((cv, dv), F32)] * 8,
    )
    back_ffn = [((rt, dt), BF, 0), ((rt, ft), BF, 0), ((ct, dt), BF, Z)]
    stat_shape = ((2, dt), F32, 0)
    def image_ffn_grads(name, *saved):
        keep, give = run(
            "grads_" + name, grads_image_ffn, [((Z * dv, wv), BF, 0)] * 2, [scalars, *saved]
        )
        return keep, along(give, 0, 0, 1)
    def core_summed(name, halves, after):
        (chunks,) = run(
            "core_sum_" + name, core_sum, [((dv, wv), BF, Z)], [scalars, *halves], after=after
        )
        return chunks
    (end,) = run(
        "grads_end", grads_end, [((n_dp, Z, (n_text + 2 * dv) // n_dp, wv), BF, 0)],
        [scalars, at3, dut3, gt3, dt3, av3, duv3, gv3, dv3],
    )
    end_cut = lax.psum_scatter(end, "dp", scatter_dimension=0, tiled=False)
    dt2, dqt2, st = run(
        "text_self_back", functools.partial(self_bwd, text_dims),
        [((rt, dt), BF, 0), ((3, rt, st_w), BF, 0), ((ct, dt), BF, Z)],
        [scalars, spread(gtb), qt2, self_text_qkv, self_text_out],
        [((rt, st_w), BF)],
    )
    dv2, dqv2, sv = run(
        "image_self_back", functools.partial(self_bwd, image_dims),
        [((rv, dv), BF, 0), ((3, rv, si_w), BF, 0), ((cv, dv), BF, Z)],
        [scalars, spread(gvb), qv2, self_image_qkv, self_image_out],
        [((rv, si_w), BF)],
    )
    gt, gtb, stat_t2 = run(
        "text_norm1_back", functools.partial(text_norm_back, 1),
        [((ct, dt), F32, 0), ((ct, dt), BF, 0), stat_shape],
        [scalars, swap(st), gt, zt1, text_gains],
    )
    st_q, sv_q, st_o, sv_o = run(
        "grads_self", grads_attention,
        [((3, dt, st_w), BF, 0), ((3, dv, si_w), BF, 0), ((st_w, dt), BF, 0), ((si_w, dv), BF, 0)],
        [scalars, xt2, dqt2, xv2, dqv2, ot2, dt2, ov2, dv2],
    )
    dt1, dut1, st = run(
        "text_ffn1_back", text_ffn_back, back_ffn,
        [scalars, spread(gtb), co_text_up, co_text_down, ut1],
    )
    dv1, duv1, gv, gvb, _ = run(
        "image_mid_back", functools.partial(image_mid_back, 0),
        [((cv, dv), BF, 0), ((cv, dv), BF, 0), ((cv, dv), F32, 0), ((cv + 16, dv), BF, 0),
         ((4, dv), F32, 0)],
        [scalars, swap(sv), gv, zv1, zv0, uv1, w_mid, image_gains, stat_v1],
        [((cv, dv), F32)] * 2,
    )
    mid_f = image_ffn_grads("mid", av, duv1, gv1, dv1)
    gt, gtb, _ = run(
        "text_norm0_back", functools.partial(text_norm_back_stats, 0),
        [((ct, dt), F32, 0), ((ct + 16, dt), BF, 0), stat_shape],
        [scalars, swap(st), gt, zt0, text_gains, stat_t2, stat_t1],
    )
    t1_up, t1_down = run(
        "grads_ffn1", grads_text_ffn, [((dt, ft), BF, 0), ((ft, dt), BF, 0)],
        [scalars, xt1, dut1, gt1, dt1],
    )
    zt, zv = spread(gtb), spread(gvb)
    mid_f = core_summed("mid", mid_f, zt[1:] + zv[1:])
    dqt0, dqv0, tq, vq, to, vo = run(
        "co_back", functools.partial(co_bwd, co_dims),
        [((3, rt, co_w), BF, 0), ((3, rv, co_w), BF, 0),
         ((3, dt, co_w), BF, 0), ((3, dv, co_w), BF, 0), ((co_w, dt), BF, 0), ((co_w, dv), BF, 0)],
        [scalars, zt, zv, qt0, qv0, co_text_out, co_image_out, xt0, xv0, ot0, ov0],
        [((rt, dt), BF), ((rv, dv), BF), ((rt, co_w), BF), ((rv, co_w), BF)],
    )
    (end_cut,) = run(
        "cut_end", cut_static, [(end_cut.shape[1:], BF, Z)], [scalars, end_cut]
    )
    end_cut = swap(end_cut)
    (s,) = run(
        "co_back_in", co_bwd_in, [(*whole, Z)],
        [scalars, dqt0, dqv0, co_text_qkv, co_image_qkv, gt, gv],
        [((rt, wt), F32), ((rv, wv), F32)],
    )
    (mid_f,) = run(
        "tensor_sum_mid", tensor_sum_stats, [((2, dv + 32, wv), BF, 0)],
        [scalars, swap(mid_f), zt, zv],
    )
    (end,) = run(
        "place_end", place_rows, [((n_text + 2 * dv, wv), BF, 0)], [scalars, end_cut]
    )
    late = lax.psum((st_q, t1_up, t1_down, sv_q, st_o, sv_o, tq, vq, to, vo, mid_f, end), "dp")
    s = swap(s)
    out_t, out_v = swap(out_t), swap(out_v)
    ffn_out = [((dt, ft), F32, 0), ((ft, dt), F32, 0)]
    image_out_shapes = [((dv, wv), F32, 0), ((wv, dv), F32, 0)]
    (st_q, t1_up, t1_down, sv_q, st_o, sv_o, tq, vq, to, vo, mid_up, mid_down, tg, ts, vg, vs,
     t_up, t_down, end_up, end_down) = run(
        "finish", finish,
        [((3, st_w, dt), F32, 0)] + ffn_out
        + [((3, dv, si_w), F32, 0), ((st_w, dt), F32, 0), ((si_w, dv), F32, 0),
           ((3, dt, co_w), F32, 0), ((3, dv, co_w), F32, 0),
           ((co_w, dt), F32, 0), ((co_w, dv), F32, 0)] + image_out_shapes
        + [((4, dt), F32, 0)] * 2 + [((4, dv), F32, 0)] * 2 + ffn_out + image_out_shapes,
        [scalars, *late],
    )
    st_q = st_q.transpose(0, 2, 1)

    text_out = in_order(out_t, rank).reshape(rt, wt)
    image_out = in_order(out_v, rank).reshape(rv, wv)
    text_grad, image_grad = parted(sum(member.astype(F32) for member in s)[None], rt, wt)
    return (
        unpad_rows(text_out, text_in.shape, nt).astype(F32),
        unpad_rows(image_out, image_in.shape, nv).astype(F32),
        unpad_rows(text_grad, text_in.shape, nt),
        unpad_rows(image_grad, image_in.shape, nv),
        tq, vq, to, vo, t1_up, t1_down, mid_up, mid_down,
        st_q, sv_q, st_o, sv_o, t_up, t_down, end_up, end_down,
        tg, ts, vg, vs,
    )


def solution(mesh):
    stream = P(None, "dp", None, "tensor")
    lengths = P(None, "dp")
    stacked = P(None, None, "tensor")
    rows = P("tensor", None)
    cols = P(None, "tensor")
    weights = (
        stacked, stacked, rows, rows, cols, rows, cols, rows,
        stacked, stacked, rows, rows, cols, rows, cols, rows,
        P(), P(), P(), P(),
    )
    in_specs = (stream, stream, lengths, lengths, stream, stream) + weights
    out_specs = (stream,) * 4 + weights
    return jax.shard_map(shards, mesh=mesh, in_specs=in_specs, out_specs=out_specs, check_vma=False)
```

```python
import functools
import math

import jax
import jax.numpy as jnp
from jax import lax
from jax.experimental import pallas as pl
from jax.experimental.pallas import tpu as pltpu
from jax.sharding import PartitionSpec as P

CO_HEAD = 128
TEXT_HEAD = 64
IMAGE_HEAD = 128
EPS = 1e-05
FILL = -1000000000.0
ROOT_HALF = 0.7071067811865476
INV_ROOT_TWO_PI = 0.3989422804014327
F32 = jnp.float32
BF = jnp.bfloat16
Z = 4
COST = pl.CostEstimate(flops=20_000_000_000, bytes_accessed=1000, transcendentals=0)
LENGTHS = 5


def dot(a, b):
    return lax.dot_general(a, b, (((1,), (0,)), ((), ())), preferred_element_type=F32)


def dot_nt(a, b):
    return lax.dot_general(a, b, (((1,), (1,)), ((), ())), preferred_element_type=F32)


def dot_tn(a, b):
    return lax.dot_general(a, b, (((0,), (0,)), ((), ())), preferred_element_type=F32)


def part(index, size):
    return pl.ds(pl.multiple_of(index * size, size), size)


def row_ids(count, step, samples):
    place = lax.broadcasted_iota(jnp.int32, (count, 1), 0)
    ids = jnp.zeros((count, 1), jnp.int32)
    for s in range(1, samples):
        ids = ids + (place >= s * step).astype(jnp.int32)
    return ids


def key_ids(pos, first, m, step, samples, count):
    place = lax.broadcasted_iota(jnp.int32, (1, count), 1)
    ids = jnp.full((1, count), -1, jnp.int32)
    for s in range(samples):
        live = pos[first + m * samples + s]
        ids = jnp.where((place >= s * step) & (place < s * step + live), s, ids)
    return ids


def probabilities(q, k, same, scale):
    s = jnp.where(same, dot_nt(q, k) * scale, FILL)
    e = jnp.exp(s - jnp.max(s, axis=-1, keepdims=True))
    return e / jnp.sum(e, axis=-1, keepdims=True)


def head_fwd(q, k, v, same, scale):
    return dot(probabilities(q, k, same, scale).astype(BF), v).astype(BF)


def head_bwd(q, k, v, same, scale, do):
    p = probabilities(q, k, same, scale)
    dv = dot_tn(p.astype(BF), do)
    dp = dot_nt(do, v)
    ds = (p * (dp - jnp.sum(dp * p, axis=-1, keepdims=True))).astype(BF)
    dq = dot(ds, k) * scale
    dk = dot_tn(ds, q) * scale
    return dq.astype(BF), dk.astype(BF), dv.astype(BF)


def gelu(u):
    return u * (1.0 + lax.erf(u * ROOT_HALF)) * 0.5


def gelu_slope(u):
    return (1.0 + lax.erf(u * ROOT_HALF)) * 0.5 + u * jnp.exp(u * u * -0.5) * INV_ROOT_TWO_PI


def normalise(z):
    centre = z - jnp.mean(z, axis=-1, keepdims=True)
    rstd = lax.rsqrt(jnp.mean(centre * centre, axis=-1, keepdims=True) + EPS)
    return centre * rstd, rstd


def norm_back(z, gain, dy):
    xhat, rstd = normalise(z)
    dxh = dy * gain
    dz = rstd * (
        dxh
        - jnp.mean(dxh, axis=-1, keepdims=True)
        - xhat * jnp.mean(dxh * xhat, axis=-1, keepdims=True)
    )
    return dz, jnp.sum(dy * xhat, axis=0, keepdims=True), jnp.sum(dy, axis=0, keepdims=True)


class Arriving:
    in_loop = False

    def __init__(self, ref, copy):
        self.ref, self.copy = ref, copy
        self.shape, self.dtype = ref.shape, ref.dtype

    def wait(self):
        if self.copy is not None:
            assert not Arriving.in_loop
            self.copy.wait()
            self.copy = None

    def __getitem__(self, index):
        self.wait()
        return self.ref[index]

    @property
    def at(self):
        self.wait()
        return self.ref.at


class Scalars:
    def __init__(self, places, *lengths):
        self.places, self.lengths = places, lengths

    def __getitem__(self, i):
        if i < LENGTHS:
            return self.places[i]
        micro, samples = self.lengths[0].shape
        which, at = divmod(i - LENGTHS, micro * samples)
        return self.lengths[which][at // samples, at % samples]


class View:
    def __init__(self, array, index, shape):
        self.array, self.index, self.shape, self.dtype = array, index, shape, array.dtype


class Leaving:
    def __init__(self, ref, target, sem):
        self.ref, self.target, self.sem, self.sent = ref, target, sem, False
        self.copy = pltpu.make_async_copy(ref, target, sem)
        self.shape, self.dtype, self.at = ref.shape, ref.dtype, ref.at

    def send(self):
        if not self.sent:
            self.copy.start()
            self.sent = True

    def send_part(self, index, last):
        pltpu.make_async_copy(self.ref.at[index], self.target.at[index], self.sem).start()
        self.sent = last

    def __getitem__(self, index):
        return self.ref[index]

    def __setitem__(self, index, value):
        assert not self.sent
        self.ref[index] = value


def send(*refs):
    for ref in refs:
        for one in ref if isinstance(ref, list) else [ref]:
            one.send()


def ready(*refs):
    for ref in refs:
        for one in ref if isinstance(ref, list) else [ref]:
            one.wait()


def tiles(count, tile, body):
    def step(i, carry):
        body(part(i, tile))
        return carry

    Arriving.in_loop = True
    lax.fori_loop(0, count // tile, step, 0)
    Arriving.in_loop = False


def total(refs, rows):
    acc = refs[0][rows, :].astype(F32)
    for ref in refs[1:]:
        acc = acc + ref[rows, :].astype(F32)
    return acc


def lanes_in_order(values, r, width):
    near = [values[0], values[3], values[2], values[1]]
    joined = jnp.concatenate([value.astype(F32) for value in near], axis=1)
    return pltpu.roll(joined, r * width, 1)


def lanes_from_own(values, r, width):
    return pltpu.roll(values, ((Z - r) & 3) * width, 1)


def rows_in_order(full, refs, r):
    size = full.shape[0] // Z
    for k, ref in enumerate(refs):
        full[part((r - k) & 3, size), :] = ref[0:size, :]


def packed_rows(rows, width, wide):
    return rows * width // wide if width < wide else rows


def put_text(ref, at, value):
    rows, width = value.shape
    wide = ref.shape[1]
    main = packed_rows(rows, width, wide)
    rest = rows - main
    ref[at : at + main, 0:width] = value[0:main]
    for j in range(width // (wide - width)):
        cols = slice(j * (wide - width), (j + 1) * (wide - width))
        ref[at + j * rest : at + (j + 1) * rest, width:wide] = value[main:rows, cols]


def get_text(ref, at, rows, width):
    wide = ref.shape[1]
    if width == wide:
        return ref[at : at + rows, :]
    main = packed_rows(rows, width, wide)
    rest = rows - main
    tail = [
        ref[at + j * rest : at + (j + 1) * rest, width:wide]
        for j in range(width // (wide - width))
    ]
    return jnp.concatenate([ref[at : at + main, 0:width], jnp.concatenate(tail, axis=1)], axis=0)


def split(refs, *counts):
    found, at = [], 0
    for count in counts:
        found.append(refs[at] if count == 0 else list(refs[at : at + count]))
        at += max(count, 1)
    assert at == len(refs)
    return found


def co_fwd(dims, *refs):
    rank, both, wt, wv, pt, pv, xt, xv, bt, bv, qt, qv, ot, ov, st, sv = split(
        refs, 0, 4, 0, 0, 0, 0, 0, 0, 0, 0, 0, 0, 0, 0, 4, 4
    )
    samples, text, regions, nt, nv = dims
    r = rank[0]
    rows_t, rows_v = xt.shape[0], xv.shape[0]
    width_t, width_v = xt.shape[1] // Z, xv.shape[1] // Z
    ct, cv = bt.shape[0], bv.shape[0]
    tin = [get_text(ref, rows_v, rows_t, width_t) for ref in both]
    xt[...] = lanes_in_order(tin, r, width_t).astype(BF)
    for k, ref in enumerate(both):
        xv[:, part((r - k) & 3, width_v)] = ref[0:rows_v, :]
    bt[...] = xt[part(r, ct), :]
    bv[...] = xv[part(r, cv), :]
    send(xt, xv, bt, bv)
    for i in range(3):
        qt[i] = dot(xt[...], wt[i]).astype(BF)

    def project(rows):
        for i in range(3):
            qv[i, rows, :] = dot(xv[rows, :], wv[i]).astype(BF)

    ready(wv)
    tiles(xv.shape[0], cv, project)
    send(qt, qv)
    scale = CO_HEAD ** (-0.5)
    rid_t, rid_v = row_ids(nt, text, samples), row_ids(nv, regions, samples)
    for m in range(2):
        rt, rv = slice(m * nt, (m + 1) * nt), slice(m * nv, (m + 1) * nv)
        same_tv = rid_t == key_ids(rank, LENGTHS + 2 * samples, m, regions, samples, nv)
        same_vt = rid_v == key_ids(rank, LENGTHS, m, text, samples, nt)
        for h in range(qt.shape[2] // CO_HEAD):
            c = slice(h * CO_HEAD, (h + 1) * CO_HEAD)
            ot[rt, c] = head_fwd(qt[0, rt, c], qv[1, rv, c], qv[2, rv, c], same_tv, scale)
            ov[rv, c] = head_fwd(qv[0, rv, c], qt[1, rt, c], qt[2, rt, c], same_vt, scale)
    for k in range(Z):
        c = (r + k) & 3
        st[k][...] = dot(ot[part(c, ct), :], pt[...]).astype(BF)
        sv[k][...] = dot(ov[part(c, cv), :], pv[...]).astype(BF)
        send(st[k], sv[k])


def co_bwd(dims, *refs):
    (rank, dt, dv, qt, qv, pt, pv, xt, xv, ot, ov,
     dqt, dqv, tq, vq, to, vo, zt, zv, dot_s, dov_s) = split(
        refs, 0, 4, 4, *([0] * 18)
    )
    samples, text, regions, nt, nv = dims
    r = rank[0]
    cv = zv.shape[0] // Z
    rows_in_order(zt, dt, r)
    rows_in_order(zv, dv, r)
    dot_s[...] = dot_nt(zt[...], pt[...]).astype(BF)

    def back_out(rows):
        dov_s[rows, :] = dot_nt(zv[rows, :], pv[...]).astype(BF)

    ready(pv)
    tiles(zv.shape[0], cv, back_out)
    scale = CO_HEAD ** (-0.5)
    rid_t, rid_v = row_ids(nt, text, samples), row_ids(nv, regions, samples)
    for m in range(2):
        rt, rv = slice(m * nt, (m + 1) * nt), slice(m * nv, (m + 1) * nv)
        same_tv = rid_t == key_ids(rank, LENGTHS + 2 * samples, m, regions, samples, nv)
        same_vt = rid_v == key_ids(rank, LENGTHS, m, text, samples, nt)
        for h in range(qt.shape[2] // CO_HEAD):
            c = slice(h * CO_HEAD, (h + 1) * CO_HEAD)
            a, b, d = head_bwd(
                qt[0, rt, c], qv[1, rv, c], qv[2, rv, c], same_tv, scale, dot_s[rt, c]
            )
            dqt[0, rt, c], dqv[1, rv, c], dqv[2, rv, c] = a, b, d
            a, b, d = head_bwd(
                qv[0, rv, c], qt[1, rt, c], qt[2, rt, c], same_vt, scale, dov_s[rv, c]
            )
            dqv[0, rv, c], dqt[1, rt, c], dqt[2, rt, c] = a, b, d
    send(dqt, dqv)
    for i in range(3):
        matrix_whole(tq.at[i], xt, dqt.at[i])
        matrix_whole(vq.at[i], xv, dqv.at[i])
    send(tq, vq)
    matrix_whole(to, ot, zt)
    matrix_whole(vo, ov, zv)


def co_bwd_in(*refs):
    rank, dqt, dqv, wt, wv, gt, gv, s, acc_t, acc_v = split(
        refs, 0, 0, 0, 0, 0, 0, 0, 4, 0, 0
    )
    r = rank[0]
    rows_v = acc_v.shape[0]
    ct, cv = gt.shape[0], gv.shape[0]
    width_t, width_v = acc_t.shape[1], acc_v.shape[1]
    own_t = lanes_from_own(gt[...], r, width_t)
    for k in range(Z):
        c = (r + k) & 3
        acc_t[...] = sum(dot_nt(dqt[i], wt[i, part(c, width_t), :]) for i in range(3))
        acc_t[part(r, ct), :] += own_t[:, k * width_t : (k + 1) * width_t]
        put_text(s[k], rows_v, acc_t[...].astype(BF))

        ready(wv, dqv)

        def back_in(rows):
            acc_v[rows, :] = sum(
                dot_nt(dqv[i, rows, :], wv[i, part(c, width_v), :]) for i in range(3)
            )

        tiles(acc_v.shape[0], cv, back_in)
        acc_v[part(r, cv), :] += gv[:, part(c, width_v)]
        s[k][0:rows_v, :] = acc_v[...].astype(BF)
        send(s[k])


def self_fwd(dims, *refs):
    rank, xin, w, po, x, q, o, s = split(refs, 0, 4, 0, 0, 0, 0, 0, 4)
    samples, step, n, head, first = dims
    r = rank[0]
    size = xin[0].shape[0]
    rows_in_order(x, xin, r)
    send(x)

    def project(rows):
        for i in range(3):
            q[i, rows, :] = dot(x[rows, :], w[i]).astype(BF)

    ready(w)
    tiles(x.shape[0], size, project)
    send(q)
    rid = row_ids(n, step, samples)
    for m in range(2):
        rm = slice(m * n, (m + 1) * n)
        same = rid == key_ids(rank, first, m, step, samples, n)
        for h in range(q.shape[2] // head):
            c = slice(h * head, (h + 1) * head)
            o[rm, c] = head_fwd(q[0, rm, c], q[1, rm, c], q[2, rm, c], same, head ** (-0.5))
    send(o)
    for k in range(Z):
        s[k][...] = dot(o[part((r + k) & 3, size), :], po[...]).astype(BF)
        send(s[k])


def self_bwd(dims, *refs):
    rank, din, q, w, po, z, dq, s, do = split(refs, 0, 4, 0, 0, 0, 0, 0, 4, 0)
    samples, step, n, head, first = dims
    r = rank[0]
    size = din[0].shape[0]
    rows_in_order(z, din, r)
    send(z)

    def back_out(rows):
        do[rows, :] = dot_nt(z[rows, :], po[...]).astype(BF)

    ready(po)
    tiles(z.shape[0], size, back_out)
    rid = row_ids(n, step, samples)
    for m in range(2):
        rm = slice(m * n, (m + 1) * n)
        same = rid == key_ids(rank, first, m, step, samples, n)
        for h in range(q.shape[2] // head):
            c = slice(h * head, (h + 1) * head)
            a, b, d = head_bwd(
                q[0, rm, c], q[1, rm, c], q[2, rm, c], same, head ** (-0.5), do[rm, c]
            )
            dq[0, rm, c], dq[1, rm, c], dq[2, rm, c] = a, b, d
    send(dq)
    for k in range(Z):
        rows = part((r + k) & 3, size)
        s[k][...] = sum(dot_nt(dq[i, rows, :], w[i]) for i in range(3)).astype(BF)
        send(s[k])


def text_total(base, s):
    return base[...].astype(F32) + total(s, slice(None))


def stat_rows(out, at, *stats):
    every = jnp.concatenate([ref[...] for ref in stats], axis=0)
    pad = jnp.zeros((out.shape[0] - at - every.shape[0], out.shape[1]), F32)
    out[at : out.shape[0], :] = jnp.concatenate([every, pad], axis=0).astype(BF)


def cut(*refs):
    pos, whole, out = split(refs, 0, 0, 4)
    for k in range(Z):
        out[k][...] = whole[(pos[0] + k) & 3]


def text_norm(position, *refs):
    rank, s, base, gains, shifts, z, y, out = split(refs, 0, 4, 0, 0, 0, 0, 0, 0)
    zz = text_total(base, s)
    z[...] = zz
    yy = normalise(zz)[0] * gains[position : position + 1, :] + shifts[position : position + 1, :]
    y[...] = yy
    out[...] = yy.astype(BF)


def text_norm_back(position, *refs):
    rank, s, base, z, gains, dz, out, stat = split(refs, 0, 4, 0, 0, 0, 0, 0, 0)
    d, dg, ds = norm_back(z[...], gains[position : position + 1, :], text_total(base, s))
    dz[...] = d
    out[...] = d.astype(BF)
    stat[0:1, :] = dg
    stat[1:2, :] = ds


def text_norm_back_stats(position, *refs):
    rank, s, base, z, gains, stat_1, stat_2, dz, out, stat = split(
        refs, 0, 4, 0, 0, 0, 0, 0, 0, 0, 0
    )
    d, dg, ds = norm_back(z[...], gains[position : position + 1, :], text_total(base, s))
    dz[...] = d
    rows = d.shape[0]
    out[0:rows, :] = d.astype(BF)
    stat[0:1, :] = dg
    stat[1:2, :] = ds
    stat_rows(out, rows, stat, stat_1, stat_2)


def text_turn(position, *refs):
    (rank, s, base, cot, w, gains, shifts, out, a, g, d1b, du, dz, send_on, stat,
     u, x, d1) = split(refs, 0, 4, 0, 4, 0, 0, 0, 4, 0, 0, 0, 0, 0, 0, 0, 0, 0, 0)
    r = rank[0]
    g0, b0 = gains[position : position + 1, :], shifts[position : position + 1, :]
    g1, b1 = gains[position + 1 : position + 2, :], shifts[position + 1 : position + 2, :]
    rows, width = base.shape[0], base.shape[1] // Z
    at = cot[0].shape[0] - packed_rows(rows, width, cot[0].shape[1])
    wide, deep = w.shape[2], base.shape[1]
    blocks = deep // wide
    z0 = text_total(base, s)
    x[...] = normalise(z0)[0] * g0 + b0
    a[...] = x[...].astype(BF)
    send(a)
    down = blocks * deep
    for c in range(Z):
        for j in range(blocks):
            cols = slice((c * blocks + j) * wide, (c * blocks + j + 1) * wide)
            uu = dot(a[...], w[c, j * deep : (j + 1) * deep, :])
            u[:, cols] = uu
            g[:, cols] = gelu(uu).astype(BF)
    send(g)
    for j in range(blocks):
        cols = slice(j * wide, (j + 1) * wide)
        acc = x[:, cols]
        for c in range(Z):
            own = slice(c * deep, (c + 1) * deep)
            acc = acc + dot(g[:, own], w[c, down + j * deep : down + (j + 1) * deep, :])
        x[:, cols] = acc
    z1 = x[...]
    y = lanes_from_own(normalise(z1)[0] * g1 + b1, r, width)
    for k in range(Z):
        out[k][...] = y[:, k * width : (k + 1) * width].astype(BF)
        send(out[k])
    dy = lanes_in_order([get_text(ref, at, rows, width) for ref in cot], r, width)
    d, dg, ds = norm_back(z1, g1, dy)
    d1[...] = d
    d1b[...] = d.astype(BF)
    send(d1b)
    stat[2:3, :] = dg
    stat[3:4, :] = ds
    for c in range(Z):
        own = slice(c * deep, (c + 1) * deep)
        back = sum(
            dot_nt(
                d1b[:, j * wide : (j + 1) * wide],
                w[c, down + j * deep : down + (j + 1) * deep, :],
            )
            for j in range(blocks)
        )
        du[:, own] = (back * gelu_slope(u[:, own])).astype(BF)
    send(du)
    back = d1[...]
    for c in range(Z):
        for j in range(blocks):
            cols = slice((c * blocks + j) * wide, (c * blocks + j + 1) * wide)
            back = back + dot_nt(du[:, cols], w[c, j * deep : (j + 1) * deep, :])
    d, dg, ds = norm_back(z0, g0, back)
    dz[...] = d
    send_on[...] = d.astype(BF)
    stat[0:1, :] = dg
    stat[1:2, :] = ds


def text_ffn(*refs):
    rank, xin, up, down, x, u, g, s = split(refs, 0, 4, 0, 0, 0, 0, 0, 4)
    r = rank[0]
    size = xin[0].shape[0]
    rows_in_order(x, xin, r)

    def hidden(rows):
        uu = dot(x[rows, :], up[...])
        u[rows, :] = uu
        g[rows, :] = gelu(uu).astype(BF)

    ready(up)
    tiles(x.shape[0], size, hidden)
    send(x, u, g)
    for k in range(Z):
        s[k][...] = dot(g[part((r + k) & 3, size), :], down[...]).astype(BF)
        send(s[k])


def text_ffn_back(*refs):
    rank, din, up, down, u, z, du, s = split(refs, 0, 4, 0, 0, 0, 0, 0, 4)
    r = rank[0]
    size = din[0].shape[0]
    rows_in_order(z, din, r)

    def hidden(rows):
        du[rows, :] = (dot_nt(z[rows, :], down[...]) * gelu_slope(u[rows, :])).astype(BF)

    ready(down, u)
    tiles(z.shape[0], size, hidden)
    send(z, du)
    for k in range(Z):
        s[k][...] = dot_nt(du[part((r + k) & 3, size), :], up[...]).astype(BF)


def image_hidden(a, w, u, g):
    width = w.shape[2]
    depth = w.shape[1] // 2
    for c in range(Z):
        cols = slice(c * width, (c + 1) * width)
        uu = dot(a[...], w[c, 0:depth, :])
        u[:, cols] = uu
        g[:, cols] = gelu(uu).astype(BF)


def image_down(af, g, w, z):
    width = w.shape[2]
    depth = w.shape[1] // 2
    for n in range(Z):
        out = slice(n * width, (n + 1) * width)
        acc = af[:, out]
        rows = slice(depth + n * width, depth + (n + 1) * width)
        for c in range(Z):
            cols = slice(c * width, (c + 1) * width)
            acc = acc + dot(g[:, cols], w[c, rows, :])
        z[:, out] = acc


def image_hidden_back(dzb, w, u, du):
    width = w.shape[2]
    depth = w.shape[1] // 2
    for c in range(Z):
        cols = slice(c * width, (c + 1) * width)
        dg = sum(
            dot_nt(
                dzb[:, n * width : (n + 1) * width],
                w[c, depth + n * width : depth + (n + 1) * width, :],
            )
            for n in range(Z)
        )
        du[:, cols] = (dg * gelu_slope(u[:, cols])).astype(BF)


def image_up_back(dz, du, w, da):
    width = w.shape[2]
    width = w.shape[2]
    for n in range(Z):
        out = slice(n * width, (n + 1) * width)
        acc = dz[:, out]
        for c in range(Z):
            cols = slice(c * width, (c + 1) * width)
            acc = acc + dot_nt(du[:, cols], w[c, n * width : (n + 1) * width, :])
        da[:, out] = acc


def image_mid(position, *refs):
    rank, s, base, w, gains, shifts, z0, a, u, g, z1, y, yb, af = split(
        refs, 0, 4, 0, 0, 0, 0, 0, 0, 0, 0, 0, 0, 0, 0
    )
    g0, b0 = gains[position : position + 1, :], shifts[position : position + 1, :]
    g1, b1 = gains[position + 1 : position + 2, :], shifts[position + 1 : position + 2, :]

    def first(rows):
        zz = base[rows, :].astype(F32) + total(s, rows)
        z0[rows, :] = zz
        aa = normalise(zz)[0] * g0 + b0
        af[rows, :] = aa
        a[rows, :] = aa.astype(BF)

    ready(base, s, gains, shifts)
    tiles(z0.shape[0], 32, first)
    send(z0, a)
    image_hidden(a, w, u, g)
    send(u, g)
    image_down(af, g, w, z1)
    send(z1)

    def second(rows):
        yy = normalise(z1[rows, :])[0] * g1 + b1
        y[rows, :] = yy
        yb[rows, :] = yy.astype(BF)

    tiles(z0.shape[0], 32, second)


def image_mid_back(position, *refs):
    rank, s, base, z1, z0, u, w, gains, stat_1, d1b, du, d0, d0b, stat, d1, da = split(
        refs, 0, 4, 0, 0, 0, 0, 0, 0, 0, 0, 0, 0, 0, 0, 0, 0
    )
    g0 = gains[position : position + 1, :]
    g1 = gains[position + 1 : position + 2, :]
    stat[...] = jnp.zeros_like(stat)

    def first(rows):
        d, dg, ds = norm_back(z1[rows, :], g1, base[rows, :] + total(s, rows))
        d1[rows, :] = d
        d1b[rows, :] = d.astype(BF)
        stat[2:3, :] += dg
        stat[3:4, :] += ds

    ready(z1, base, s)
    tiles(z0.shape[0], 32, first)
    image_hidden_back(d1b, w, u, du)
    image_up_back(d1, du, w, da)
    ready(z0)

    def second(rows):
        d, dg, ds = norm_back(z0[rows, :], g0, da[rows, :])
        d0[rows, :] = d
        d0b[rows, :] = d.astype(BF)
        stat[0:1, :] += dg
        stat[1:2, :] += ds

    tiles(z0.shape[0], 32, second)
    stat_rows(d0b, z0.shape[0], stat, stat_1)


def image_turn(position, *refs):
    (rank, s, base, cot, w, gains, shifts, out, a, g, d1b, du, d0, d0b, stat,
     z0, af, u, z1, y, dy, d1, da) = split(
        refs, 0, 4, 0, 4, 0, 0, 0, 4, 0, 0, 0, 0, 0, 0, 0, 0, 0, 0, 0, 0, 0, 0, 0
    )
    r = rank[0]
    g0, b0 = gains[position : position + 1, :], shifts[position : position + 1, :]
    g1, b1 = gains[position + 1 : position + 2, :], shifts[position + 1 : position + 2, :]
    width = dy.shape[1] // Z
    stat[...] = jnp.zeros_like(stat)
    for k, ref in enumerate(cot):
        dy[:, part((r - k) & 3, width)] = ref[0 : dy.shape[0], :].astype(F32)

    def first(rows):
        zz = base[rows, :] + total(s, rows)
        z0[rows, :] = zz
        aa = normalise(zz)[0] * g0 + b0
        af[rows, :] = aa
        a[rows, :] = aa.astype(BF)

    ready(base, s, gains, shifts)
    tiles(z0.shape[0], 32, first)
    image_hidden(a, w, u, g)
    image_down(af, g, w, z1)

    def second(rows):
        zz = z1[rows, :]
        y[rows, :] = normalise(zz)[0] * g1 + b1
        d, dg, ds = norm_back(zz, g1, dy[rows, :])
        d1[rows, :] = d
        d1b[rows, :] = d.astype(BF)
        stat[2:3, :] += dg
        stat[3:4, :] += ds

    tiles(z0.shape[0], 32, second)
    for k in range(Z):
        out[k][...] = y[:, part((r + k) & 3, width)].astype(BF)
    image_hidden_back(d1b, w, u, du)
    image_up_back(d1, du, w, da)

    def third(rows):
        d, dg, ds = norm_back(z0[rows, :], g0, da[rows, :])
        d0[rows, :] = d
        d0b[rows, :] = d.astype(BF)
        stat[0:1, :] += dg
        stat[1:2, :] += ds

    tiles(z0.shape[0], 32, third)


def ffn_pieces(core, keep, give, a, du, g, dz):
    width = a.shape[1] // Z
    half = a.shape[1] // 2
    for out, which in ((keep, core), (give, 1 - core)):
        cols = part(which, half)
        left_up, right_down = a[:, cols], dz[:, cols]
        for c in range(Z):
            block = slice(c * width, (c + 1) * width)
            row = c * 2 * half
            out[row : row + half, :] = dot_tn(left_up, du[:, block]).astype(BF)
            down = dot_tn(g[:, block], right_down).astype(BF)
            for j in range(half // width):
                at = row + half + j * width
                out[at : at + width, :] = down[:, j * width : (j + 1) * width]


def matrix_whole(out, left, right):
    step = 256 if left.shape[1] % 256 == 0 else left.shape[1]
    for j in range(left.shape[1] // step):
        rows = slice(j * step, (j + 1) * step)
        out[rows, :] = dot_tn(left[:, rows], right[...]).astype(BF)
    if isinstance(out, Leaving):
        send(out)


def grads_image_ffn(*refs):
    pos, a, du, g, dz, keep, give = refs
    ffn_pieces(pos[3], keep, give, a, du, g, dz)


def grads_end(*refs):
    pos, x, du, g, dz, xv, duv, gv, dzv, out = refs
    count, size, wide = out.shape[0], out.shape[2], out.shape[3]
    deep, tall = x.shape[1], xv.shape[1]
    blocks = deep // wide
    ready(x, du, g, dz, xv, duv, gv, dzv)

    def write(c, row, value):
        value = value.astype(BF)
        for d in range(row // size, (row + value.shape[0] - 1) // size + 1):
            lo, hi = max(row, d * size), min(row + value.shape[0], (d + 1) * size)
            out[d, c, lo - d * size : hi - d * size, :] = value[lo - row : hi - row]

    for c in range(Z):
        for j in range(blocks):
            cols = slice((c * blocks + j) * wide, (c * blocks + j + 1) * wide)
            write(c, j * deep, dot_tn(x[...], du[:, cols]))
            own, cols = slice(c * deep, (c + 1) * deep), slice(j * wide, (j + 1) * wide)
            write(c, (blocks + j) * deep, dot_tn(g[:, own], dz[:, cols]))
        row = 2 * blocks * deep
        cols = slice(c * wide, (c + 1) * wide)
        for n in range(tall // wide):
            rows = slice(n * wide, (n + 1) * wide)
            write(c, row + n * wide, dot_tn(xv[:, rows], duv[:, cols]))
            write(c, row + tall + n * wide, dot_tn(gv[:, cols], dzv[:, rows]))
        out.send_part((slice(None), c), c == Z - 1)


def cut_static(*refs):
    pos, whole, out = split(refs, 0, 0, 4)
    for k in range(Z):
        out[k][...] = whole[-k % Z]


def grads_text_ffn(*refs):
    pos, x, du, g, dz, up, down = refs
    matrix_whole(up, x, du)
    matrix_whole(down, g, dz)


def grads_attention(*refs):
    pos, xt, dqt, xv, dqv, ot, dzt, ov, dzv, tq, vq, to, vo = refs
    for i in range(3):
        matrix_whole(tq.at[i], xt, dqt.at[i])
        matrix_whole(vq.at[i], xv, dqv.at[i])
    matrix_whole(to, ot, dzt)
    matrix_whole(vo, ov, dzv)


def core_sum(*refs):
    pos, keep, recv, out = split(refs, 0, 0, 0, 4)
    size = out[0].shape[0]
    for k in range(Z):
        rows = slice(-k % Z * size, (-k % Z + 1) * size)
        out[k][...] = (keep[rows, :].astype(F32) + recv[rows, :].astype(F32)).astype(BF)


def tensor_sum_stats(*refs):
    pos, s, text, image, end, out, rows_out = split(refs, 0, 4, 4, 4, 4, 0, 0)
    rows_out[...] = jnp.zeros(rows_out.shape, BF)
    size, rows = s[0].shape[0], 16
    out[pos[3], 0:size, :] = total(s, slice(None)).astype(BF)
    out[1 - pos[3], 0:size, :] = jnp.zeros(s[0].shape, BF)
    last = [slice(x[0].shape[0] - rows, x[0].shape[0] - rows // 2) for x in (text, image)]
    wide, tall = out.shape[2], image[0].shape[1]
    narrow = total(text, last[0])
    narrow = jnp.concatenate(
        [narrow, jnp.zeros((narrow.shape[0], tall - narrow.shape[1]), F32)], axis=1
    )
    stats = jnp.concatenate([narrow, total(image, last[1])], axis=0).astype(BF)
    for j in range(Z):
        at = size + (j % 2) * rows
        out[j // 2, at : at + rows, :] = stats[:, j * wide : (j + 1) * wide]
    send(out)
    rows_out[part(pos[4], end[0].shape[0]), :] = total(end, slice(None)).astype(BF)


def finish(*refs):
    count = 10
    stq, ins, both, end = refs[1], refs[2 : 1 + count], refs[1 + count], refs[2 + count]
    stqo, outs = refs[3 + count], refs[4 + count : 3 + 2 * count]
    up, down, tg, ts, vg, vs = refs[3 + 2 * count : 9 + 2 * count]
    end_refs = refs[9 + 2 * count :]
    for source, out in zip(ins, outs):
        out[...] = source[...].astype(F32)
        send(out)
    for j in range(3):
        stqo[j] = stq[j].astype(F32).T
    send(stqo)
    half, wide = up.shape[0] // 2, up.shape[1]
    for h in range(2):
        up[h * half : (h + 1) * half, :] = both[h, 0:half, :].astype(F32)
        for j in range(half // wide):
            at, to = half + j * wide, h * half + j * wide
            down[:, to : to + wide] = both[h, at : at + wide, :].astype(F32)
    send(up, down)
    blocks = [both[j // 2, 2 * half + j % 2 * 16 : 2 * half + j % 2 * 16 + 16, :] for j in range(Z)]
    stats = jnp.concatenate(blocks, axis=1).astype(F32)
    for i in range(4):
        tg[i : i + 1, :] = stats[2 * i : 2 * i + 1, 0 : tg.shape[1]]
        ts[i : i + 1, :] = stats[2 * i + 1 : 2 * i + 2, 0 : tg.shape[1]]
        vg[i : i + 1, :] = stats[8 + 2 * i : 9 + 2 * i, :]
        vs[i : i + 1, :] = stats[9 + 2 * i : 10 + 2 * i, :]
    up, down, image_up, image_down = end_refs
    deep, tall = up.shape[0], image_up.shape[0]
    blocks = deep // wide
    for j in range(blocks):
        cols = slice(j * wide, (j + 1) * wide)
        up[:, cols] = end[j * deep : (j + 1) * deep, :].astype(F32)
        down[:, cols] = end[(blocks + j) * deep : (blocks + j + 1) * deep, :].astype(F32)
    send(up, down)
    at = 2 * blocks * deep
    image_up[...] = end[at : at + tall, :].astype(F32)
    for j in range(tall // wide):
        row = at + tall + j * wide
        image_down[:, j * wide : (j + 1) * wide] = end[row : row + wide, :].astype(F32)


def placed(array):
    if any(array is one for one in arrived):
        return array
    return pltpu.with_memory_space_constraint(array, pltpu.HBM)


latest = []


def follow(results):
    latest[:] = [min(results, key=lambda x: x.size)]


def run(name, body, outs, args, scratch=(), after=()):
    after = latest + list(after)
    flat = [None]
    for arg in args[1:]:
        flat.extend(arg if isinstance(arg, (list, tuple)) else [arg])
    shapes, groups = [], []
    for shape, dtype, count in outs:
        groups.append(count)
        shapes.extend([pltpu.HBM(shape, dtype)] * max(count, 1))
    scratch = [jax.ShapeDtypeStruct(shape, dtype) for shape, dtype in scratch]
    held = sum(
        math.prod(x.shape) * jnp.dtype(x.dtype).itemsize for x in flat[1:] + shapes + scratch
    )
    n_in, n_out = len(flat) - 1, len(shapes)
    first = 1 + n_in + len(after)
    stage = first + n_out
    indices = [x.index if isinstance(x, View) else None for x in flat[1:]]

    def staged_body(*refs):
        refs = (Scalars(*refs[:3]), *refs[3:])
        sems = refs[-1]
        moves = [
            pltpu.make_async_copy(ref if index is None else ref.at[index], place, sems.at[i])
            for i, (ref, index, place) in enumerate(zip(refs[1 : 1 + n_in], indices, refs[stage:]))
        ]
        for move in moves:
            move.start()
        operands = [Arriving(ref, move) for ref, move in zip(refs[stage:], moves)]
        results = [
            Leaving(ref, target, sems.at[n_in + i])
            for i, (ref, target) in enumerate(zip(refs[stage + n_in :], refs[first:stage]))
        ]
        body(refs[0], *operands, *results, *refs[stage + n_in + n_out : -1])
        for operand in operands:
            operand.wait()
        for result in results:
            result.send()
        for result in results:
            result.copy.wait()

    hbm, free = pl.BlockSpec(memory_space=pltpu.HBM), pl.BlockSpec(memory_space=pl.ANY)
    arrays = [x.array if isinstance(x, View) else x for x in flat[1:]]
    results = pl.pallas_call(
        staged_body,
        out_shape=shapes,
        in_specs=[pl.BlockSpec(memory_space=pltpu.SMEM)] * 3 + [free] * (first - 1),
        out_specs=[hbm] * n_out,
        scratch_shapes=[pltpu.VMEM(x.shape, x.dtype) for x in flat[1:] + shapes + scratch]
        + [pltpu.SemaphoreType.DMA((n_in + n_out,))],
        compiler_params=pltpu.CompilerParams(
            vmem_limit_bytes=min(60 << 20, max(16 << 20, held + (8 << 20)))
        ),
        cost_estimate=COST,
        name=name,
    )(
        *args[0], *[placed(x) for x in arrays + after])
    follow(results)
    return split(list(results), *groups)


def cut_weights(scalars, groups, n_dp, wide):
    flat = [matrix for group in groups for matrix in group]
    sizes = [sum(math.prod(m.shape) for m in group) // wide // n_dp for group in groups]
    step = 16

    def body(pos_ref, *refs):
        out, sem = refs[-2:]
        sources, base = list(refs[: len(flat)]), 0
        for group, size in zip(groups, sizes):
            steps, offset = size // step, 0
            begin = pos_ref[4] * steps
            for matrix in group:
                source = sources.pop(0)
                rows, width = matrix.shape
                for j in range(width // wide):
                    first = jnp.clip(offset // step - begin, 0, steps)
                    last = jnp.clip((offset + rows) // step - begin, 0, steps)

                    def move(i, carry, source=source, offset=offset, j=j, base=base, begin=begin):
                        row = pl.multiple_of((begin + i) * step - offset, step)
                        to = pl.multiple_of(base + i * step, step)
                        pltpu.make_async_copy(
                            source.at[pl.ds(row, step), pl.ds(j * wide, wide)],
                            out.at[pl.ds(to, step), :],
                            sem,
                        ).start()
                        return carry

                    lax.fori_loop(first, last, move, 0)
                    offset += rows
            base += size
        pltpu.make_async_copy(out, out, sem).wait()

    hbm, free = pl.BlockSpec(memory_space=pltpu.HBM), pl.BlockSpec(memory_space=pl.ANY)
    after = list(latest)
    result = pl.pallas_call(
        body,
        out_shape=pltpu.HBM((sum(sizes), wide), BF),
        in_specs=[pl.BlockSpec(memory_space=pltpu.SMEM)] + [free] * (len(flat) + len(after)),
        out_specs=hbm,
        scratch_shapes=[pltpu.SemaphoreType.DMA(())],
        cost_estimate=COST,
        name="cut_weights",
    )(scalars[0], *[placed(x) for x in flat + after])
    follow([result])
    return result


arrived = []


def shift(values, k):
    arrived.append(lax.ppermute(values, "tensor", [(i, (i + k) % Z) for i in range(Z)]))
    return arrived[-1]


def spread(own):
    return [own] + [shift(own, k) for k in (1, 2, 3)]


def swap(chunks):
    return [chunks[0]] + [shift(chunks[k], k) for k in (1, 2, 3)]


def along(values, dy, dx, dc):
    pairs = []
    for y in range(4):
        for x in range(4):
            for c in range(2):
                to = (((y + dy) % 4) * 4 + (x + dx) % 4) * 2 + (c + dc) % 2
                pairs.append(((y * 4 + x) * 2 + c, to))
    arrived.append(lax.ppermute(values, "dp", pairs))
    return arrived[-1]


def pad_rows(values, n):
    micro, samples, rows, width = values.shape
    flat = values.reshape(micro, samples * rows, width)
    flat = jnp.pad(flat, ((0, 0), (0, n - samples * rows), (0, 0)))
    return flat.reshape(micro * n, width)


def unpad_rows(values, shape, n):
    micro, samples, rows, width = shape
    return values.reshape(micro, n, width)[:, : samples * rows].reshape(shape)


def joined(text, image, chunks):
    wide, width = image.shape[1], text.shape[1]
    t = text.reshape(chunks, text.shape[0] // chunks, width)
    main = packed_rows(t.shape[1], width, wide)
    rest = t[:, main:].reshape(chunks, t.shape[1] - main, width // (wide - width), wide - width)
    rest = rest.transpose(0, 2, 1, 3).reshape(chunks, main, wide - width)
    t = jnp.concatenate([t[:, :main], rest], axis=2)
    v = image.reshape(chunks, image.shape[0] // chunks, wide)
    return jnp.concatenate([v, t], axis=1)


def parted(both, text_rows, width):
    wide = both.shape[2]
    main = packed_rows(text_rows, width, wide)
    image, t = both[:, : both.shape[1] - main], both[:, both.shape[1] - main :]
    parts = width // (wide - width)
    rest = t[:, :, width:].reshape(t.shape[0], parts, main // parts, wide - width)
    rest = rest.transpose(0, 2, 1, 3).reshape(t.shape[0], main // parts, width)
    text = jnp.concatenate([t[:, :, :width], rest], axis=1)
    return text.reshape(-1, width), image.reshape(-1, wide)


def in_order(chunks, rank):
    ring = jnp.stack([chunks[0], chunks[3], chunks[2], chunks[1]] * 2)
    return lax.dynamic_slice_in_dim(ring, (Z - rank) & 3, Z, 0)


def shards(
    text_in, image_in, caption_len, region_count, text_cot, image_cot,
    co_text_qkv, co_image_qkv, co_text_out, co_image_out,
    co_text_up, co_text_down, co_image_up, co_image_down,
    self_text_qkv, self_image_qkv, self_text_out, self_image_out,
    text_up, text_down, image_up, image_down,
    text_gains, text_shifts, image_gains, image_shifts,
):
    arrived.clear()
    latest.clear()
    rank = lax.axis_index("tensor")
    place = lax.axis_index("dp")
    n_dp = lax.axis_size("dp")
    pos = jnp.stack([rank, (place // 2) % 4, place // 8, place % 2, place]).astype(jnp.int32)
    scalars = [pos, caption_len, region_count]
    micro, samples, text, wt = text_in.shape
    regions, wv = image_in.shape[2:]
    dt, dv = wt * Z, wv * Z
    nt = -(-samples * text // 64) * 64
    nv = -(-samples * regions // 64) * 64
    rt, rv = micro * nt, micro * nv
    ct, cv = rt // Z, rv // Z
    co_w = co_text_qkv.shape[2]
    st_w = self_text_qkv.shape[2]
    si_w = self_image_qkv.shape[2]
    ft = co_text_up.shape[1]
    shard = ((cv + packed_rows(ct, wt, wv), wv), BF)
    whole = ((rv + packed_rows(rt, wt, wv), wv), BF)

    groups = [(co_image_up, co_image_down), (text_up, text_down, image_up, image_down)]
    cuts = cut_weights(scalars, groups, n_dp, wv)
    shards_in = joined(pad_rows(text_in, nt), pad_rows(image_in, nv), 1)[0]
    n_cut = 2 * dv // n_dp
    pieces = spread(cuts)
    w_mid = lax.all_gather(
        jnp.stack([piece[:n_cut] for piece in pieces]), "dp", axis=1, tiled=True
    )
    w_end = lax.all_gather(
        jnp.stack([piece[n_cut:] for piece in pieces]), "dp", axis=1, tiled=True
    )
    both = spread(shards_in)
    co_dims = (samples, text, regions, nt, nv)
    text_dims = (samples, text, nt, TEXT_HEAD, LENGTHS)
    image_dims = (samples, regions, nv, IMAGE_HEAD, LENGTHS + micro * samples)
    xt0, xv0, bt, bv, qt0, qv0, ot0, ov0, st, sv = run(
        "co_fwd", functools.partial(co_fwd, co_dims),
        [((rt, dt), BF, 0), ((rv, dv), BF, 0), ((ct, dt), BF, 0), ((cv, dv), BF, 0),
         ((3, rt, co_w), BF, 0), ((3, rv, co_w), BF, 0), ((rt, co_w), BF, 0),
         ((rv, co_w), BF, 0), ((ct, dt), BF, Z), ((cv, dv), BF, Z)],
        [scalars, both, co_text_qkv, co_image_qkv, co_text_out, co_image_out],
    )
    n_text = 2 * dt * (ft // wv)
    w_text = View(w_end, (slice(None), pl.ds(0, n_text)), (Z, n_text, wv))
    w_image = View(w_end, (slice(None), pl.ds(n_text, 2 * dv)), (Z, 2 * dv, wv))
    norm_t = [((ct, dt), F32, 0), ((ct, dt), F32, 0), ((ct, dt), BF, 0)]
    ffn_t = [((rt, dt), BF, 0), ((rt, ft), F32, 0), ((rt, ft), BF, 0), ((ct, dt), BF, Z)]
    zt0, at, atb = run(
        "text_norm0", functools.partial(text_norm, 0), norm_t,
        [scalars, swap(st), bt, text_gains, text_shifts],
    )
    xt1, ut1, gt1, st = run(
        "text_ffn1", text_ffn, ffn_t, [scalars, spread(atb), co_text_up, co_text_down]
    )
    zv0, av, uv1, gv1, zv1, bv, bvb = run(
        "image_mid", functools.partial(image_mid, 0),
        [((cv, dv), F32, 0), ((cv, dv), BF, 0), ((cv, dv), F32, 0), ((cv, dv), BF, 0),
         ((cv, dv), F32, 0), ((cv, dv), F32, 0), ((cv, dv), BF, 0)],
        [scalars, swap(sv), bv, w_mid, image_gains, image_shifts],
        [((cv, dv), F32)],
    )
    zt1, bt, btb = run(
        "text_norm1", functools.partial(text_norm, 1), norm_t,
        [scalars, swap(st), at, text_gains, text_shifts],
    )
    cot = joined(pad_rows(text_cot, nt), pad_rows(image_cot, nv), Z)
    (cot,) = run("cut", cut, [(*shard, Z)], [scalars, cot])
    cot = swap(cot)
    xt2, qt2, ot2, st = run(
        "text_self", functools.partial(self_fwd, text_dims),
        [((rt, dt), BF, 0), ((3, rt, st_w), BF, 0), ((rt, st_w), BF, 0), ((ct, dt), BF, Z)],
        [scalars, spread(btb), self_text_qkv, self_text_out],
    )
    xv2, qv2, ov2, sv = run(
        "image_self", functools.partial(self_fwd, image_dims),
        [((rv, dv), BF, 0), ((3, rv, si_w), BF, 0), ((rv, si_w), BF, 0), ((cv, dv), BF, Z)],
        [scalars, spread(bvb), self_image_qkv, self_image_out],
    )
    hidden = Z * ft
    out_t, at3, gt3, dt3, dut3, gt, gtb, stat_t1 = run(
        "text_turn", functools.partial(text_turn, 2),
        [((ct, wt), BF, Z), ((ct, dt), BF, 0), ((ct, hidden), BF, 0), ((ct, dt), BF, 0),
         ((ct, hidden), BF, 0), ((ct, dt), F32, 0), ((ct, dt), BF, 0), ((4, dt), F32, 0)],
        [scalars, swap(st), bt, cot, w_text, text_gains, text_shifts],
        [((ct, hidden), F32), ((ct, dt), F32), ((ct, dt), F32)],
    )
    out_v, av3, gv3, dv3, duv3, gv, gvb, stat_v1 = run(
        "image_turn", functools.partial(image_turn, 2),
        [((cv, wv), BF, Z), ((cv, dv), BF, 0), ((cv, dv), BF, 0), ((cv, dv), BF, 0),
         ((cv, dv), BF, 0), ((cv, dv), F32, 0), ((cv, dv), BF, 0), ((4, dv), F32, 0)],
        [scalars, swap(sv), bv, cot, w_image, image_gains, image_shifts],
        [((cv, dv), F32)] * 8,
    )
    back_ffn = [((rt, dt), BF, 0), ((rt, ft), BF, 0), ((ct, dt), BF, Z)]
    stat_shape = ((2, dt), F32, 0)
    def image_ffn_grads(name, *saved):
        keep, give = run(
            "grads_" + name, grads_image_ffn, [((Z * dv, wv), BF, 0)] * 2, [scalars, *saved]
        )
        return keep, along(give, 0, 0, 1)
    def core_summed(name, halves, after):
        (chunks,) = run(
            "core_sum_" + name, core_sum, [((dv, wv), BF, Z)], [scalars, *halves], after=after
        )
        return chunks
    (end,) = run(
        "grads_end", grads_end, [((n_dp, Z, (n_text + 2 * dv) // n_dp, wv), BF, 0)],
        [scalars, at3, dut3, gt3, dt3, av3, duv3, gv3, dv3],
    )
    end_cut = lax.psum_scatter(end, "dp", scatter_dimension=0, tiled=False)
    dt2, dqt2, st = run(
        "text_self_back", functools.partial(self_bwd, text_dims),
        [((rt, dt), BF, 0), ((3, rt, st_w), BF, 0), ((ct, dt), BF, Z)],
        [scalars, spread(gtb), qt2, self_text_qkv, self_text_out],
        [((rt, st_w), BF)],
    )
    dv2, dqv2, sv = run(
        "image_self_back", functools.partial(self_bwd, image_dims),
        [((rv, dv), BF, 0), ((3, rv, si_w), BF, 0), ((cv, dv), BF, Z)],
        [scalars, spread(gvb), qv2, self_image_qkv, self_image_out],
        [((rv, si_w), BF)],
    )
    gt, gtb, stat_t2 = run(
        "text_norm1_back", functools.partial(text_norm_back, 1),
        [((ct, dt), F32, 0), ((ct, dt), BF, 0), stat_shape],
        [scalars, swap(st), gt, zt1, text_gains],
    )
    st_q, sv_q, st_o, sv_o = run(
        "grads_self", grads_attention,
        [((3, dt, st_w), BF, 0), ((3, dv, si_w), BF, 0), ((st_w, dt), BF, 0), ((si_w, dv), BF, 0)],
        [scalars, xt2, dqt2, xv2, dqv2, ot2, dt2, ov2, dv2],
    )
    dt1, dut1, st = run(
        "text_ffn1_back", text_ffn_back, back_ffn,
        [scalars, spread(gtb), co_text_up, co_text_down, ut1],
    )
    dv1, duv1, gv, gvb, _ = run(
        "image_mid_back", functools.partial(image_mid_back, 0),
        [((cv, dv), BF, 0), ((cv, dv), BF, 0), ((cv, dv), F32, 0), ((cv + 16, dv), BF, 0),
         ((4, dv), F32, 0)],
        [scalars, swap(sv), gv, zv1, zv0, uv1, w_mid, image_gains, stat_v1],
        [((cv, dv), F32)] * 2,
    )
    mid_f = image_ffn_grads("mid", av, duv1, gv1, dv1)
    gt, gtb, _ = run(
        "text_norm0_back", functools.partial(text_norm_back_stats, 0),
        [((ct, dt), F32, 0), ((ct + 16, dt), BF, 0), stat_shape],
        [scalars, swap(st), gt, zt0, text_gains, stat_t2, stat_t1],
    )
    t1_up, t1_down = run(
        "grads_ffn1", grads_text_ffn, [((dt, ft), BF, 0), ((ft, dt), BF, 0)],
        [scalars, xt1, dut1, gt1, dt1],
    )
    zt, zv = spread(gtb), spread(gvb)
    mid_f = core_summed("mid", mid_f, zt[1:] + zv[1:])
    (end_cut,) = run(
        "cut_end", cut_static, [(end_cut.shape[1:], BF, Z)], [scalars, end_cut]
    )
    end_cut = swap(end_cut)
    dqt0, dqv0, tq, vq, to, vo = run(
        "co_back", functools.partial(co_bwd, co_dims),
        [((3, rt, co_w), BF, 0), ((3, rv, co_w), BF, 0),
         ((3, dt, co_w), BF, 0), ((3, dv, co_w), BF, 0), ((co_w, dt), BF, 0), ((co_w, dv), BF, 0)],
        [scalars, zt, zv, qt0, qv0, co_text_out, co_image_out, xt0, xv0, ot0, ov0],
        [((rt, dt), BF), ((rv, dv), BF), ((rt, co_w), BF), ((rv, co_w), BF)],
    )
    (s,) = run(
        "co_back_in", co_bwd_in, [(*whole, Z)],
        [scalars, dqt0, dqv0, co_text_qkv, co_image_qkv, gt, gv],
        [((rt, wt), F32), ((rv, wv), F32)],
    )
    mid_f, end = run(
        "last_sums", tensor_sum_stats,
        [((2, dv + 32, wv), BF, 0), ((n_text + 2 * dv, wv), BF, 0)],
        [scalars, swap(mid_f), zt, zv, end_cut],
    )
    late = lax.psum((st_q, t1_up, t1_down, sv_q, st_o, sv_o, tq, vq, to, vo, mid_f, end), "dp")
    s = swap(s)
    out_t, out_v = swap(out_t), swap(out_v)
    ffn_out = [((dt, ft), F32, 0), ((ft, dt), F32, 0)]
    image_out_shapes = [((dv, wv), F32, 0), ((wv, dv), F32, 0)]
    (st_q, t1_up, t1_down, sv_q, st_o, sv_o, tq, vq, to, vo, mid_up, mid_down, tg, ts, vg, vs,
     t_up, t_down, end_up, end_down) = run(
        "finish", finish,
        [((3, st_w, dt), F32, 0)] + ffn_out
        + [((3, dv, si_w), F32, 0), ((st_w, dt), F32, 0), ((si_w, dv), F32, 0),
           ((3, dt, co_w), F32, 0), ((3, dv, co_w), F32, 0),
           ((co_w, dt), F32, 0), ((co_w, dv), F32, 0)] + image_out_shapes
        + [((4, dt), F32, 0)] * 2 + [((4, dv), F32, 0)] * 2 + ffn_out + image_out_shapes,
        [scalars, *late],
    )
    st_q = st_q.transpose(0, 2, 1)

    text_out = in_order(out_t, rank).reshape(rt, wt)
    image_out = in_order(out_v, rank).reshape(rv, wv)
    text_grad, image_grad = parted(sum(member.astype(F32) for member in s)[None], rt, wt)
    return (
        unpad_rows(text_out, text_in.shape, nt).astype(F32),
        unpad_rows(image_out, image_in.shape, nv).astype(F32),
        unpad_rows(text_grad, text_in.shape, nt),
        unpad_rows(image_grad, image_in.shape, nv),
        tq, vq, to, vo, t1_up, t1_down, mid_up, mid_down,
        st_q, sv_q, st_o, sv_o, t_up, t_down, end_up, end_down,
        tg, ts, vg, vs,
    )


def solution(mesh):
    stream = P(None, "dp", None, "tensor")
    lengths = P(None, "dp")
    stacked = P(None, None, "tensor")
    rows = P("tensor", None)
    cols = P(None, "tensor")
    weights = (
        stacked, stacked, rows, rows, cols, rows, cols, rows,
        stacked, stacked, rows, rows, cols, rows, cols, rows,
        P(), P(), P(), P(),
    )
    in_specs = (stream, stream, lengths, lengths, stream, stream) + weights
    out_specs = (stream,) * 4 + weights
    return jax.shard_map(shards, mesh=mesh, in_specs=in_specs, out_specs=out_specs, check_vma=False)
```

```python
import functools
import math

import jax
import jax.numpy as jnp
from jax import lax
from jax.experimental import pallas as pl
from jax.experimental.pallas import tpu as pltpu
from jax.sharding import PartitionSpec as P

CO_HEAD = 128
TEXT_HEAD = 64
IMAGE_HEAD = 128
EPS = 1e-05
FILL = -1000000000.0
ROOT_HALF = 0.7071067811865476
INV_ROOT_TWO_PI = 0.3989422804014327
F32 = jnp.float32
BF = jnp.bfloat16
Z = 4
COST = pl.CostEstimate(flops=20_000_000_000, bytes_accessed=1000, transcendentals=0)
LENGTHS = 5


def dot(a, b):
    return lax.dot_general(a, b, (((1,), (0,)), ((), ())), preferred_element_type=F32)


def dot_nt(a, b):
    return lax.dot_general(a, b, (((1,), (1,)), ((), ())), preferred_element_type=F32)


def dot_tn(a, b):
    return lax.dot_general(a, b, (((0,), (0,)), ((), ())), preferred_element_type=F32)


def part(index, size):
    return pl.ds(pl.multiple_of(index * size, size), size)


def row_ids(count, step, samples):
    place = lax.broadcasted_iota(jnp.int32, (count, 1), 0)
    ids = jnp.zeros((count, 1), jnp.int32)
    for s in range(1, samples):
        ids = ids + (place >= s * step).astype(jnp.int32)
    return ids


def key_ids(pos, first, m, step, samples, count):
    place = lax.broadcasted_iota(jnp.int32, (1, count), 1)
    ids = jnp.full((1, count), -1, jnp.int32)
    for s in range(samples):
        live = pos[first + m * samples + s]
        ids = jnp.where((place >= s * step) & (place < s * step + live), s, ids)
    return ids


def probabilities(q, k, same, scale):
    s = jnp.where(same, dot_nt(q, k) * scale, FILL)
    e = jnp.exp(s - jnp.max(s, axis=-1, keepdims=True))
    return e / jnp.sum(e, axis=-1, keepdims=True)


def head_fwd(q, k, v, same, scale):
    return dot(probabilities(q, k, same, scale).astype(BF), v).astype(BF)


def head_bwd(q, k, v, same, scale, do):
    p = probabilities(q, k, same, scale)
    dv = dot_tn(p.astype(BF), do)
    dp = dot_nt(do, v)
    ds = (p * (dp - jnp.sum(dp * p, axis=-1, keepdims=True))).astype(BF)
    dq = dot(ds, k) * scale
    dk = dot_tn(ds, q) * scale
    return dq.astype(BF), dk.astype(BF), dv.astype(BF)


def gelu(u):
    return u * (1.0 + lax.erf(u * ROOT_HALF)) * 0.5


def gelu_slope(u):
    return (1.0 + lax.erf(u * ROOT_HALF)) * 0.5 + u * jnp.exp(u * u * -0.5) * INV_ROOT_TWO_PI


def normalise(z):
    centre = z - jnp.mean(z, axis=-1, keepdims=True)
    rstd = lax.rsqrt(jnp.mean(centre * centre, axis=-1, keepdims=True) + EPS)
    return centre * rstd, rstd


def norm_back(z, gain, dy):
    xhat, rstd = normalise(z)
    dxh = dy * gain
    dz = rstd * (
        dxh
        - jnp.mean(dxh, axis=-1, keepdims=True)
        - xhat * jnp.mean(dxh * xhat, axis=-1, keepdims=True)
    )
    return dz, jnp.sum(dy * xhat, axis=0, keepdims=True), jnp.sum(dy, axis=0, keepdims=True)


class Arriving:
    in_loop = False

    def __init__(self, ref, copy):
        self.ref, self.copy = ref, copy
        self.shape, self.dtype = ref.shape, ref.dtype

    def wait(self):
        if self.copy is not None:
            assert not Arriving.in_loop
            self.copy.wait()
            self.copy = None

    def __getitem__(self, index):
        self.wait()
        return self.ref[index]

    @property
    def at(self):
        self.wait()
        return self.ref.at


class Scalars:
    def __init__(self, places, *lengths):
        self.places, self.lengths = places, lengths

    def __getitem__(self, i):
        if i < LENGTHS:
            return self.places[i]
        micro, samples = self.lengths[0].shape
        which, at = divmod(i - LENGTHS, micro * samples)
        return self.lengths[which][at // samples, at % samples]


class View:
    def __init__(self, array, index, shape):
        self.array, self.index, self.shape, self.dtype = array, index, shape, array.dtype


class Leaving:
    def __init__(self, ref, target, sem):
        self.ref, self.target, self.sem, self.sent = ref, target, sem, False
        self.copy = pltpu.make_async_copy(ref, target, sem)
        self.shape, self.dtype, self.at = ref.shape, ref.dtype, ref.at

    def send(self):
        if not self.sent:
            self.copy.start()
            self.sent = True

    def send_part(self, index, last):
        pltpu.make_async_copy(self.ref.at[index], self.target.at[index], self.sem).start()
        self.sent = last

    def __getitem__(self, index):
        return self.ref[index]

    def __setitem__(self, index, value):
        assert not self.sent
        self.ref[index] = value


def send(*refs):
    for ref in refs:
        for one in ref if isinstance(ref, list) else [ref]:
            one.send()


def ready(*refs):
    for ref in refs:
        for one in ref if isinstance(ref, list) else [ref]:
            one.wait()


def tiles(count, tile, body):
    def step(i, carry):
        body(part(i, tile))
        return carry

    Arriving.in_loop = True
    lax.fori_loop(0, count // tile, step, 0)
    Arriving.in_loop = False


def total(refs, rows):
    acc = refs[0][rows, :].astype(F32)
    for ref in refs[1:]:
        acc = acc + ref[rows, :].astype(F32)
    return acc


def lanes_in_order(values, r, width):
    near = [values[0], values[3], values[2], values[1]]
    joined = jnp.concatenate([value.astype(F32) for value in near], axis=1)
    return pltpu.roll(joined, r * width, 1)


def lanes_from_own(values, r, width):
    return pltpu.roll(values, ((Z - r) & 3) * width, 1)


def rows_in_order(full, refs, r):
    size = full.shape[0] // Z
    for k, ref in enumerate(refs):
        full[part((r - k) & 3, size), :] = ref[0:size, :]


def packed_rows(rows, width, wide):
    return rows * width // wide if width < wide else rows


def put_text(ref, at, value):
    rows, width = value.shape
    wide = ref.shape[1]
    main = packed_rows(rows, width, wide)
    rest = rows - main
    ref[at : at + main, 0:width] = value[0:main]
    for j in range(width // (wide - width)):
        cols = slice(j * (wide - width), (j + 1) * (wide - width))
        ref[at + j * rest : at + (j + 1) * rest, width:wide] = value[main:rows, cols]


def get_text(ref, at, rows, width):
    wide = ref.shape[1]
    if width == wide:
        return ref[at : at + rows, :]
    main = packed_rows(rows, width, wide)
    rest = rows - main
    tail = [
        ref[at + j * rest : at + (j + 1) * rest, width:wide]
        for j in range(width // (wide - width))
    ]
    return jnp.concatenate([ref[at : at + main, 0:width], jnp.concatenate(tail, axis=1)], axis=0)


def split(refs, *counts):
    found, at = [], 0
    for count in counts:
        found.append(refs[at] if count == 0 else list(refs[at : at + count]))
        at += max(count, 1)
    assert at == len(refs)
    return found


def co_fwd(dims, *refs):
    rank, both, wt, wv, pt, pv, xt, xv, bt, bv, qt, qv, ot, ov, st, sv = split(
        refs, 0, 4, 0, 0, 0, 0, 0, 0, 0, 0, 0, 0, 0, 0, 4, 4
    )
    samples, text, regions, nt, nv = dims
    r = rank[0]
    rows_t, rows_v = xt.shape[0], xv.shape[0]
    width_t, width_v = xt.shape[1] // Z, xv.shape[1] // Z
    ct, cv = bt.shape[0], bv.shape[0]
    tin = [get_text(ref, rows_v, rows_t, width_t) for ref in both]
    xt[...] = lanes_in_order(tin, r, width_t).astype(BF)
    for k, ref in enumerate(both):
        xv[:, part((r - k) & 3, width_v)] = ref[0:rows_v, :]
    bt[...] = xt[part(r, ct), :]
    bv[...] = xv[part(r, cv), :]
    send(xt, xv, bt, bv)
    for i in range(3):
        qt[i] = dot(xt[...], wt[i]).astype(BF)

    def project(rows):
        for i in range(3):
            qv[i, rows, :] = dot(xv[rows, :], wv[i]).astype(BF)

    ready(wv)
    tiles(xv.shape[0], cv, project)
    send(qt, qv)
    scale = CO_HEAD ** (-0.5)
    rid_t, rid_v = row_ids(nt, text, samples), row_ids(nv, regions, samples)
    for m in range(2):
        rt, rv = slice(m * nt, (m + 1) * nt), slice(m * nv, (m + 1) * nv)
        same_tv = rid_t == key_ids(rank, LENGTHS + 2 * samples, m, regions, samples, nv)
        same_vt = rid_v == key_ids(rank, LENGTHS, m, text, samples, nt)
        for h in range(qt.shape[2] // CO_HEAD):
            c = slice(h * CO_HEAD, (h + 1) * CO_HEAD)
            ot[rt, c] = head_fwd(qt[0, rt, c], qv[1, rv, c], qv[2, rv, c], same_tv, scale)
            ov[rv, c] = head_fwd(qv[0, rv, c], qt[1, rt, c], qt[2, rt, c], same_vt, scale)
    for k in range(Z):
        c = (r + k) & 3
        st[k][...] = dot(ot[part(c, ct), :], pt[...]).astype(BF)
        sv[k][...] = dot(ov[part(c, cv), :], pv[...]).astype(BF)
        send(st[k], sv[k])


def co_bwd(dims, *refs):
    (rank, dt, dv, qt, qv, pt, pv, xt, xv, ot, ov,
     dqt, dqv, tq, vq, to, vo, zt, zv, dot_s, dov_s) = split(
        refs, 0, 4, 4, *([0] * 18)
    )
    samples, text, regions, nt, nv = dims
    r = rank[0]
    cv = zv.shape[0] // Z
    rows_in_order(zt, dt, r)
    rows_in_order(zv, dv, r)
    dot_s[...] = dot_nt(zt[...], pt[...]).astype(BF)

    def back_out(rows):
        dov_s[rows, :] = dot_nt(zv[rows, :], pv[...]).astype(BF)

    ready(pv)
    tiles(zv.shape[0], cv, back_out)
    scale = CO_HEAD ** (-0.5)
    rid_t, rid_v = row_ids(nt, text, samples), row_ids(nv, regions, samples)
    for m in range(2):
        rt, rv = slice(m * nt, (m + 1) * nt), slice(m * nv, (m + 1) * nv)
        same_tv = rid_t == key_ids(rank, LENGTHS + 2 * samples, m, regions, samples, nv)
        same_vt = rid_v == key_ids(rank, LENGTHS, m, text, samples, nt)
        for h in range(qt.shape[2] // CO_HEAD):
            c = slice(h * CO_HEAD, (h + 1) * CO_HEAD)
            a, b, d = head_bwd(
                qt[0, rt, c], qv[1, rv, c], qv[2, rv, c], same_tv, scale, dot_s[rt, c]
            )
            dqt[0, rt, c], dqv[1, rv, c], dqv[2, rv, c] = a, b, d
            a, b, d = head_bwd(
                qv[0, rv, c], qt[1, rt, c], qt[2, rt, c], same_vt, scale, dov_s[rv, c]
            )
            dqv[0, rv, c], dqt[1, rt, c], dqt[2, rt, c] = a, b, d
    send(dqt, dqv)
    for i in range(3):
        matrix_whole(tq.at[i], xt, dqt.at[i])
        matrix_whole(vq.at[i], xv, dqv.at[i])
    send(tq, vq)
    matrix_whole(to, ot, zt)
    matrix_whole(vo, ov, zv)


def co_bwd_in(*refs):
    rank, dqt, dqv, wt, wv, gt, gv, s, acc_t, acc_v = split(
        refs, 0, 0, 0, 0, 0, 0, 0, 4, 0, 0
    )
    r = rank[0]
    rows_v = acc_v.shape[0]
    ct, cv = gt.shape[0], gv.shape[0]
    width_t, width_v = acc_t.shape[1], acc_v.shape[1]
    own_t = lanes_from_own(gt[...], r, width_t)
    for k in range(Z):
        c = (r + k) & 3
        acc_t[...] = sum(dot_nt(dqt[i], wt[i, part(c, width_t), :]) for i in range(3))
        acc_t[part(r, ct), :] += own_t[:, k * width_t : (k + 1) * width_t]
        put_text(s[k], rows_v, acc_t[...].astype(BF))

        ready(wv, dqv)

        def back_in(rows):
            acc_v[rows, :] = sum(
                dot_nt(dqv[i, rows, :], wv[i, part(c, width_v), :]) for i in range(3)
            )

        tiles(acc_v.shape[0], cv, back_in)
        acc_v[part(r, cv), :] += gv[:, part(c, width_v)]
        s[k][0:rows_v, :] = acc_v[...].astype(BF)
        send(s[k])


def self_fwd(dims, *refs):
    rank, xin, w, po, x, q, o, s = split(refs, 0, 4, 0, 0, 0, 0, 0, 4)
    samples, step, n, head, first = dims
    r = rank[0]
    size = xin[0].shape[0]
    rows_in_order(x, xin, r)
    send(x)

    def project(rows):
        for i in range(3):
            q[i, rows, :] = dot(x[rows, :], w[i]).astype(BF)

    ready(w)
    tiles(x.shape[0], size, project)
    send(q)
    rid = row_ids(n, step, samples)
    for m in range(2):
        rm = slice(m * n, (m + 1) * n)
        same = rid == key_ids(rank, first, m, step, samples, n)
        for h in range(q.shape[2] // head):
            c = slice(h * head, (h + 1) * head)
            o[rm, c] = head_fwd(q[0, rm, c], q[1, rm, c], q[2, rm, c], same, head ** (-0.5))
    send(o)
    for k in range(Z):
        s[k][...] = dot(o[part((r + k) & 3, size), :], po[...]).astype(BF)
        send(s[k])


def self_bwd(dims, *refs):
    rank, din, q, w, po, z, dq, s, do = split(refs, 0, 4, 0, 0, 0, 0, 0, 4, 0)
    samples, step, n, head, first = dims
    r = rank[0]
    size = din[0].shape[0]
    rows_in_order(z, din, r)
    send(z)

    def back_out(rows):
        do[rows, :] = dot_nt(z[rows, :], po[...]).astype(BF)

    ready(po)
    tiles(z.shape[0], size, back_out)
    rid = row_ids(n, step, samples)
    for m in range(2):
        rm = slice(m * n, (m + 1) * n)
        same = rid == key_ids(rank, first, m, step, samples, n)
        for h in range(q.shape[2] // head):
            c = slice(h * head, (h + 1) * head)
            a, b, d = head_bwd(
                q[0, rm, c], q[1, rm, c], q[2, rm, c], same, head ** (-0.5), do[rm, c]
            )
            dq[0, rm, c], dq[1, rm, c], dq[2, rm, c] = a, b, d
    send(dq)
    for k in range(Z):
        rows = part((r + k) & 3, size)
        s[k][...] = sum(dot_nt(dq[i, rows, :], w[i]) for i in range(3)).astype(BF)
        send(s[k])


def text_total(base, s):
    return base[...].astype(F32) + total(s, slice(None))


def stat_rows(out, at, *stats):
    every = jnp.concatenate([ref[...] for ref in stats], axis=0)
    pad = jnp.zeros((out.shape[0] - at - every.shape[0], out.shape[1]), F32)
    out[at : out.shape[0], :] = jnp.concatenate([every, pad], axis=0).astype(BF)


def cut(*refs):
    pos, whole, out = split(refs, 0, 0, 4)
    for k in range(Z):
        out[k][...] = whole[(pos[0] + k) & 3]


def text_norm(position, *refs):
    rank, s, base, gains, shifts, z, y, out = split(refs, 0, 4, 0, 0, 0, 0, 0, 0)
    zz = text_total(base, s)
    z[...] = zz
    yy = normalise(zz)[0] * gains[position : position + 1, :] + shifts[position : position + 1, :]
    y[...] = yy
    out[...] = yy.astype(BF)


def text_norm_back(position, *refs):
    rank, s, base, z, gains, dz, out, stat = split(refs, 0, 4, 0, 0, 0, 0, 0, 0)
    d, dg, ds = norm_back(z[...], gains[position : position + 1, :], text_total(base, s))
    dz[...] = d
    out[...] = d.astype(BF)
    stat[0:1, :] = dg
    stat[1:2, :] = ds


def text_norm_back_stats(position, *refs):
    rank, s, base, z, gains, stat_1, stat_2, dz, out, stat = split(
        refs, 0, 4, 0, 0, 0, 0, 0, 0, 0, 0
    )
    d, dg, ds = norm_back(z[...], gains[position : position + 1, :], text_total(base, s))
    dz[...] = d
    rows = d.shape[0]
    out[0:rows, :] = d.astype(BF)
    stat[0:1, :] = dg
    stat[1:2, :] = ds
    stat_rows(out, rows, stat, stat_1, stat_2)


def text_turn(position, *refs):
    (rank, s, base, cot, w, gains, shifts, out, a, g, d1b, du, dz, send_on, stat,
     u, x, d1) = split(refs, 0, 4, 0, 4, 0, 0, 0, 4, 0, 0, 0, 0, 0, 0, 0, 0, 0, 0)
    r = rank[0]
    g0, b0 = gains[position : position + 1, :], shifts[position : position + 1, :]
    g1, b1 = gains[position + 1 : position + 2, :], shifts[position + 1 : position + 2, :]
    rows, width = base.shape[0], base.shape[1] // Z
    at = cot[0].shape[0] - packed_rows(rows, width, cot[0].shape[1])
    wide, deep = w.shape[2], base.shape[1]
    blocks = deep // wide
    z0 = text_total(base, s)
    x[...] = normalise(z0)[0] * g0 + b0
    a[...] = x[...].astype(BF)
    send(a)
    down = blocks * deep
    for c in range(Z):
        for j in range(blocks):
            cols = slice((c * blocks + j) * wide, (c * blocks + j + 1) * wide)
            uu = dot(a[...], w[c, j * deep : (j + 1) * deep, :])
            u[:, cols] = uu
            g[:, cols] = gelu(uu).astype(BF)
    send(g)
    for j in range(blocks):
        cols = slice(j * wide, (j + 1) * wide)
        acc = x[:, cols]
        for c in range(Z):
            own = slice(c * deep, (c + 1) * deep)
            acc = acc + dot(g[:, own], w[c, down + j * deep : down + (j + 1) * deep, :])
        x[:, cols] = acc
    z1 = x[...]
    y = lanes_from_own(normalise(z1)[0] * g1 + b1, r, width)
    for k in range(Z):
        out[k][...] = y[:, k * width : (k + 1) * width].astype(BF)
        send(out[k])
    dy = lanes_in_order([get_text(ref, at, rows, width) for ref in cot], r, width)
    d, dg, ds = norm_back(z1, g1, dy)
    d1[...] = d
    d1b[...] = d.astype(BF)
    send(d1b)
    stat[2:3, :] = dg
    stat[3:4, :] = ds
    for c in range(Z):
        own = slice(c * deep, (c + 1) * deep)
        back = sum(
            dot_nt(
                d1b[:, j * wide : (j + 1) * wide],
                w[c, down + j * deep : down + (j + 1) * deep, :],
            )
            for j in range(blocks)
        )
        du[:, own] = (back * gelu_slope(u[:, own])).astype(BF)
    send(du)
    back = d1[...]
    for c in range(Z):
        for j in range(blocks):
            cols = slice((c * blocks + j) * wide, (c * blocks + j + 1) * wide)
            back = back + dot_nt(du[:, cols], w[c, j * deep : (j + 1) * deep, :])
    d, dg, ds = norm_back(z0, g0, back)
    dz[...] = d
    send_on[...] = d.astype(BF)
    stat[0:1, :] = dg
    stat[1:2, :] = ds


def text_ffn(*refs):
    rank, xin, up, down, x, u, g, s = split(refs, 0, 4, 0, 0, 0, 0, 0, 4)
    r = rank[0]
    size = xin[0].shape[0]
    rows_in_order(x, xin, r)

    def hidden(rows):
        uu = dot(x[rows, :], up[...])
        u[rows, :] = uu
        g[rows, :] = gelu(uu).astype(BF)

    ready(up)
    tiles(x.shape[0], size, hidden)
    send(x, u, g)
    for k in range(Z):
        s[k][...] = dot(g[part((r + k) & 3, size), :], down[...]).astype(BF)
        send(s[k])


def text_ffn_back(*refs):
    rank, din, up, down, u, z, du, s = split(refs, 0, 4, 0, 0, 0, 0, 0, 4)
    r = rank[0]
    size = din[0].shape[0]
    rows_in_order(z, din, r)

    def hidden(rows):
        du[rows, :] = (dot_nt(z[rows, :], down[...]) * gelu_slope(u[rows, :])).astype(BF)

    ready(down, u)
    tiles(z.shape[0], size, hidden)
    send(z, du)
    for k in range(Z):
        s[k][...] = dot_nt(du[part((r + k) & 3, size), :], up[...]).astype(BF)


def image_hidden(a, w, u, g):
    width = w.shape[2]
    depth = w.shape[1] // 2
    for c in range(Z):
        cols = slice(c * width, (c + 1) * width)
        uu = dot(a[...], w[c, 0:depth, :])
        u[:, cols] = uu
        g[:, cols] = gelu(uu).astype(BF)


def image_down(af, g, w, z):
    width = w.shape[2]
    depth = w.shape[1] // 2
    for n in range(Z):
        out = slice(n * width, (n + 1) * width)
        acc = af[:, out]
        rows = slice(depth + n * width, depth + (n + 1) * width)
        for c in range(Z):
            cols = slice(c * width, (c + 1) * width)
            acc = acc + dot(g[:, cols], w[c, rows, :])
        z[:, out] = acc


def image_hidden_back(dzb, w, u, du):
    width = w.shape[2]
    depth = w.shape[1] // 2
    for c in range(Z):
        cols = slice(c * width, (c + 1) * width)
        dg = sum(
            dot_nt(
                dzb[:, n * width : (n + 1) * width],
                w[c, depth + n * width : depth + (n + 1) * width, :],
            )
            for n in range(Z)
        )
        du[:, cols] = (dg * gelu_slope(u[:, cols])).astype(BF)


def image_up_back(dz, du, w, da):
    width = w.shape[2]
    width = w.shape[2]
    for n in range(Z):
        out = slice(n * width, (n + 1) * width)
        acc = dz[:, out]
        for c in range(Z):
            cols = slice(c * width, (c + 1) * width)
            acc = acc + dot_nt(du[:, cols], w[c, n * width : (n + 1) * width, :])
        da[:, out] = acc


def image_mid(position, *refs):
    rank, s, base, w, gains, shifts, z0, a, u, g, z1, y, yb, af = split(
        refs, 0, 4, 0, 0, 0, 0, 0, 0, 0, 0, 0, 0, 0, 0
    )
    g0, b0 = gains[position : position + 1, :], shifts[position : position + 1, :]
    g1, b1 = gains[position + 1 : position + 2, :], shifts[position + 1 : position + 2, :]

    def first(rows):
        zz = base[rows, :].astype(F32) + total(s, rows)
        z0[rows, :] = zz
        aa = normalise(zz)[0] * g0 + b0
        af[rows, :] = aa
        a[rows, :] = aa.astype(BF)

    ready(base, s, gains, shifts)
    tiles(z0.shape[0], 32, first)
    send(z0, a)
    image_hidden(a, w, u, g)
    send(u, g)
    image_down(af, g, w, z1)
    send(z1)

    def second(rows):
        yy = normalise(z1[rows, :])[0] * g1 + b1
        y[rows, :] = yy
        yb[rows, :] = yy.astype(BF)

    tiles(z0.shape[0], 32, second)


def image_mid_back(position, *refs):
    rank, s, base, z1, z0, u, w, gains, stat_1, d1b, du, d0, d0b, stat, d1, da = split(
        refs, 0, 4, 0, 0, 0, 0, 0, 0, 0, 0, 0, 0, 0, 0, 0, 0
    )
    g0 = gains[position : position + 1, :]
    g1 = gains[position + 1 : position + 2, :]
    stat[...] = jnp.zeros_like(stat)

    def first(rows):
        d, dg, ds = norm_back(z1[rows, :], g1, base[rows, :] + total(s, rows))
        d1[rows, :] = d
        d1b[rows, :] = d.astype(BF)
        stat[2:3, :] += dg
        stat[3:4, :] += ds

    ready(z1, base, s)
    tiles(z0.shape[0], 32, first)
    image_hidden_back(d1b, w, u, du)
    image_up_back(d1, du, w, da)
    ready(z0)

    def second(rows):
        d, dg, ds = norm_back(z0[rows, :], g0, da[rows, :])
        d0[rows, :] = d
        d0b[rows, :] = d.astype(BF)
        stat[0:1, :] += dg
        stat[1:2, :] += ds

    tiles(z0.shape[0], 32, second)
    stat_rows(d0b, z0.shape[0], stat, stat_1)


def image_turn(position, *refs):
    (rank, s, base, cot, w, gains, shifts, out, a, g, d1b, du, d0, d0b, stat,
     z0, af, u, z1, y, dy, d1, da) = split(
        refs, 0, 4, 0, 4, 0, 0, 0, 4, 0, 0, 0, 0, 0, 0, 0, 0, 0, 0, 0, 0, 0, 0, 0
    )
    r = rank[0]
    g0, b0 = gains[position : position + 1, :], shifts[position : position + 1, :]
    g1, b1 = gains[position + 1 : position + 2, :], shifts[position + 1 : position + 2, :]
    width = dy.shape[1] // Z
    stat[...] = jnp.zeros_like(stat)
    for k, ref in enumerate(cot):
        dy[:, part((r - k) & 3, width)] = ref[0 : dy.shape[0], :].astype(F32)

    def first(rows):
        zz = base[rows, :] + total(s, rows)
        z0[rows, :] = zz
        aa = normalise(zz)[0] * g0 + b0
        af[rows, :] = aa
        a[rows, :] = aa.astype(BF)

    ready(base, s, gains, shifts)
    tiles(z0.shape[0], 32, first)
    image_hidden(a, w, u, g)
    image_down(af, g, w, z1)

    def second(rows):
        zz = z1[rows, :]
        y[rows, :] = normalise(zz)[0] * g1 + b1
        d, dg, ds = norm_back(zz, g1, dy[rows, :])
        d1[rows, :] = d
        d1b[rows, :] = d.astype(BF)
        stat[2:3, :] += dg
        stat[3:4, :] += ds

    tiles(z0.shape[0], 32, second)
    for k in range(Z):
        out[k][...] = y[:, part((r + k) & 3, width)].astype(BF)
    image_hidden_back(d1b, w, u, du)
    image_up_back(d1, du, w, da)

    def third(rows):
        d, dg, ds = norm_back(z0[rows, :], g0, da[rows, :])
        d0[rows, :] = d
        d0b[rows, :] = d.astype(BF)
        stat[0:1, :] += dg
        stat[1:2, :] += ds

    tiles(z0.shape[0], 32, third)


def ffn_pieces(core, keep, give, a, du, g, dz):
    width = a.shape[1] // Z
    half = a.shape[1] // 2
    for out, which in ((keep, core), (give, 1 - core)):
        cols = part(which, half)
        left_up, right_down = a[:, cols], dz[:, cols]
        for c in range(Z):
            block = slice(c * width, (c + 1) * width)
            row = c * 2 * half
            out[row : row + half, :] = dot_tn(left_up, du[:, block]).astype(BF)
            down = dot_tn(g[:, block], right_down).astype(BF)
            for j in range(half // width):
                at = row + half + j * width
                out[at : at + width, :] = down[:, j * width : (j + 1) * width]


def matrix_whole(out, left, right):
    step = 256 if left.shape[1] % 256 == 0 else left.shape[1]
    for j in range(left.shape[1] // step):
        rows = slice(j * step, (j + 1) * step)
        out[rows, :] = dot_tn(left[:, rows], right[...]).astype(BF)
    if isinstance(out, Leaving):
        send(out)


def grads_image_ffn(*refs):
    pos, a, du, g, dz, keep, give = refs
    ffn_pieces(pos[3], keep, give, a, du, g, dz)


def grads_end(*refs):
    pos, x, du, g, dz, xv, duv, gv, dzv, out = refs
    count, size, wide = out.shape[0], out.shape[2], out.shape[3]
    deep, tall = x.shape[1], xv.shape[1]
    blocks = deep // wide
    ready(x, du, g, dz, xv, duv, gv, dzv)

    def write(c, row, value):
        value = value.astype(BF)
        for d in range(row // size, (row + value.shape[0] - 1) // size + 1):
            lo, hi = max(row, d * size), min(row + value.shape[0], (d + 1) * size)
            out[d, c, lo - d * size : hi - d * size, :] = value[lo - row : hi - row]

    for c in range(Z):
        for j in range(blocks):
            cols = slice((c * blocks + j) * wide, (c * blocks + j + 1) * wide)
            write(c, j * deep, dot_tn(x[...], du[:, cols]))
            own, cols = slice(c * deep, (c + 1) * deep), slice(j * wide, (j + 1) * wide)
            write(c, (blocks + j) * deep, dot_tn(g[:, own], dz[:, cols]))
        row = 2 * blocks * deep
        cols = slice(c * wide, (c + 1) * wide)
        for n in range(tall // wide):
            rows = slice(n * wide, (n + 1) * wide)
            write(c, row + n * wide, dot_tn(xv[:, rows], duv[:, cols]))
            write(c, row + tall + n * wide, dot_tn(gv[:, cols], dzv[:, rows]))
        out.send_part((slice(None), c), c == Z - 1)


def cut_static(*refs):
    pos, whole, out = split(refs, 0, 0, 4)
    for k in range(Z):
        out[k][...] = whole[-k % Z]


def grads_text_ffn(*refs):
    pos, x, du, g, dz, up, down = refs
    matrix_whole(up, x, du)
    matrix_whole(down, g, dz)


def grads_attention(*refs):
    pos, xt, dqt, xv, dqv, ot, dzt, ov, dzv, tq, vq, to, vo = refs
    for i in range(3):
        matrix_whole(tq.at[i], xt, dqt.at[i])
        matrix_whole(vq.at[i], xv, dqv.at[i])
    matrix_whole(to, ot, dzt)
    matrix_whole(vo, ov, dzv)


def core_sum(*refs):
    pos, keep, recv, out = split(refs, 0, 0, 0, 4)
    size = out[0].shape[0]
    for k in range(Z):
        rows = slice(-k % Z * size, (-k % Z + 1) * size)
        out[k][...] = (keep[rows, :].astype(F32) + recv[rows, :].astype(F32)).astype(BF)


def tensor_sum_stats(*refs):
    pos, s, text, image, end, out, rows_out = split(refs, 0, 4, 4, 4, 4, 0, 0)
    rows_out[...] = jnp.zeros(rows_out.shape, BF)
    size, rows = s[0].shape[0], 16
    out[pos[3], 0:size, :] = total(s, slice(None)).astype(BF)
    out[1 - pos[3], 0:size, :] = jnp.zeros(s[0].shape, BF)
    last = [slice(x[0].shape[0] - rows, x[0].shape[0] - rows // 2) for x in (text, image)]
    wide, tall = out.shape[2], image[0].shape[1]
    narrow = total(text, last[0])
    narrow = jnp.concatenate(
        [narrow, jnp.zeros((narrow.shape[0], tall - narrow.shape[1]), F32)], axis=1
    )
    stats = jnp.concatenate([narrow, total(image, last[1])], axis=0).astype(BF)
    for j in range(Z):
        at = size + (j % 2) * rows
        out[j // 2, at : at + rows, :] = stats[:, j * wide : (j + 1) * wide]
    send(out)
    rows_out[part(pos[4], end[0].shape[0]), :] = total(end, slice(None)).astype(BF)


def finish(*refs):
    count = 10
    stq, ins, both, end = refs[1], refs[2 : 1 + count], refs[1 + count], refs[2 + count]
    stqo, outs = refs[3 + count], refs[4 + count : 3 + 2 * count]
    up, down, tg, ts, vg, vs = refs[3 + 2 * count : 9 + 2 * count]
    end_refs = refs[9 + 2 * count :]
    for source, out in zip(ins, outs):
        out[...] = source[...].astype(F32)
        send(out)
    for j in range(3):
        stqo[j] = stq[j].astype(F32).T
    send(stqo)
    half, wide = up.shape[0] // 2, up.shape[1]
    for h in range(2):
        up[h * half : (h + 1) * half, :] = both[h, 0:half, :].astype(F32)
        for j in range(half // wide):
            at, to = half + j * wide, h * half + j * wide
            down[:, to : to + wide] = both[h, at : at + wide, :].astype(F32)
    send(up, down)
    blocks = [both[j // 2, 2 * half + j % 2 * 16 : 2 * half + j % 2 * 16 + 16, :] for j in range(Z)]
    stats = jnp.concatenate(blocks, axis=1).astype(F32)
    for i in range(4):
        tg[i : i + 1, :] = stats[2 * i : 2 * i + 1, 0 : tg.shape[1]]
        ts[i : i + 1, :] = stats[2 * i + 1 : 2 * i + 2, 0 : tg.shape[1]]
        vg[i : i + 1, :] = stats[8 + 2 * i : 9 + 2 * i, :]
        vs[i : i + 1, :] = stats[9 + 2 * i : 10 + 2 * i, :]
    up, down, image_up, image_down = end_refs
    deep, tall = up.shape[0], image_up.shape[0]
    blocks = deep // wide
    for j in range(blocks):
        cols = slice(j * wide, (j + 1) * wide)
        up[:, cols] = end[j * deep : (j + 1) * deep, :].astype(F32)
        down[:, cols] = end[(blocks + j) * deep : (blocks + j + 1) * deep, :].astype(F32)
    send(up, down)
    at = 2 * blocks * deep
    image_up[...] = end[at : at + tall, :].astype(F32)
    for j in range(tall // wide):
        row = at + tall + j * wide
        image_down[:, j * wide : (j + 1) * wide] = end[row : row + wide, :].astype(F32)


def placed(array):
    if any(array is one for one in arrived):
        return array
    return pltpu.with_memory_space_constraint(array, pltpu.HBM)


latest = []


def follow(results):
    latest[:] = [min(results, key=lambda x: x.size)]


def run(name, body, outs, args, scratch=(), after=()):
    after = latest + list(after)
    flat = [None]
    for arg in args[1:]:
        flat.extend(arg if isinstance(arg, (list, tuple)) else [arg])
    shapes, groups = [], []
    for shape, dtype, count in outs:
        groups.append(count)
        shapes.extend([pltpu.HBM(shape, dtype)] * max(count, 1))
    scratch = [jax.ShapeDtypeStruct(shape, dtype) for shape, dtype in scratch]
    held = sum(
        math.prod(x.shape) * jnp.dtype(x.dtype).itemsize for x in flat[1:] + shapes + scratch
    )
    n_in, n_out = len(flat) - 1, len(shapes)
    first = 1 + n_in + len(after)
    stage = first + n_out
    indices = [x.index if isinstance(x, View) else None for x in flat[1:]]

    def staged_body(*refs):
        refs = (Scalars(*refs[:3]), *refs[3:])
        sems = refs[-1]
        moves = [
            pltpu.make_async_copy(ref if index is None else ref.at[index], place, sems.at[i])
            for i, (ref, index, place) in enumerate(zip(refs[1 : 1 + n_in], indices, refs[stage:]))
        ]
        for move in moves:
            move.start()
        operands = [Arriving(ref, move) for ref, move in zip(refs[stage:], moves)]
        results = [
            Leaving(ref, target, sems.at[n_in + i])
            for i, (ref, target) in enumerate(zip(refs[stage + n_in :], refs[first:stage]))
        ]
        body(refs[0], *operands, *results, *refs[stage + n_in + n_out : -1])
        for operand in operands:
            operand.wait()
        for result in results:
            result.send()
        for result in results:
            result.copy.wait()

    hbm, free = pl.BlockSpec(memory_space=pltpu.HBM), pl.BlockSpec(memory_space=pl.ANY)
    arrays = [x.array if isinstance(x, View) else x for x in flat[1:]]
    results = pl.pallas_call(
        staged_body,
        out_shape=shapes,
        in_specs=[pl.BlockSpec(memory_space=pltpu.SMEM)] * 3 + [free] * (first - 1),
        out_specs=[hbm] * n_out,
        scratch_shapes=[pltpu.VMEM(x.shape, x.dtype) for x in flat[1:] + shapes + scratch]
        + [pltpu.SemaphoreType.DMA((n_in + n_out,))],
        compiler_params=pltpu.CompilerParams(
            vmem_limit_bytes=min(60 << 20, max(16 << 20, held + (8 << 20)))
        ),
        cost_estimate=COST,
        name=name,
    )(
        *args[0], *[placed(x) for x in arrays + after])
    follow(results)
    return split(list(results), *groups)


def cut_weights(scalars, groups, n_dp, wide):
    flat = [matrix for group in groups for matrix in group]
    sizes = [sum(math.prod(m.shape) for m in group) // wide // n_dp for group in groups]
    step = 16

    def body(pos_ref, *refs):
        out, sem = refs[-2:]
        sources, base = list(refs[: len(flat)]), 0
        for group, size in zip(groups, sizes):
            steps, offset = size // step, 0
            begin = pos_ref[4] * steps
            for matrix in group:
                source = sources.pop(0)
                rows, width = matrix.shape
                for j in range(width // wide):
                    first = jnp.clip(offset // step - begin, 0, steps)
                    last = jnp.clip((offset + rows) // step - begin, 0, steps)

                    def move(i, carry, source=source, offset=offset, j=j, base=base, begin=begin):
                        row = pl.multiple_of((begin + i) * step - offset, step)
                        to = pl.multiple_of(base + i * step, step)
                        pltpu.make_async_copy(
                            source.at[pl.ds(row, step), pl.ds(j * wide, wide)],
                            out.at[pl.ds(to, step), :],
                            sem,
                        ).start()
                        return carry

                    lax.fori_loop(first, last, move, 0)
                    offset += rows
            base += size
        pltpu.make_async_copy(out, out, sem).wait()

    hbm, free = pl.BlockSpec(memory_space=pltpu.HBM), pl.BlockSpec(memory_space=pl.ANY)
    after = list(latest)
    result = pl.pallas_call(
        body,
        out_shape=pltpu.HBM((sum(sizes), wide), BF),
        in_specs=[pl.BlockSpec(memory_space=pltpu.SMEM)] + [free] * (len(flat) + len(after)),
        out_specs=hbm,
        scratch_shapes=[pltpu.SemaphoreType.DMA(())],
        cost_estimate=COST,
        name="cut_weights",
    )(scalars[0], *[placed(x) for x in flat + after])
    follow([result])
    return result


arrived = []


def shift(values, k):
    arrived.append(lax.ppermute(values, "tensor", [(i, (i + k) % Z) for i in range(Z)]))
    return arrived[-1]


def spread(own):
    return [own] + [shift(own, k) for k in (1, 2, 3)]


def swap(chunks):
    return [chunks[0]] + [shift(chunks[k], k) for k in (1, 2, 3)]


def along(values, dy, dx, dc):
    pairs = []
    for y in range(4):
        for x in range(4):
            for c in range(2):
                to = (((y + dy) % 4) * 4 + (x + dx) % 4) * 2 + (c + dc) % 2
                pairs.append(((y * 4 + x) * 2 + c, to))
    arrived.append(lax.ppermute(values, "dp", pairs))
    return arrived[-1]


def pad_rows(values, n):
    micro, samples, rows, width = values.shape
    flat = values.reshape(micro, samples * rows, width)
    flat = jnp.pad(flat, ((0, 0), (0, n - samples * rows), (0, 0)))
    return flat.reshape(micro * n, width)


def unpad_rows(values, shape, n):
    micro, samples, rows, width = shape
    return values.reshape(micro, n, width)[:, : samples * rows].reshape(shape)


def joined(text, image, chunks):
    wide, width = image.shape[1], text.shape[1]
    t = text.reshape(chunks, text.shape[0] // chunks, width)
    main = packed_rows(t.shape[1], width, wide)
    rest = t[:, main:].reshape(chunks, t.shape[1] - main, width // (wide - width), wide - width)
    rest = rest.transpose(0, 2, 1, 3).reshape(chunks, main, wide - width)
    t = jnp.concatenate([t[:, :main], rest], axis=2)
    v = image.reshape(chunks, image.shape[0] // chunks, wide)
    return jnp.concatenate([v, t], axis=1)


def parted(both, text_rows, width):
    wide = both.shape[2]
    main = packed_rows(text_rows, width, wide)
    image, t = both[:, : both.shape[1] - main], both[:, both.shape[1] - main :]
    parts = width // (wide - width)
    rest = t[:, :, width:].reshape(t.shape[0], parts, main // parts, wide - width)
    rest = rest.transpose(0, 2, 1, 3).reshape(t.shape[0], main // parts, width)
    text = jnp.concatenate([t[:, :, :width], rest], axis=1)
    return text.reshape(-1, width), image.reshape(-1, wide)


def in_order(chunks, rank):
    ring = jnp.stack([chunks[0], chunks[3], chunks[2], chunks[1]] * 2)
    return lax.dynamic_slice_in_dim(ring, (Z - rank) & 3, Z, 0)


def shards(
    text_in, image_in, caption_len, region_count, text_cot, image_cot,
    co_text_qkv, co_image_qkv, co_text_out, co_image_out,
    co_text_up, co_text_down, co_image_up, co_image_down,
    self_text_qkv, self_image_qkv, self_text_out, self_image_out,
    text_up, text_down, image_up, image_down,
    text_gains, text_shifts, image_gains, image_shifts,
):
    arrived.clear()
    latest.clear()
    rank = lax.axis_index("tensor")
    place = lax.axis_index("dp")
    n_dp = lax.axis_size("dp")
    pos = jnp.stack([rank, (place // 2) % 4, place // 8, place % 2, place]).astype(jnp.int32)
    scalars = [pos, caption_len, region_count]
    micro, samples, text, wt = text_in.shape
    regions, wv = image_in.shape[2:]
    dt, dv = wt * Z, wv * Z
    nt = -(-samples * text // 64) * 64
    nv = -(-samples * regions // 64) * 64
    rt, rv = micro * nt, micro * nv
    ct, cv = rt // Z, rv // Z
    co_w = co_text_qkv.shape[2]
    st_w = self_text_qkv.shape[2]
    si_w = self_image_qkv.shape[2]
    ft = co_text_up.shape[1]
    shard = ((cv + packed_rows(ct, wt, wv), wv), BF)
    whole = ((rv + packed_rows(rt, wt, wv), wv), BF)

    groups = [(co_image_up, co_image_down), (text_up, text_down, image_up, image_down)]
    cuts = cut_weights(scalars, groups, n_dp, wv)
    shards_in = joined(pad_rows(text_in, nt), pad_rows(image_in, nv), 1)[0]
    n_cut = 2 * dv // n_dp
    pieces = spread(cuts)
    w_mid = lax.all_gather(
        jnp.stack([piece[:n_cut] for piece in pieces]), "dp", axis=1, tiled=True
    )
    w_end = lax.all_gather(
        jnp.stack([piece[n_cut:] for piece in pieces]), "dp", axis=1, tiled=True
    )
    both = spread(shards_in)
    co_dims = (samples, text, regions, nt, nv)
    text_dims = (samples, text, nt, TEXT_HEAD, LENGTHS)
    image_dims = (samples, regions, nv, IMAGE_HEAD, LENGTHS + micro * samples)
    xt0, xv0, bt, bv, qt0, qv0, ot0, ov0, st, sv = run(
        "co_fwd", functools.partial(co_fwd, co_dims),
        [((rt, dt), BF, 0), ((rv, dv), BF, 0), ((ct, dt), BF, 0), ((cv, dv), BF, 0),
         ((3, rt, co_w), BF, 0), ((3, rv, co_w), BF, 0), ((rt, co_w), BF, 0),
         ((rv, co_w), BF, 0), ((ct, dt), BF, Z), ((cv, dv), BF, Z)],
        [scalars, both, co_text_qkv, co_image_qkv, co_text_out, co_image_out],
    )
    n_text = 2 * dt * (ft // wv)
    w_text = View(w_end, (slice(None), pl.ds(0, n_text)), (Z, n_text, wv))
    w_image = View(w_end, (slice(None), pl.ds(n_text, 2 * dv)), (Z, 2 * dv, wv))
    norm_t = [((ct, dt), F32, 0), ((ct, dt), F32, 0), ((ct, dt), BF, 0)]
    ffn_t = [((rt, dt), BF, 0), ((rt, ft), F32, 0), ((rt, ft), BF, 0), ((ct, dt), BF, Z)]
    zt0, at, atb = run(
        "text_norm0", functools.partial(text_norm, 0), norm_t,
        [scalars, swap(st), bt, text_gains, text_shifts],
    )
    xt1, ut1, gt1, st = run(
        "text_ffn1", text_ffn, ffn_t, [scalars, spread(atb), co_text_up, co_text_down]
    )
    zv0, av, uv1, gv1, zv1, bv, bvb = run(
        "image_mid", functools.partial(image_mid, 0),
        [((cv, dv), F32, 0), ((cv, dv), BF, 0), ((cv, dv), F32, 0), ((cv, dv), BF, 0),
         ((cv, dv), F32, 0), ((cv, dv), F32, 0), ((cv, dv), BF, 0)],
        [scalars, swap(sv), bv, w_mid, image_gains, image_shifts],
        [((cv, dv), F32)],
    )
    zt1, bt, btb = run(
        "text_norm1", functools.partial(text_norm, 1), norm_t,
        [scalars, swap(st), at, text_gains, text_shifts],
    )
    cot = joined(pad_rows(text_cot, nt), pad_rows(image_cot, nv), Z)
    (cot,) = run("cut", cut, [(*shard, Z)], [scalars, cot])
    cot = swap(cot)
    xt2, qt2, ot2, st = run(
        "text_self", functools.partial(self_fwd, text_dims),
        [((rt, dt), BF, 0), ((3, rt, st_w), BF, 0), ((rt, st_w), BF, 0), ((ct, dt), BF, Z)],
        [scalars, spread(btb), self_text_qkv, self_text_out],
    )
    xv2, qv2, ov2, sv = run(
        "image_self", functools.partial(self_fwd, image_dims),
        [((rv, dv), BF, 0), ((3, rv, si_w), BF, 0), ((rv, si_w), BF, 0), ((cv, dv), BF, Z)],
        [scalars, spread(bvb), self_image_qkv, self_image_out],
    )
    hidden = Z * ft
    out_t, at3, gt3, dt3, dut3, gt, gtb, stat_t1 = run(
        "text_turn", functools.partial(text_turn, 2),
        [((ct, wt), BF, Z), ((ct, dt), BF, 0), ((ct, hidden), BF, 0), ((ct, dt), BF, 0),
         ((ct, hidden), BF, 0), ((ct, dt), F32, 0), ((ct, dt), BF, 0), ((4, dt), F32, 0)],
        [scalars, swap(st), bt, cot, w_text, text_gains, text_shifts],
        [((ct, hidden), F32), ((ct, dt), F32), ((ct, dt), F32)],
    )
    out_v, av3, gv3, dv3, duv3, gv, gvb, stat_v1 = run(
        "image_turn", functools.partial(image_turn, 2),
        [((cv, wv), BF, Z), ((cv, dv), BF, 0), ((cv, dv), BF, 0), ((cv, dv), BF, 0),
         ((cv, dv), BF, 0), ((cv, dv), F32, 0), ((cv, dv), BF, 0), ((4, dv), F32, 0)],
        [scalars, swap(sv), bv, cot, w_image, image_gains, image_shifts],
        [((cv, dv), F32)] * 8,
    )
    back_ffn = [((rt, dt), BF, 0), ((rt, ft), BF, 0), ((ct, dt), BF, Z)]
    stat_shape = ((2, dt), F32, 0)
    def image_ffn_grads(name, *saved):
        keep, give = run(
            "grads_" + name, grads_image_ffn, [((Z * dv, wv), BF, 0)] * 2, [scalars, *saved]
        )
        return keep, along(give, 0, 0, 1)
    def core_summed(name, halves, after):
        (chunks,) = run(
            "core_sum_" + name, core_sum, [((dv, wv), BF, Z)], [scalars, *halves], after=after
        )
        return chunks
    (end,) = run(
        "grads_end", grads_end, [((n_dp, Z, (n_text + 2 * dv) // n_dp, wv), BF, 0)],
        [scalars, at3, dut3, gt3, dt3, av3, duv3, gv3, dv3],
    )
    end_cut = lax.psum_scatter(end, "dp", scatter_dimension=0, tiled=False)
    dt2, dqt2, st = run(
        "text_self_back", functools.partial(self_bwd, text_dims),
        [((rt, dt), BF, 0), ((3, rt, st_w), BF, 0), ((ct, dt), BF, Z)],
        [scalars, spread(gtb), qt2, self_text_qkv, self_text_out],
        [((rt, st_w), BF)],
    )
    dv2, dqv2, sv = run(
        "image_self_back", functools.partial(self_bwd, image_dims),
        [((rv, dv), BF, 0), ((3, rv, si_w), BF, 0), ((cv, dv), BF, Z)],
        [scalars, spread(gvb), qv2, self_image_qkv, self_image_out],
        [((rv, si_w), BF)],
    )
    gt, gtb, stat_t2 = run(
        "text_norm1_back", functools.partial(text_norm_back, 1),
        [((ct, dt), F32, 0), ((ct, dt), BF, 0), stat_shape],
        [scalars, swap(st), gt, zt1, text_gains],
    )
    st_q, sv_q, st_o, sv_o = run(
        "grads_self", grads_attention,
        [((3, dt, st_w), BF, 0), ((3, dv, si_w), BF, 0), ((st_w, dt), BF, 0), ((si_w, dv), BF, 0)],
        [scalars, xt2, dqt2, xv2, dqv2, ot2, dt2, ov2, dv2],
    )
    dt1, dut1, st = run(
        "text_ffn1_back", text_ffn_back, back_ffn,
        [scalars, spread(gtb), co_text_up, co_text_down, ut1],
    )
    dv1, duv1, gv, gvb, _ = run(
        "image_mid_back", functools.partial(image_mid_back, 0),
        [((cv, dv), BF, 0), ((cv, dv), BF, 0), ((cv, dv), F32, 0), ((cv + 16, dv), BF, 0),
         ((4, dv), F32, 0)],
        [scalars, swap(sv), gv, zv1, zv0, uv1, w_mid, image_gains, stat_v1],
        [((cv, dv), F32)] * 2,
    )
    mid_f = image_ffn_grads("mid", av, duv1, gv1, dv1)
    zv = spread(gvb)
    gt, gtb, _ = run(
        "text_norm0_back", functools.partial(text_norm_back_stats, 0),
        [((ct, dt), F32, 0), ((ct + 16, dt), BF, 0), stat_shape],
        [scalars, swap(st), gt, zt0, text_gains, stat_t2, stat_t1],
        after=[zv[1], zv[3]],
    )
    t1_up, t1_down = run(
        "grads_ffn1", grads_text_ffn, [((dt, ft), BF, 0), ((ft, dt), BF, 0)],
        [scalars, xt1, dut1, gt1, dt1],
    )
    zt = spread(gtb)
    mid_f = core_summed("mid", mid_f, zt[1:] + zv[1:])
    (end_cut,) = run(
        "cut_end", cut_static, [(end_cut.shape[1:], BF, Z)], [scalars, end_cut]
    )
    end_cut = swap(end_cut)
    dqt0, dqv0, tq, vq, to, vo = run(
        "co_back", functools.partial(co_bwd, co_dims),
        [((3, rt, co_w), BF, 0), ((3, rv, co_w), BF, 0),
         ((3, dt, co_w), BF, 0), ((3, dv, co_w), BF, 0), ((co_w, dt), BF, 0), ((co_w, dv), BF, 0)],
        [scalars, zt, zv, qt0, qv0, co_text_out, co_image_out, xt0, xv0, ot0, ov0],
        [((rt, dt), BF), ((rv, dv), BF), ((rt, co_w), BF), ((rv, co_w), BF)],
    )
    (s,) = run(
        "co_back_in", co_bwd_in, [(*whole, Z)],
        [scalars, dqt0, dqv0, co_text_qkv, co_image_qkv, gt, gv],
        [((rt, wt), F32), ((rv, wv), F32)],
    )
    mid_f, end = run(
        "last_sums", tensor_sum_stats,
        [((2, dv + 32, wv), BF, 0), ((n_text + 2 * dv, wv), BF, 0)],
        [scalars, swap(mid_f), zt, zv, end_cut],
    )
    late = lax.psum((st_q, t1_up, t1_down, sv_q, st_o, sv_o, tq, vq, to, vo, mid_f, end), "dp")
    s = swap(s)
    out_t, out_v = swap(out_t), swap(out_v)
    ffn_out = [((dt, ft), F32, 0), ((ft, dt), F32, 0)]
    image_out_shapes = [((dv, wv), F32, 0), ((wv, dv), F32, 0)]
    (st_q, t1_up, t1_down, sv_q, st_o, sv_o, tq, vq, to, vo, mid_up, mid_down, tg, ts, vg, vs,
     t_up, t_down, end_up, end_down) = run(
        "finish", finish,
        [((3, st_w, dt), F32, 0)] + ffn_out
        + [((3, dv, si_w), F32, 0), ((st_w, dt), F32, 0), ((si_w, dv), F32, 0),
           ((3, dt, co_w), F32, 0), ((3, dv, co_w), F32, 0),
           ((co_w, dt), F32, 0), ((co_w, dv), F32, 0)] + image_out_shapes
        + [((4, dt), F32, 0)] * 2 + [((4, dv), F32, 0)] * 2 + ffn_out + image_out_shapes,
        [scalars, *late],
    )
    st_q = st_q.transpose(0, 2, 1)

    text_out = in_order(out_t, rank).reshape(rt, wt)
    image_out = in_order(out_v, rank).reshape(rv, wv)
    text_grad, image_grad = parted(sum(member.astype(F32) for member in s)[None], rt, wt)
    return (
        unpad_rows(text_out, text_in.shape, nt).astype(F32),
        unpad_rows(image_out, image_in.shape, nv).astype(F32),
        unpad_rows(text_grad, text_in.shape, nt),
        unpad_rows(image_grad, image_in.shape, nv),
        tq, vq, to, vo, t1_up, t1_down, mid_up, mid_down,
        st_q, sv_q, st_o, sv_o, t_up, t_down, end_up, end_down,
        tg, ts, vg, vs,
    )


def solution(mesh):
    stream = P(None, "dp", None, "tensor")
    lengths = P(None, "dp")
    stacked = P(None, None, "tensor")
    rows = P("tensor", None)
    cols = P(None, "tensor")
    weights = (
        stacked, stacked, rows, rows, cols, rows, cols, rows,
        stacked, stacked, rows, rows, cols, rows, cols, rows,
        P(), P(), P(), P(),
    )
    in_specs = (stream, stream, lengths, lengths, stream, stream) + weights
    out_specs = (stream,) * 4 + weights
    return jax.shard_map(shards, mesh=mesh, in_specs=in_specs, out_specs=out_specs, check_vma=False)
```
